256 devices in a mesh: row: 32 (over z_lo, x, y), col: 8 (over z_hi, core).
Axes of the slice: x: 4, y: 4, z: 8 (z_hi: 4, z_lo: 2; z = z_hi * 2 + z_lo), core: 2. Of those that a mesh axis runs over, the one named last changes fastest.
Arguments:
- grad_out: bfloat16 [64, 512, 2048], P(None, 'row', 'col'), may hold values from -6 to 6
- row_feat: bfloat16 [512, 64], P('row'), may hold values from -6 to 6
- col_feat: bfloat16 [2048, 64], P('col'), may hold values from -6 to 6
- conv_one: bfloat16 [3, 3, 64, 64], replicated, may hold values from -0.25 to 0.25
- bias_one: float32 [64], replicated, may hold values from -3 to 3
- conv_two: bfloat16 [3, 3, 64, 64], replicated, may hold values from -0.25 to 0.25
Outputs:
- row_grad: float32 [512, 64], P('row')
- col_grad: float32 [2048, 64], P('col')
- grad_conv_one: float32 [3, 3, 64, 64], replicated
- grad_bias: float32 [64], replicated
- grad_conv_two: float32 [3, 3, 64, 64], replicated
The draws below stay inside these ranges and needn't reach their ends.
All inputs are finite; a program needn't handle non-finite values.
Results may differ from the reference program's by a relative error of at most 0.0065.
Values may be sent and summed in bfloat16 or wider, within the bound.
No kernel may reach another device: no remote copies, remote signals or barrier semaphores. Data moves between devices by JAX's collectives and lax.ppermute only.
A program may use at most 128 MiB of HBM per device.

```python
import math
import jax
import jax.numpy as jnp
from jax import lax

C = 64
NR = 512
NC = 2048


def levels(rng, shape, shards, least, high):
    def one(position, shards_of):
        draws = jax.random.uniform(jax.random.fold_in(jax.random.fold_in(rng, 6), position), (shards_of,), jnp.float32, least / len(shards), high / len(shards))
        return jnp.repeat(jnp.exp(draws), shape[position] // shards_of).reshape((-1,) + (1,) * (len(shape) - position - 1))

    level = one(*shards[0])
    for cut in shards[1:]:
        level = level * one(*cut)
    return level


def bell_draw(own_key, dims, width, bound, split=(), dtype=jnp.bfloat16):
    entries = width * jax.random.normal(own_key, dims, jnp.float32)
    if split:
        entries = entries * levels(own_key, dims, split, -0.22, 0.18)
    return jnp.clip(entries, -bound, bound).astype(dtype)


def setup_inputs(seed: int = 0) -> dict:
    key_list = jax.random.split(jax.random.key(seed), 7)
    grad_out = bell_draw(key_list[0], (C, NR, NC), 1.0, 6.0, ((1, 32), (2, 8)))
    row_feat = bell_draw(key_list[1], (NR, C), 1.0, 6.0, ((0, 32),))
    col_feat = bell_draw(key_list[2], (NC, C), 1.0, 6.0, ((0, 8),))
    conv_one = bell_draw(key_list[3], (3, 3, C, C), (9 * C) ** -0.5, 0.25)
    bias_one = bell_draw(key_list[4], (C,), 0.5, 3.0, (), jnp.float32)
    conv_two = bell_draw(key_list[5], (3, 3, C, C), (9 * C) ** -0.5, 0.25)
    return {"grad_out": grad_out, "row_feat": row_feat, "col_feat": col_feat, "conv_one": conv_one, "bias_one": bias_one, "conv_two": conv_two}


def shifted(padded, shift_r, shift_c, rows, cols):
    return padded[:, 8 + 8 * shift_r:8 + 8 * shift_r + rows, 8 + 8 * shift_c:8 + 8 * shift_c + cols]

def pad_map(field):
    return jnp.pad(field, ((0, 0), (8, 8), (8, 8)))

def forward_conv(kernel, field):
    rows, cols = (field.shape[1], field.shape[2])
    padded = pad_map(field)
    total = jnp.zeros((kernel.shape[2], rows, cols), jnp.float32)
    for tap_r in range(3):
        for tap_c in range(3):
            piece = shifted(padded, tap_r - 1, tap_c - 1, rows, cols).astype(jnp.float32)
            total = total + jnp.einsum('oi,irc->orc', kernel[tap_r, tap_c].astype(jnp.float32), piece)
    return total

def transpose_conv(kernel, field):
    rows, cols = (field.shape[1], field.shape[2])
    padded = pad_map(field)
    total = jnp.zeros((kernel.shape[3], rows, cols), jnp.float32)
    for tap_r in range(3):
        for tap_c in range(3):
            piece = shifted(padded, 1 - tap_r, 1 - tap_c, rows, cols).astype(jnp.float32)
            total = total + jnp.einsum('oi,orc->irc', kernel[tap_r, tap_c].astype(jnp.float32), piece)
    return total

def kernel_grad(upper, field):
    rows, cols = (field.shape[1], field.shape[2])
    padded = pad_map(field)
    upper_f = upper.astype(jnp.float32)
    taps = []
    for tap_r in range(3):
        line = []
        for tap_c in range(3):
            piece = shifted(padded, tap_r - 1, tap_c - 1, rows, cols).astype(jnp.float32)
            line.append(jnp.einsum('orc,irc->oi', upper_f, piece))
        taps.append(jnp.stack(line))
    return jnp.stack(taps)

def reference(grad_out, row_feat, col_feat, conv_one, bias_one, conv_two):
    rows, cols = (grad_out.shape[1], grad_out.shape[2])
    field = (row_feat.T.astype(jnp.float32)[:, :, None] + col_feat.T.astype(jnp.float32)[:, None, :]).astype(jnp.bfloat16)
    pre = forward_conv(conv_one, field) + bias_one[:, None, None]
    act = jax.nn.silu(pre).astype(jnp.bfloat16)
    back = transpose_conv(conv_two, grad_out)
    sig = jax.nn.sigmoid(pre)
    inner = (back * (sig * (1.0 + pre * (1.0 - sig)))).astype(jnp.bfloat16)
    grad_in = grad_out.astype(jnp.float32) + transpose_conv(conv_one, inner)
    row_grad = lax.optimization_barrier(jnp.sum(grad_in, axis=2)).T / math.sqrt(cols)
    col_grad = lax.optimization_barrier(jnp.sum(grad_in, axis=1)).T / math.sqrt(rows)
    whole = math.sqrt(rows * cols)
    grad_conv_one = kernel_grad(inner, field) / whole
    grad_bias = lax.optimization_barrier(jnp.sum(inner.astype(jnp.float32), axis=(1, 2))) / whole
    grad_conv_two = kernel_grad(grad_out, act) / whole
    return (row_grad, col_grad, grad_conv_one, grad_bias, grad_conv_two)
```

```python
import math

import jax
import jax.numpy as jnp
from jax import lax
from jax.experimental import pallas as pl
from jax.experimental.pallas import tpu as pltpu
from jax.sharding import PartitionSpec as P

F32, BF16 = jnp.float32, jnp.bfloat16
NN = (((1,), (0,)), ((), ()))
NT = (((1,), (1,)), ((), ()))
TN = (((0,), (0,)), ((), ()))
CH = 64
LANES = 128


def dot(x, y, dims):
    return lax.dot_general(x, y, dims, preferred_element_type=F32)


def dot_exact(x, y, dims):
    return lax.dot_general(
        x.astype(F32), y.astype(F32), dims, precision=lax.Precision.HIGHEST, preferred_element_type=F32
    )


def chunk_rows(n_row):
    weights, chans = 9 * CH // n_row, CH // n_row
    return weights, chans, weights + 3 * chans


def pack_kernel(grad_ref, row_ref, col_ref, out_ref, rows_scr):
    rows_scr[...] = grad_ref[:, :, :LANES].astype(F32).reshape(CH * 16, LANES)
    lane = lax.broadcasted_iota(jnp.int32, (CH, LANES), 1)
    for half in range(2):
        packed = jnp.zeros((CH, LANES), F32)
        for k in range(8):
            strip = rows_scr[pl.ds(half * 8 + k, CH, stride=16), :]
            if k:
                strip = pltpu.roll(strip, 16 * k, 1)
            packed = jnp.where((lane >= 16 * k) & (lane < 16 * k + 16), strip, packed)
        out_ref[half * CH : (half + 1) * CH, :] = packed.astype(BF16)
    out_ref[2 * CH :, :] = jnp.concatenate(
        [row_ref[...].astype(F32), col_ref[:16, :].astype(F32)], axis=1
    ).astype(BF16)


def main_kernel(
    n_row, n_col, grad_ref, next_ref, right_ref, diag_ref, row_ref, col_ref, w2_ref, k1c_ref, k1ct_ref, k1f_ref,
    bias_ref, out_ref, own_ref, rows_scr, x_scr, act_scr, inner_scr, ind_scr, back_scr, pre_scr, w_scr,
):
    cols = grad_ref.shape[2]
    seam = jnp.where(lax.axis_index("row") == n_row - 1, 0.0, 1.0).astype(F32)
    last_col = lax.axis_index("col") == n_col - 1

    def lane_of(shape):
        return lax.broadcasted_iota(jnp.int32, shape, 1) % cols

    def valid(lane, tap):
        if tap == 1:
            return jnp.ones(lane.shape, jnp.bool_)
        if tap == 0:
            crossing = lane >= cols - 8
        else:
            crossing = (lane >= cols - 16) & (lane < cols - 8)
        return jnp.logical_not(crossing & last_col)

    lane = lane_of((CH, cols))
    keep_low, keep_high = valid(lane, 0), valid(lane, 2)
    col_sum = jnp.zeros((CH, cols), F32)
    for side, (tile_ref, strip_ref) in enumerate(((grad_ref, right_ref), (next_ref, diag_ref))):
        for piece in range(cols // LANES):
            wide = tile_ref[:, :, LANES * piece : LANES * (piece + 1)]
            rows_scr[piece] = wide.astype(F32).reshape(CH * 16, LANES)
        for half in range(2):
            strip = strip_ref[half * CH : (half + 1) * CH, :].astype(F32)
            blk = 2 * side + half
            for k in range(8):
                line = jnp.concatenate(
                    [rows_scr[p, pl.ds(half * 8 + k, CH, stride=16), :] for p in range(cols // LANES)], axis=1
                )
                if side == 0:
                    col_sum = col_sum + line
                edge = pltpu.roll(strip, LANES - 16 * k, 1) if k else strip
                wide = jnp.concatenate([line, edge], axis=1)
                shift_one = pltpu.roll(wide, cols + LANES - 8, 1)[:, :cols]
                shift_two = pltpu.roll(wide, cols + LANES - 16, 1)[:, :cols]
                rows, span = slice(blk * CH, (blk + 1) * CH), slice(k * cols, (k + 1) * cols)
                x_scr[2, rows, span] = jnp.where(keep_low, line, 0.0).astype(BF16)
                x_scr[1, rows, span] = shift_one.astype(BF16)
                x_scr[0, rows, span] = jnp.where(keep_high, shift_two, 0.0).astype(BF16)

    row_ext = jnp.concatenate([row_ref[...], diag_ref[2 * CH :, :CH]], axis=0).astype(F32)
    col_ext = jnp.concatenate([col_ref[...], diag_ref[2 * CH :, CH:]], axis=0).astype(F32)
    blocks = [row_ext[8 * k : 8 * k + 8, :] for k in range(4)]
    row_cat = jnp.concatenate(
        [
            jnp.concatenate([blocks[0], blocks[1], blocks[2] * seam], axis=1),
            jnp.concatenate([blocks[1] * seam, blocks[2], blocks[3]], axis=1),
        ],
        axis=0,
    )
    place = lax.broadcasted_iota(jnp.int32, (cols, CH), 0)
    col_cat = jnp.concatenate(
        [jnp.where(valid(place, tap), col_ext[8 * tap : 8 * tap + cols, :], 0.0) for tap in range(3)], axis=1
    ).astype(BF16)
    col_terms = dot(k1c_ref[...], col_cat, NT)
    low, mid, high = (col_terms[CH * a : CH * (a + 1)] for a in range(3))
    bias = bias_ref[...]
    col_part = jnp.concatenate([low + mid + seam * high + bias, seam * low + mid + high + bias], axis=0)
    row_terms = dot(k1f_ref[...], row_cat.astype(BF16), NT)
    row_part = jnp.concatenate(
        [
            jnp.concatenate([row_terms[CH * b : CH * (b + 1), 8 * rb : 8 * rb + 8] for b in range(3)], axis=1)
            for rb in range(2)
        ],
        axis=0,
    )

    ind_lane = lax.broadcasted_iota(jnp.int32, (8, 8 * cols), 1)
    ind_row = lax.broadcasted_iota(jnp.int32, (8, 8 * cols), 0)
    for tap in range(3):
        hit = (ind_lane // cols == ind_row) & valid(ind_lane % cols, tap)
        ind_scr[8 * tap : 8 * tap + 8, :] = jnp.where(hit, 1.0, 0.0)
    indicator = ind_scr[...]
    pre_scr[...] = dot_exact(row_part, indicator, NN)
    x_all = x_scr[...].reshape(3 * 4 * CH, 8 * cols)
    back_scr[...] = dot(w2_ref[...], x_all, NN)

    inner_sum = jnp.zeros((2 * CH, cols), F32)
    for k in range(8):
        span = slice(k * cols, (k + 1) * cols)
        pre = pre_scr[:, span] + col_part
        sig = 1.0 / (1.0 + jnp.exp(-pre))
        act_scr[:, span] = (pre * sig).astype(BF16)
        inner = (back_scr[:, span] * (sig * (1.0 + pre * (1.0 - sig)))).astype(BF16)
        inner_scr[:, span] = inner
        inner_sum = inner_sum + inner.astype(F32)

    full = dot(x_all, act_scr[...], NT)
    both = jnp.concatenate([inner_scr[...], x_scr[1, : 2 * CH, :]], axis=0)
    sums = dot(indicator.astype(BF16), both, NT)
    row_sums = jnp.concatenate(
        [
            jnp.concatenate([sums[8 * b : 8 * b + 8, CH * rb : CH * (rb + 1)] for b in range(3)], axis=1)
            for rb in range(2)
        ],
        axis=0,
    )
    grad_rows = sums[8:16, 2 * CH :]
    spread_row = dot_exact(row_sums, k1f_ref[...], NN)

    def part(rb, a):
        return spread_row[8 * rb : 8 * rb + 8, CH * a : CH * (a + 1)]

    own_ref[...] = grad_rows + jnp.concatenate([part(0, 0), part(0, 1) + seam * part(1, 0)], axis=1)
    beyond = jnp.concatenate([seam * part(0, 2) + part(1, 1), part(1, 2)], axis=1)
    first, second = inner_sum[:CH], inner_sum[CH:]
    col_sums = jnp.concatenate([first + seam * second, first + second, seam * first + second], axis=0)
    spread_col = dot_exact(k1ct_ref[...], col_sums, NN)
    nothing = jnp.zeros((CH, LANES), F32)
    total = jnp.concatenate([col_sum, nothing], axis=1)
    for tap in range(3):
        piece = jnp.where(valid(lane, tap), spread_col[CH * tap : CH * (tap + 1)], 0.0)
        piece = jnp.concatenate([piece, nothing], axis=1)
        total = total + (pltpu.roll(piece, 8 * tap, 1) if tap else piece)
    one_row = dot_exact(row_sums, row_cat, TN)
    one_col = dot_exact(col_sums, col_cat, NN)
    gap = jnp.zeros((32, cols), F32)
    bias_row = dot_exact(jnp.ones((8, cols), F32), jnp.concatenate([gap, first + second, gap], axis=0), NT)
    for a in range(3):
        for b in range(3):
            one = one_row[CH * b : CH * (b + 1), CH * a : CH * (a + 1)]
            one = one + one_col[CH * a : CH * (a + 1), CH * b : CH * (b + 1)]
            at = [CH * (4 * b + rb + 2 - a) for rb in range(2)]
            zero, unit = full[at[0] : at[0] + CH, :CH], full[at[1] : at[1] + CH, CH:]
            if a == 0:
                zero = zero * seam
            if a == 2:
                unit = unit * seam
            w_scr[CH * (3 * a + b) : CH * (3 * a + b + 1), :] = jnp.concatenate([one, zero + unit], axis=1)

    weights, chans, sums_end = chunk_rows(n_row)
    tail = total[:, cols:] + bias_row[:1, :]
    for j in range(n_row):
        out_ref[j, :weights, :] = w_scr[weights * j : weights * (j + 1), :]
        mine = slice(chans * j, chans * (j + 1))
        out_ref[j, weights : weights + chans, :] = total[mine, :LANES]
        out_ref[j, weights + chans : weights + 2 * chans, :] = total[mine, LANES:cols]
        out_ref[j, weights + 2 * chans : sums_end, :] = tail[mine]
        out_ref[j, sums_end:, :] = beyond


def row_sum_kernel(n_row, n_col, got_ref, own_ref, out_ref):
    sums_end = chunk_rows(n_row)[2]
    before = lax.rem(lax.axis_index("row") + n_row - 1, n_row)
    total = got_ref[0, :sums_end, :]
    for j in range(1, n_row):
        total = total + got_ref[j, :sums_end, :]
    rows = own_ref[...] + got_ref[before, sums_end:, :]
    for k in range(n_col):
        out_ref[k, :sums_end, :] = total
        out_ref[k, sums_end:, :] = rows


def col_sum_kernel(n_row, n_col, cols, got_ref, row_ref, bias_ref, out_ref):
    weights, chans, sums_end = chunk_rows(n_row)
    me = lax.axis_index("col")
    before = lax.rem(me + n_col - 1, n_col)
    whole = math.sqrt(16 * n_row * cols * n_col)
    total = got_ref[0]
    for k in range(1, n_col):
        total = total + got_ref[k]
    rows = total[sums_end:, :] * (1.0 / math.sqrt(cols * n_col))
    row_ref[0:8, :] = rows[:, :CH]
    row_ref[8:16, :] = rows[:, CH:]
    bias_ref[...] = total[sums_end - 1 : sums_end, 32 : 32 + CH] * (1.0 / whole)
    scale = 1.0 / math.sqrt(16 * n_row)
    edge = got_ref[before, weights + 2 * chans : sums_end, :]
    edge = jnp.where(lax.broadcasted_iota(jnp.int32, edge.shape, 1) < 16, edge, 0.0)
    low = (got_ref[me, weights : weights + chans, :] + edge) * scale
    high = got_ref[me, weights + chans : weights + 2 * chans, :] * scale
    share = total[:weights, :] * (1.0 / whole)
    for j in range(n_row):
        out_ref[j, :weights, :] = share
        out_ref[j, weights : weights + chans, :] = low
        out_ref[j, weights + chans : weights + 2 * chans, :] = high
        if weights + 2 * chans < out_ref.shape[1]:
            out_ref[j, weights + 2 * chans :, :] = jnp.zeros((out_ref.shape[1] - weights - 2 * chans, LANES), F32)


def spread_kernel(n_row, got_ref, col_ref, one_ref, two_ref, col_scr):
    weights, chans, _ = chunk_rows(n_row)
    for j in range(n_row):
        share = got_ref[j, :weights, :]
        one_ref[weights * j : weights * (j + 1), :] = share[:, :CH]
        two_ref[weights * j : weights * (j + 1), :] = share[:, CH:]
        col_scr[chans * j : chans * (j + 1), :LANES] = got_ref[j, weights : weights + chans, :]
        col_scr[chans * j : chans * (j + 1), LANES:] = got_ref[j, weights + chans : weights + 2 * chans, :]
    col_ref[...] = col_scr[...].T


PARAMS = pltpu.CompilerParams(vmem_limit_bytes=48 * 1024 * 1024)


def sds(shape, dtype=F32):
    return jax.ShapeDtypeStruct(shape, dtype)


def shards(n_row, n_col, grad_out, row_feat, col_feat, conv_one, bias_one, conv_two):
    cols = grad_out.shape[2]
    weights, chans, sums_end = chunk_rows(n_row)
    nxt = lax.ppermute(grad_out, "row", [(k, (k - 1) % n_row) for k in range(n_row)])
    strip = pl.pallas_call(
        pack_kernel,
        out_shape=sds((2 * CH + 16, LANES), BF16),
        scratch_shapes=[pltpu.VMEM((CH * 16, LANES), F32)],
        compiler_params=PARAMS,
    )(grad_out, row_feat, col_feat)
    right = lax.ppermute(strip, "col", [(k, (k - 1) % n_col) for k in range(n_col)])
    pairs = [
        (r * n_col + c, (r - 1) % n_row * n_col + (c - 1) % n_col) for r in range(n_row) for c in range(n_col)
    ]
    diag = lax.ppermute(strip, ("row", "col"), pairs)

    is_last = lax.axis_index("row") == n_row - 1
    turned = jnp.transpose(conv_two[::-1], (3, 1, 0, 2))
    zero = jnp.where(is_last, turned.at[:, :, 2].set(0), turned)
    unit = jnp.where(is_last, turned.at[:, :, 0].set(0), turned)
    gap = ((0, 0), (0, 0))
    w2 = jnp.concatenate(
        [jnp.pad(zero, gap + ((0, 1), (0, 0))), jnp.pad(unit, gap + ((1, 0), (0, 0)))], axis=0
    ).reshape(2 * CH, 12 * CH)
    k1c = jnp.transpose(conv_one, (0, 2, 1, 3)).reshape(3 * CH, 3 * CH)
    k1f = jnp.transpose(conv_one, (1, 2, 0, 3)).reshape(3 * CH, 3 * CH)

    chunks, own = pl.pallas_call(
        lambda *refs: main_kernel(n_row, n_col, *refs),
        out_shape=(sds((n_row, sums_end + 8, LANES)), sds((8, LANES))),
        scratch_shapes=[
            pltpu.VMEM((cols // LANES, CH * 16, LANES), F32),
            pltpu.VMEM((3, 4 * CH, 8 * cols), BF16),
            pltpu.VMEM((2 * CH, 8 * cols), BF16),
            pltpu.VMEM((2 * CH, 8 * cols), BF16),
            pltpu.VMEM((24, 8 * cols), F32),
            pltpu.VMEM((2 * CH, 8 * cols), F32),
            pltpu.VMEM((2 * CH, 8 * cols), F32),
            pltpu.VMEM((9 * CH, LANES), F32),
        ],
        compiler_params=PARAMS,
    )(grad_out, nxt, right, diag, row_feat, col_feat, w2, k1c, k1c.T, k1f, bias_one[:, None])
    got = lax.all_to_all(chunks, "row", 0, 0)
    copies = pl.pallas_call(
        lambda *refs: row_sum_kernel(n_row, n_col, *refs),
        out_shape=sds((n_col, sums_end + 8, LANES)),
        compiler_params=PARAMS,
    )(got, own)
    got = lax.all_to_all(copies, "col", 0, 0)
    end = -(-(weights + 2 * chans) // 8) * 8
    row_grad, bias_grad, copies = pl.pallas_call(
        lambda *refs: col_sum_kernel(n_row, n_col, cols, *refs),
        out_shape=(sds((16, CH)), sds((1, CH)), sds((n_row, end, LANES))),
        compiler_params=PARAMS,
    )(got)
    got = lax.all_to_all(copies, "row", 0, 0)
    col_grad, one, two = pl.pallas_call(
        lambda *refs: spread_kernel(n_row, *refs),
        out_shape=(sds((cols, CH)), sds((9 * CH, CH)), sds((9 * CH, CH))),
        scratch_shapes=[pltpu.VMEM((CH, cols), F32)],
        compiler_params=PARAMS,
    )(got)
    shape = conv_one.shape
    return row_grad, col_grad, one.reshape(shape), bias_grad[0], two.reshape(shape)


def solution(mesh):
    in_specs = (P(None, "row", "col"), P("row", None), P("col", None), P(), P(), P())
    out_specs = (P("row", None), P("col", None), P(), P(), P())
    n_row, n_col = mesh.shape["row"], mesh.shape["col"]
    return jax.shard_map(
        lambda *args: shards(n_row, n_col, *args), mesh=mesh, in_specs=in_specs, out_specs=out_specs, check_vma=False
    )
```

```python
import math

import jax
import jax.numpy as jnp
from jax import lax
from jax.experimental import pallas as pl
from jax.experimental.pallas import tpu as pltpu
from jax.sharding import PartitionSpec as P

F32, BF16 = jnp.float32, jnp.bfloat16
NN = (((1,), (0,)), ((), ()))
NT = (((1,), (1,)), ((), ()))
TN = (((0,), (0,)), ((), ()))
CH = 64
LANES = 128


def dot(x, y, dims):
    return lax.dot_general(x, y, dims, preferred_element_type=F32)


def dot_exact(x, y, dims):
    return lax.dot_general(
        x.astype(F32), y.astype(F32), dims, precision=lax.Precision.HIGHEST, preferred_element_type=F32
    )


def chunk_rows(n_row):
    weights, chans = 9 * CH // n_row, CH // n_row
    return weights, chans, weights + 3 * chans


def dot_split(x, y, dims):
    high = x.astype(BF16)
    low = (x - high.astype(F32)).astype(BF16)
    y = y.astype(BF16)
    return dot(high, y, dims) + dot(low, y, dims)


def pack_kernel(row_ref, col_ref, out_ref):
    rows = row_ref[...].astype(F32)
    out_ref[:16, :] = jnp.concatenate([rows, jnp.zeros_like(rows)], axis=1).astype(BF16)
    cols = col_ref.shape[1]
    lane = lax.broadcasted_iota(jnp.int32, (CH, LANES), 1)
    first, last = col_ref[:, :LANES].astype(F32), col_ref[:, cols - LANES :].astype(F32)
    out_ref[16:, :] = jnp.where(lane < LANES // 2, first, last).astype(BF16)


def off_edge(axis, index):
    return jnp.where(lax.axis_index(axis) == index, 0.0, 1.0).astype(F32)


def indicator(cols, n_col):
    lane = lax.broadcasted_iota(jnp.int32, (8, cols), 1)
    row = lax.broadcasted_iota(jnp.int32, (8, cols), 0)
    me = lax.axis_index("col")
    off_map = ((lane < 8) & (me == 0), lane < 0, (lane >= cols - 8) & (me == n_col - 1))
    edge_lane = lax.broadcasted_iota(jnp.int32, (8, LANES), 1)
    edge_row = lax.broadcasted_iota(jnp.int32, (8, LANES), 0)
    edge = jnp.where(edge_lane // 16 == edge_row, 1.0, 0.0)
    taps = []
    for tap in range(3):
        on_map = jnp.logical_not(off_map[tap])
        main = [jnp.where(on_map & (row == k), 1.0, 0.0) for k in range(8)]
        taps.append(jnp.concatenate(main + [edge], axis=1))
    return jnp.concatenate(taps, axis=0).astype(BF16)


def own_kernel(n_col, grad_ref, w2_ref, x_ref, back_ref, grad_rows_ref, grad_cols_ref, ind_ref, rows_scr):
    cols = grad_ref.shape[2]
    lane = lax.broadcasted_iota(jnp.int32, (CH, cols), 1)
    edge_lane = lax.broadcasted_iota(jnp.int32, (CH, LANES), 1)
    for piece in range(cols // LANES):
        wide = grad_ref[:, :, LANES * piece : LANES * (piece + 1)]
        rows_scr[piece] = wide.astype(F32).reshape(CH * 16, LANES)
    col_sum = jnp.zeros((CH, cols), F32)
    for half in range(2):
        rows = slice(half * CH, (half + 1) * CH)
        left = right = jnp.zeros((CH, LANES), F32)
        for k in range(8):
            pieces = [rows_scr[p, pl.ds(half * 8 + k, CH, stride=16), :] for p in range(cols // LANES)]
            line = jnp.concatenate(pieces, axis=1)
            col_sum = col_sum + line
            span = slice(k * cols, (k + 1) * cols)
            x_ref[1, rows, span] = line.astype(BF16)
            x_ref[0, rows, span] = jnp.where(lane < cols - 8, pltpu.roll(line, cols - 8, 1), 0.0).astype(BF16)
            x_ref[2, rows, span] = jnp.where(lane >= 8, pltpu.roll(line, 8, 1), 0.0).astype(BF16)
            first = pltpu.roll(pieces[0], 16 * k, 1) if k else pieces[0]
            last = pltpu.roll(pieces[-1], 16 * k + 16, 1) if k < 7 else pieces[-1]
            here = edge_lane // 16 == k
            left = jnp.where(here & (edge_lane % 16 < 8), first, left)
            right = jnp.where(here & (edge_lane % 16 >= 8), last, right)
        x_ref[0, rows, 8 * cols :] = left.astype(BF16)
        x_ref[1, rows, 8 * cols :] = jnp.zeros((CH, LANES), BF16)
        x_ref[2, rows, 8 * cols :] = right.astype(BF16)
    grad_cols_ref[...] = col_sum
    hits = indicator(cols, n_col)
    ind_ref[...] = hits
    row = lax.broadcasted_iota(jnp.int32, (8, 8 * cols), 0)
    span = lax.broadcasted_iota(jnp.int32, (8, 8 * cols), 1) // cols
    grad_rows_ref[...] = dot(jnp.where(row == span, 1.0, 0.0).astype(BF16), x_ref[1, :, : 8 * cols], NT)
    x_all = x_ref[...].reshape(6 * CH, x_ref.shape[2])
    back_ref[...] = dot(w2_ref[...], x_all, NN)


def main_kernel(
    n_row, n_col, prev_ref, next_ref, row_ref, col_ref, k1c_ref, k1ct_ref, k1f_ref, bias_ref,
    x_ref, back_ref, grad_rows_ref, grad_cols_ref, ind_ref,
    out_ref, own_ref, pre_scr, act_scr, inner_scr, w_scr, chunk_scr,
):
    cols = col_ref.shape[1]
    top, bottom = off_edge("row", 0), off_edge("row", n_row - 1)
    left, right = off_edge("col", 0), off_edge("col", n_col - 1)
    edge_lane = lax.broadcasted_iota(jnp.int32, (CH, LANES), 1)
    row_ext = jnp.concatenate(
        [top * prev_ref[:16, :CH].astype(F32), row_ref[...].astype(F32), bottom * next_ref[:16, :CH].astype(F32)],
        axis=0,
    )
    row_cat = jnp.concatenate([row_ext[8 * a : 8 * a + 32] for a in range(3)], axis=1).astype(BF16)
    col_ext = jnp.concatenate(
        [left * prev_ref[16:, :].astype(F32), col_ref[...].astype(F32), right * next_ref[16:, :].astype(F32)], axis=1
    )
    taps = []
    for tap in range(3):
        moved = pltpu.roll(col_ext, (8 * (1 - tap)) % (cols + 2 * LANES), 1) if tap != 1 else col_ext
        low, high = pltpu.roll(moved[:, :LANES], 8, 1), pltpu.roll(moved[:, LANES + cols :], 8, 1)
        edge = jnp.where(edge_lane < 8, low, jnp.where(edge_lane < 16, high, 0.0))
        for width in (16, 32, 64):
            edge = edge + pltpu.roll(edge, width, 1)
        taps.append(jnp.concatenate([moved[:, LANES : LANES + cols], edge], axis=1))
    col_cat = jnp.concatenate(taps, axis=0).astype(BF16)
    terms = dot(k1c_ref[...], col_cat, NN)
    low, mid, high = (terms[CH * a : CH * (a + 1)] for a in range(3))
    mid = mid + bias_ref[...]
    col_part = [low + mid + high, top * low + mid + high, low + mid + bottom * high, low + mid + high]
    row_terms = dot(k1f_ref[...], row_cat, NT)
    row_part = jnp.concatenate(
        [
            jnp.concatenate([row_terms[CH * b : CH * (b + 1), 8 * eb : 8 * eb + 8] for b in range(3)], axis=1)
            for eb in range(4)
        ],
        axis=0,
    )
    hits = ind_ref[...]
    pre_scr[...] = dot_split(row_part, hits, NN)
    on_map = jnp.where(edge_lane % 16 < 8, left, right)
    sums_of = []
    for eb in range(4):
        rows = slice(CH * eb, CH * (eb + 1))
        total = jnp.zeros((CH, cols), F32)
        for k in range(9):
            span = slice(k * cols, (k + 1) * cols) if k < 8 else slice(8 * cols, 8 * cols + LANES)
            pre = pre_scr[rows, span] + (col_part[eb][:, :cols] if k < 8 else col_part[eb][:, cols:])
            sig = 1.0 / (1.0 + jnp.exp(-pre))
            held = sig
            if eb == 0:
                held = held * top
            if eb == 3:
                held = held * bottom
            if k == 8:
                held = held * on_map
            act_scr[rows, span] = (pre * held).astype(BF16)
            inner = (back_ref[rows, span] * (held * (1.0 + pre * (1.0 - sig)))).astype(BF16)
            inner_scr[rows, span] = inner
            if k < 8:
                total = total + inner.astype(F32)
            else:
                total = jnp.concatenate([total, inner.astype(F32)], axis=1)
        sums_of.append(total)

    full = dot(x_ref[...].reshape(6 * CH, x_ref.shape[2]), act_scr[...], NT)
    sums = dot(hits, inner_scr[...], NT)
    row_sums = jnp.concatenate(
        [
            jnp.concatenate([sums[8 * b : 8 * b + 8, CH * eb : CH * (eb + 1)] for b in range(3)], axis=1)
            for eb in range(4)
        ],
        axis=0,
    )
    spread_row = dot_split(row_sums, k1f_ref[...], NN)

    def part(eb, a):
        return spread_row[8 * eb : 8 * eb + 8, CH * a : CH * (a + 1)]

    reached = [sum(part(eb, pb - eb) for eb in range(4) if 0 <= pb - eb <= 2) for pb in range(6)]
    above, mine, below = (jnp.concatenate(reached[2 * k : 2 * k + 2], axis=1) for k in range(3))
    own_ref[...] = grad_rows_ref[...] + mine
    whole = sums_of[0] + sums_of[1] + sums_of[2] + sums_of[3]
    col_sums = jnp.concatenate(
        [whole - (1.0 - top) * sums_of[1], whole, whole - (1.0 - bottom) * sums_of[2]], axis=0
    )
    high = col_sums.astype(BF16)
    rest = (col_sums - high.astype(F32)).astype(BF16)
    k1ct = k1ct_ref[...]
    spread_col = dot(k1ct, high, NN) + dot(k1ct, rest, NN)
    nothing = jnp.zeros((CH, LANES), F32)
    total = jnp.concatenate([nothing, grad_cols_ref[...], nothing], axis=1)
    for tap in range(3):
        piece = spread_col[CH * tap : CH * (tap + 1)]
        edge = piece[:, cols:]
        for width in (16, 32, 64):
            edge = edge + pltpu.roll(edge, width, 1)
        low = jnp.where(edge_lane >= LANES - 8, pltpu.roll(edge, LANES - 8, 1), 0.0)
        high_edge = jnp.where(edge_lane < 8, pltpu.roll(edge, LANES - 8, 1), 0.0)
        piece = jnp.concatenate([low, piece[:, :cols], high_edge], axis=1)
        total = total + (pltpu.roll(piece, (8 * (tap - 1)) % (cols + 2 * LANES), 1) if tap != 1 else piece)
    one_row = dot_split(row_sums, row_cat, TN)
    one_col = dot(high, col_cat, NT) + dot(rest, col_cat, NT)
    gap = jnp.zeros((32, cols + LANES), F32)
    bias_row = dot_exact(jnp.ones((8, cols + LANES), F32), jnp.concatenate([gap, whole, gap], axis=0), NT)
    for a in range(3):
        for b in range(3):
            one = one_row[CH * b : CH * (b + 1), CH * a : CH * (a + 1)]
            one = one + one_col[CH * a : CH * (a + 1), CH * b : CH * (b + 1)]
            two = [
                full[CH * (2 * b + gb) : CH * (2 * b + gb + 1), CH * (a + gb) : CH * (a + gb + 1)] for gb in range(2)
            ]
            w_scr[CH * (3 * a + b) : CH * (3 * a + b + 1), :] = jnp.concatenate([one, two[0] + two[1]], axis=1)

    weights, chans, sums_end = chunk_rows(n_row)
    tail = total[:, :LANES] + total[:, cols + LANES :] + bias_row[:1, :]
    before = lax.axis_index("row") - 1
    for j in range(n_row):
        chunk_scr[j, :weights, :] = w_scr[weights * j : weights * (j + 1), :]
        share = slice(chans * j, chans * (j + 1))
        chunk_scr[j, weights : weights + chans, :] = total[share, LANES : 2 * LANES]
        chunk_scr[j, weights + chans : weights + 2 * chans, :] = total[share, cols : cols + LANES]
        chunk_scr[j, weights + 2 * chans : sums_end, :] = tail[share]
        chunk_scr[j, sums_end:, :] = jnp.where(before == j, above, below)
    out_ref[...] = chunk_scr[...].astype(BF16)


def row_sum_kernel(n_row, n_col, got_ref, own_ref, out_ref):
    sums_end = chunk_rows(n_row)[2]
    me = lax.axis_index("row")
    total = got_ref[0].astype(F32)
    for j in range(1, n_row):
        total = total + got_ref[j].astype(F32)
    total = total[:sums_end]
    before = got_ref[jnp.maximum(me - 1, 0)].astype(F32)[sums_end:]
    after = got_ref[jnp.minimum(me + 1, n_row - 1)].astype(F32)[sums_end:]
    rows = own_ref[...] + off_edge("row", 0) * before + off_edge("row", n_row - 1) * after
    for k in range(n_col):
        out_ref[k, :sums_end, :] = total
        out_ref[k, sums_end:, :] = rows


def col_sum_kernel(n_row, n_col, cols, got_ref, row_ref, bias_ref, out_ref):
    weights, chans, sums_end = chunk_rows(n_row)
    me = lax.axis_index("col")
    whole = math.sqrt(16 * n_row * cols * n_col)
    total = got_ref[0]
    for k in range(1, n_col):
        total = total + got_ref[k]
    rows = total[sums_end:, :] * (1.0 / math.sqrt(cols * n_col))
    row_ref[0:8, :] = rows[:, :CH]
    row_ref[8:16, :] = rows[:, CH:]
    bias_ref[...] = total[sums_end - 1 : sums_end, 32 : 32 + CH] * (1.0 / whole)
    scale = 1.0 / math.sqrt(16 * n_row)
    before = got_ref[jnp.maximum(me - 1, 0), weights + 2 * chans : sums_end, :] * off_edge("col", 0)
    after = got_ref[jnp.minimum(me + 1, n_col - 1), weights + 2 * chans : sums_end, :] * off_edge("col", n_col - 1)
    lane = lax.broadcasted_iota(jnp.int32, before.shape, 1)
    low = got_ref[me, weights : weights + chans, :] + jnp.where(lane < 16, before, 0.0)
    high = got_ref[me, weights + chans : weights + 2 * chans, :] + jnp.where(lane >= LANES - 16, after, 0.0)
    share = total[:weights, :] * (1.0 / whole)
    for j in range(n_row):
        out_ref[j, :weights, :] = share
        out_ref[j, weights : weights + chans, :] = low * scale
        out_ref[j, weights + chans : weights + 2 * chans, :] = high * scale
        if weights + 2 * chans < out_ref.shape[1]:
            out_ref[j, weights + 2 * chans :, :] = jnp.zeros((out_ref.shape[1] - weights - 2 * chans, LANES), F32)


def spread_kernel(n_row, got_ref, col_ref, one_ref, two_ref):
    weights, chans, _ = chunk_rows(n_row)
    for j in range(n_row):
        share = got_ref[j, :weights, :]
        one_ref[weights * j : weights * (j + 1), :] = share[:, :CH]
        two_ref[weights * j : weights * (j + 1), :] = share[:, CH:]
        col_ref[chans * j : chans * (j + 1), :LANES] = got_ref[j, weights : weights + chans, :]
        col_ref[chans * j : chans * (j + 1), LANES:] = got_ref[j, weights + chans : weights + 2 * chans, :]


PARAMS = pltpu.CompilerParams(vmem_limit_bytes=48 * 1024 * 1024)


def sds(shape, dtype=F32):
    return jax.ShapeDtypeStruct(shape, dtype)


def shards(n_row, n_col, grad_out, row_feat, col_feat, conv_one, bias_one, conv_two):
    cols = grad_out.shape[2]
    weights, chans, sums_end = chunk_rows(n_row)
    places = 8 * cols + LANES
    strip = pl.pallas_call(pack_kernel, out_shape=sds((16 + CH, LANES), BF16), compiler_params=PARAMS)(
        row_feat, col_feat.T
    )
    pairs = [
        (r * n_col + c, (r + 1) % n_row * n_col + (c + 1) % n_col) for r in range(n_row) for c in range(n_col)
    ]
    prev = lax.ppermute(strip, ("row", "col"), pairs)
    nxt = lax.ppermute(strip, ("row", "col"), [(target, source) for source, target in pairs])

    padded = jnp.pad(jnp.transpose(conv_two, (0, 3, 1, 2)), ((1, 1), (0, 0), (0, 0), (0, 0)))
    w2 = jnp.stack([padded[1:], padded[:-1]], axis=3).reshape(4 * CH, 6 * CH)
    k1c = jnp.transpose(conv_one, (0, 2, 1, 3)).reshape(3 * CH, 3 * CH)
    k1f = jnp.transpose(conv_one, (1, 2, 0, 3)).reshape(3 * CH, 3 * CH)

    held = pl.pallas_call(
        lambda *refs: own_kernel(n_col, *refs),
        out_shape=(
            sds((3, 2 * CH, places), BF16), sds((4 * CH, places)), sds((8, 2 * CH)), sds((CH, cols)),
            sds((24, places), BF16),
        ),
        scratch_shapes=[pltpu.VMEM((cols // LANES, CH * 16, LANES), F32)],
        compiler_params=PARAMS,
    )(grad_out, w2)
    chunks, own = pl.pallas_call(
        lambda *refs: main_kernel(n_row, n_col, *refs),
        out_shape=(sds((n_row, sums_end + 8, LANES), BF16), sds((8, LANES))),
        scratch_shapes=[
            pltpu.VMEM((4 * CH, places), F32),
            pltpu.VMEM((4 * CH, places), BF16),
            pltpu.VMEM((4 * CH, places), BF16),
            pltpu.VMEM((9 * CH, LANES), F32),
            pltpu.VMEM((n_row, sums_end + 8, LANES), F32),
        ],
        compiler_params=PARAMS,
    )(prev, nxt, row_feat, col_feat.T, k1c, k1c.T, k1f, bias_one[:, None], *held)
    got = lax.all_to_all(chunks, "row", 0, 0)
    copies = pl.pallas_call(
        lambda *refs: row_sum_kernel(n_row, n_col, *refs),
        out_shape=sds((n_col, sums_end + 8, LANES)),
        compiler_params=PARAMS,
    )(got, own)
    got = lax.all_to_all(copies, "col", 0, 0)
    end = -(-(weights + 2 * chans) // 8) * 8
    row_grad, bias_grad, copies = pl.pallas_call(
        lambda *refs: col_sum_kernel(n_row, n_col, cols, *refs),
        out_shape=(sds((16, CH)), sds((1, CH)), sds((n_row, end, LANES))),
        compiler_params=PARAMS,
    )(got)
    got = lax.all_to_all(copies, "row", 0, 0)
    col_grad, one, two = pl.pallas_call(
        lambda *refs: spread_kernel(n_row, *refs),
        out_shape=(sds((CH, cols)), sds((9 * CH, CH)), sds((9 * CH, CH))),
        compiler_params=PARAMS,
    )(got)
    shape = conv_one.shape
    return row_grad, col_grad.T, one.reshape(shape), bias_grad[0], two.reshape(shape)


def solution(mesh):
    in_specs = (P(None, "row", "col"), P("row", None), P("col", None), P(), P(), P())
    out_specs = (P("row", None), P("col", None), P(), P(), P())
    n_row, n_col = mesh.shape["row"], mesh.shape["col"]
    return jax.shard_map(
        lambda *args: shards(n_row, n_col, *args), mesh=mesh, in_specs=in_specs, out_specs=out_specs, check_vma=False
    )
```

```python
import math

import jax
import jax.numpy as jnp
from jax import lax
from jax.experimental import pallas as pl
from jax.experimental.pallas import tpu as pltpu
from jax.sharding import PartitionSpec as P

F32, BF16 = jnp.float32, jnp.bfloat16
NN = (((1,), (0,)), ((), ()))
NT = (((1,), (1,)), ((), ()))
TN = (((0,), (0,)), ((), ()))
CH = 64
LANES = 128


def dot(x, y, dims):
    return lax.dot_general(x, y, dims, preferred_element_type=F32)


def dot_exact(x, y, dims):
    return lax.dot_general(
        x.astype(F32), y.astype(F32), dims, precision=lax.Precision.HIGHEST, preferred_element_type=F32
    )


def chunk_rows(n_row):
    weights, chans = 9 * CH // n_row, CH // n_row
    return weights, chans, weights + 3 * chans


def dot_split(x, y, dims):
    high = x.astype(BF16)
    low = (x - high.astype(F32)).astype(BF16)
    y = y.astype(BF16)
    return dot(high, y, dims) + dot(low, y, dims)


def pack_kernel(row_hbm, col_hbm, out_ref, row_ref, col_ref, row_sem, col_sem):
    row_copy = pltpu.make_async_copy(row_hbm, row_ref, row_sem)
    col_copy = pltpu.make_async_copy(col_hbm, col_ref, col_sem)
    row_copy.start()
    col_copy.start()
    row_copy.wait()
    col_copy.wait()
    rows = row_ref[...].astype(F32)
    out_ref[:16, :] = jnp.concatenate([rows, jnp.zeros_like(rows)], axis=1).astype(BF16)
    cols = col_ref.shape[1]
    lane = lax.broadcasted_iota(jnp.int32, (CH, LANES), 1)
    first, last = col_ref[:, :LANES].astype(F32), col_ref[:, cols - LANES :].astype(F32)
    out_ref[16:, :] = jnp.where(lane < LANES // 2, first, last).astype(BF16)


def off_edge(axis, index):
    return jnp.where(lax.axis_index(axis) == index, 0.0, 1.0).astype(F32)


def indicator(cols, n_col):
    lane = lax.broadcasted_iota(jnp.int32, (8, cols), 1)
    row = lax.broadcasted_iota(jnp.int32, (8, cols), 0)
    me = lax.axis_index("col")
    off_map = ((lane < 8) & (me == 0), lane < 0, (lane >= cols - 8) & (me == n_col - 1))
    edge_lane = lax.broadcasted_iota(jnp.int32, (8, LANES), 1)
    edge_row = lax.broadcasted_iota(jnp.int32, (8, LANES), 0)
    edge = jnp.where(edge_lane // 16 == edge_row, 1.0, 0.0)
    taps = []
    for tap in range(3):
        on_map = jnp.logical_not(off_map[tap])
        main = [jnp.where(on_map & (row == k), 1.0, 0.0) for k in range(8)]
        taps.append(jnp.concatenate(main + [edge], axis=1))
    return jnp.concatenate(taps, axis=0).astype(BF16)


def own_kernel(
    n_col, grad_ref, one_ref, two_ref, bias_ref,
    x_ref, back_ref, grad_rows_ref, grad_cols_ref, ind_ref, k1c_ref, k1f_ref, bias_col_ref, rows_scr,
):
    cols = grad_ref.shape[2]
    one = [[one_ref[a, b].astype(F32) for b in range(3)] for a in range(3)]
    for k in range(3):
        rows = slice(CH * k, CH * (k + 1))
        k1c_ref[rows, :] = jnp.concatenate(one[k], axis=1).astype(BF16)
        k1f_ref[rows, :] = jnp.concatenate([one[a][k] for a in range(3)], axis=1).astype(BF16)
    nil = jnp.zeros((CH, CH), F32)
    two = [[two_ref[a, b].astype(F32) for b in range(3)] for a in range(3)]
    w2 = jnp.concatenate(
        [
            jnp.concatenate([two[eb - gb][b] if 0 <= eb - gb <= 2 else nil for eb in range(4)], axis=1)
            for b in range(3)
            for gb in range(2)
        ],
        axis=0,
    ).astype(BF16)
    bias = jnp.concatenate([bias_ref[...], jnp.zeros((1, LANES - CH), F32)], axis=1)
    bias_col_ref[...] = jnp.broadcast_to(bias, (8, LANES)).T[:CH, :]
    lane = lax.broadcasted_iota(jnp.int32, (CH, cols), 1)
    edge_lane = lax.broadcasted_iota(jnp.int32, (CH, LANES), 1)
    for piece in range(cols // LANES):
        wide = grad_ref[:, :, LANES * piece : LANES * (piece + 1)]
        rows_scr[piece] = wide.astype(F32).reshape(CH * 16, LANES)
    col_sum = jnp.zeros((CH, cols), F32)
    for half in range(2):
        rows = slice(half * CH, (half + 1) * CH)
        left = right = jnp.zeros((CH, LANES), F32)
        for k in range(8):
            pieces = [rows_scr[p, pl.ds(half * 8 + k, CH, stride=16), :] for p in range(cols // LANES)]
            line = jnp.concatenate(pieces, axis=1)
            col_sum = col_sum + line
            span = slice(k * cols, (k + 1) * cols)
            x_ref[1, rows, span] = line.astype(BF16)
            x_ref[0, rows, span] = jnp.where(lane < cols - 8, pltpu.roll(line, cols - 8, 1), 0.0).astype(BF16)
            x_ref[2, rows, span] = jnp.where(lane >= 8, pltpu.roll(line, 8, 1), 0.0).astype(BF16)
            first = pltpu.roll(pieces[0], 16 * k, 1) if k else pieces[0]
            last = pltpu.roll(pieces[-1], 16 * k + 16, 1) if k < 7 else pieces[-1]
            here = edge_lane // 16 == k
            left = jnp.where(here & (edge_lane % 16 < 8), first, left)
            right = jnp.where(here & (edge_lane % 16 >= 8), last, right)
        x_ref[0, rows, 8 * cols :] = left.astype(BF16)
        x_ref[1, rows, 8 * cols :] = jnp.zeros((CH, LANES), BF16)
        x_ref[2, rows, 8 * cols :] = right.astype(BF16)
    grad_cols_ref[...] = col_sum
    hits = indicator(cols, n_col)
    ind_ref[...] = hits
    row = lax.broadcasted_iota(jnp.int32, (8, 8 * cols), 0)
    span = lax.broadcasted_iota(jnp.int32, (8, 8 * cols), 1) // cols
    grad_rows_ref[...] = dot(jnp.where(row == span, 1.0, 0.0).astype(BF16), x_ref[1, :, : 8 * cols], NT)
    x_all = x_ref[...].reshape(6 * CH, x_ref.shape[2])
    back_ref[...] = dot(w2, x_all, TN)


def main_kernel(
    n_row, n_col, prev_ref, next_ref, row_ref, col_ref,
    x_ref, back_ref, grad_rows_ref, grad_cols_ref, ind_ref, k1c_ref, k1f_ref, bias_ref,
    out_ref, own_ref, pre_scr, act_scr, inner_scr, w_scr, chunk_scr,
):
    cols = col_ref.shape[1]
    top, bottom = off_edge("row", 0), off_edge("row", n_row - 1)
    left, right = off_edge("col", 0), off_edge("col", n_col - 1)
    edge_lane = lax.broadcasted_iota(jnp.int32, (CH, LANES), 1)
    row_ext = jnp.concatenate(
        [top * prev_ref[:16, :CH].astype(F32), row_ref[...].astype(F32), bottom * next_ref[:16, :CH].astype(F32)],
        axis=0,
    )
    row_cat = jnp.concatenate([row_ext[8 * a : 8 * a + 32] for a in range(3)], axis=1).astype(BF16)
    col_ext = jnp.concatenate(
        [left * prev_ref[16:, :].astype(F32), col_ref[...].astype(F32), right * next_ref[16:, :].astype(F32)], axis=1
    )
    taps = []
    for tap in range(3):
        moved = pltpu.roll(col_ext, (8 * (1 - tap)) % (cols + 2 * LANES), 1) if tap != 1 else col_ext
        low, high = pltpu.roll(moved[:, :LANES], 8, 1), pltpu.roll(moved[:, LANES + cols :], 8, 1)
        edge = jnp.where(edge_lane < 8, low, jnp.where(edge_lane < 16, high, 0.0))
        for width in (16, 32, 64):
            edge = edge + pltpu.roll(edge, width, 1)
        taps.append(jnp.concatenate([moved[:, LANES : LANES + cols], edge], axis=1))
    col_cat = jnp.concatenate(taps, axis=0).astype(BF16)
    terms = dot(k1c_ref[...], col_cat, NN)
    low, mid, high = (terms[CH * a : CH * (a + 1)] for a in range(3))
    mid = mid + bias_ref[:, :1]
    col_part = [low + mid + high, top * low + mid + high, low + mid + bottom * high, low + mid + high]
    row_terms = dot(k1f_ref[...], row_cat, NT)
    row_part = jnp.concatenate(
        [
            jnp.concatenate([row_terms[CH * b : CH * (b + 1), 8 * eb : 8 * eb + 8] for b in range(3)], axis=1)
            for eb in range(4)
        ],
        axis=0,
    )
    hits = ind_ref[...]
    pre_scr[...] = dot_split(row_part, hits, NN)
    on_map = jnp.where(edge_lane % 16 < 8, left, right)
    sums_of = []
    for eb in range(4):
        rows = slice(CH * eb, CH * (eb + 1))
        total = jnp.zeros((CH, cols), F32)
        for k in range(9):
            span = slice(k * cols, (k + 1) * cols) if k < 8 else slice(8 * cols, 8 * cols + LANES)
            pre = pre_scr[rows, span] + (col_part[eb][:, :cols] if k < 8 else col_part[eb][:, cols:])
            sig = 1.0 / (1.0 + jnp.exp(-pre))
            held = sig
            if eb == 0:
                held = held * top
            if eb == 3:
                held = held * bottom
            if k == 8:
                held = held * on_map
            act_scr[rows, span] = (pre * held).astype(BF16)
            inner = (back_ref[rows, span] * (held * (1.0 + pre * (1.0 - sig)))).astype(BF16)
            inner_scr[rows, span] = inner
            if k < 8:
                total = total + inner.astype(F32)
            else:
                total = jnp.concatenate([total, inner.astype(F32)], axis=1)
        sums_of.append(total)

    full = dot(x_ref[...].reshape(6 * CH, x_ref.shape[2]), act_scr[...], NT)
    sums = dot(hits, inner_scr[...], NT)
    row_sums = jnp.concatenate(
        [
            jnp.concatenate([sums[8 * b : 8 * b + 8, CH * eb : CH * (eb + 1)] for b in range(3)], axis=1)
            for eb in range(4)
        ],
        axis=0,
    )
    spread_row = dot_split(row_sums, k1f_ref[...], NN)

    def part(eb, a):
        return spread_row[8 * eb : 8 * eb + 8, CH * a : CH * (a + 1)]

    reached = [sum(part(eb, pb - eb) for eb in range(4) if 0 <= pb - eb <= 2) for pb in range(6)]
    above, mine, below = (jnp.concatenate(reached[2 * k : 2 * k + 2], axis=1) for k in range(3))
    own_ref[...] = grad_rows_ref[...] + mine
    whole = sums_of[0] + sums_of[1] + sums_of[2] + sums_of[3]
    col_sums = jnp.concatenate(
        [whole - (1.0 - top) * sums_of[1], whole, whole - (1.0 - bottom) * sums_of[2]], axis=0
    )
    high = col_sums.astype(BF16)
    rest = (col_sums - high.astype(F32)).astype(BF16)
    k1c = k1c_ref[...]
    spread_col = dot(k1c, high, TN) + dot(k1c, rest, TN)
    nothing = jnp.zeros((CH, LANES), F32)
    total = jnp.concatenate([nothing, grad_cols_ref[...], nothing], axis=1)
    for tap in range(3):
        piece = spread_col[CH * tap : CH * (tap + 1)]
        edge = piece[:, cols:]
        for width in (16, 32, 64):
            edge = edge + pltpu.roll(edge, width, 1)
        low = jnp.where(edge_lane >= LANES - 8, pltpu.roll(edge, LANES - 8, 1), 0.0)
        high_edge = jnp.where(edge_lane < 8, pltpu.roll(edge, LANES - 8, 1), 0.0)
        piece = jnp.concatenate([low, piece[:, :cols], high_edge], axis=1)
        total = total + (pltpu.roll(piece, (8 * (tap - 1)) % (cols + 2 * LANES), 1) if tap != 1 else piece)
    one_row = dot_split(row_sums, row_cat, TN)
    one_col = dot(high, col_cat, NT) + dot(rest, col_cat, NT)
    gap = jnp.zeros((32, cols + LANES), F32)
    bias_row = dot_exact(jnp.ones((8, cols + LANES), F32), jnp.concatenate([gap, whole, gap], axis=0), NT)
    for a in range(3):
        for b in range(3):
            one = one_row[CH * b : CH * (b + 1), CH * a : CH * (a + 1)]
            one = one + one_col[CH * a : CH * (a + 1), CH * b : CH * (b + 1)]
            two = [
                full[CH * (2 * b + gb) : CH * (2 * b + gb + 1), CH * (a + gb) : CH * (a + gb + 1)] for gb in range(2)
            ]
            w_scr[CH * (3 * a + b) : CH * (3 * a + b + 1), :] = jnp.concatenate([one, two[0] + two[1]], axis=1)

    weights, chans, sums_end = chunk_rows(n_row)
    tail = total[:, :LANES] + total[:, cols + LANES :] + bias_row[:1, :]
    before = lax.axis_index("row") - 1
    for j in range(n_row):
        chunk_scr[j, :weights, :] = w_scr[weights * j : weights * (j + 1), :]
        share = slice(chans * j, chans * (j + 1))
        chunk_scr[j, weights : weights + chans, :] = total[share, LANES : 2 * LANES]
        chunk_scr[j, weights + chans : weights + 2 * chans, :] = total[share, cols : cols + LANES]
        chunk_scr[j, weights + 2 * chans : sums_end, :] = tail[share]
        chunk_scr[j, sums_end:, :] = jnp.where(before == j, above, below)
    out_ref[...] = chunk_scr[...].astype(BF16)


def row_sum_kernel(n_row, n_col, got_ref, own_ref, out_ref):
    sums_end = chunk_rows(n_row)[2]
    me = lax.axis_index("row")
    total = got_ref[0].astype(F32)
    for j in range(1, n_row):
        total = total + got_ref[j].astype(F32)
    total = total[:sums_end]
    before = got_ref[jnp.maximum(me - 1, 0)].astype(F32)[sums_end:]
    after = got_ref[jnp.minimum(me + 1, n_row - 1)].astype(F32)[sums_end:]
    rows = own_ref[...] + off_edge("row", 0) * before + off_edge("row", n_row - 1) * after
    whole = jnp.concatenate([total, rows], axis=0).astype(BF16)
    for k in range(n_col):
        out_ref[k] = whole


def col_sum_kernel(n_row, n_col, cols, got_ref, row_ref, bias_ref, out_ref, scr):
    weights, chans, sums_end = chunk_rows(n_row)
    me = lax.axis_index("col")
    whole = math.sqrt(16 * n_row * cols * n_col)
    total = got_ref[0].astype(F32)
    for k in range(1, n_col):
        total = total + got_ref[k].astype(F32)
    rows = total[sums_end:, :] * (1.0 / math.sqrt(cols * n_col))
    row_ref[0:8, :] = rows[:, :CH]
    row_ref[8:16, :] = rows[:, CH:]
    bias_ref[...] = total[sums_end - 1 : sums_end, 32 : 32 + CH] * (1.0 / whole)
    before = got_ref[jnp.maximum(me - 1, 0)].astype(F32) * off_edge("col", 0)
    after = got_ref[jnp.minimum(me + 1, n_col - 1)].astype(F32) * off_edge("col", n_col - 1)
    mine = got_ref[me].astype(F32)
    edge = slice(weights + 2 * chans, sums_end)
    lane = lax.broadcasted_iota(jnp.int32, (chans, LANES), 1)
    low = mine[weights : weights + chans] + jnp.where(lane < 16, before[edge], 0.0)
    high = mine[weights + chans : weights + 2 * chans] + jnp.where(lane >= LANES - 16, after[edge], 0.0)
    scale = 1.0 / math.sqrt(16 * n_row)
    scr[...] = jnp.zeros(scr.shape, F32)
    scr[:weights, :] = total[:weights] * (1.0 / whole)
    scr[weights : weights + chans, :] = low * scale
    scr[weights + chans : weights + 2 * chans, :] = high * scale
    share = scr[...].astype(BF16)
    for j in range(n_row):
        out_ref[j] = share


def spread_kernel(n_row, got_ref, col_ref, one_ref, two_ref):
    weights, chans, _ = chunk_rows(n_row)
    for j in range(n_row):
        chunk = got_ref[j].astype(F32)
        one_ref[weights * j : weights * (j + 1), :] = chunk[:weights, :CH]
        two_ref[weights * j : weights * (j + 1), :] = chunk[:weights, CH:]
        col_ref[chans * j : chans * (j + 1), :LANES] = chunk[weights : weights + chans]
        col_ref[chans * j : chans * (j + 1), LANES:] = chunk[weights + chans : weights + 2 * chans]


PARAMS = pltpu.CompilerParams(vmem_limit_bytes=48 * 1024 * 1024)


def sds(shape, dtype=F32):
    return jax.ShapeDtypeStruct(shape, dtype)


def shards(n_row, n_col, grad_out, row_feat, col_feat, conv_one, bias_one, conv_two):
    cols = grad_out.shape[2]
    weights, chans, sums_end = chunk_rows(n_row)
    places = 8 * cols + LANES
    strip = pl.pallas_call(
        pack_kernel,
        out_shape=sds((16 + CH, LANES), BF16),
        in_specs=[pl.BlockSpec(memory_space=pltpu.HBM)] * 2,
        scratch_shapes=[
            pltpu.VMEM((16, CH), BF16),
            pltpu.VMEM((CH, cols), BF16),
            pltpu.SemaphoreType.DMA,
            pltpu.SemaphoreType.DMA,
        ],
        compiler_params=PARAMS,
    )(row_feat, col_feat.T)
    pairs = [
        (r * n_col + c, (r + 1) % n_row * n_col + (c + 1) % n_col) for r in range(n_row) for c in range(n_col)
    ]
    prev = lax.ppermute(strip, ("row", "col"), pairs)
    nxt = lax.ppermute(strip, ("row", "col"), [(target, source) for source, target in pairs])

    held = pl.pallas_call(
        lambda *refs: own_kernel(n_col, *refs),
        out_shape=(
            sds((3, 2 * CH, places), BF16), sds((4 * CH, places)), sds((8, 2 * CH)), sds((CH, cols)),
            sds((24, places), BF16), sds((3 * CH, 3 * CH), BF16), sds((3 * CH, 3 * CH), BF16), sds((CH, 8)),
        ),
        scratch_shapes=[pltpu.VMEM((cols // LANES, CH * 16, LANES), F32)],
        compiler_params=PARAMS,
    )(grad_out, conv_one, conv_two, bias_one.reshape(1, CH))
    chunks, own = pl.pallas_call(
        lambda *refs: main_kernel(n_row, n_col, *refs),
        out_shape=(sds((n_row, sums_end + 8, LANES), BF16), sds((8, LANES))),
        scratch_shapes=[
            pltpu.VMEM((4 * CH, places), F32),
            pltpu.VMEM((4 * CH, places), BF16),
            pltpu.VMEM((4 * CH, places), BF16),
            pltpu.VMEM((9 * CH, LANES), F32),
            pltpu.VMEM((n_row, sums_end + 8, LANES), F32),
        ],
        compiler_params=PARAMS,
    )(prev, nxt, row_feat, col_feat.T, *held)
    got = lax.all_to_all(chunks, "row", 0, 0)
    copies = pl.pallas_call(
        lambda *refs: row_sum_kernel(n_row, n_col, *refs),
        out_shape=sds((n_col, sums_end + 8, LANES), BF16),
        compiler_params=PARAMS,
    )(got, own)
    got = lax.all_to_all(copies, "col", 0, 0)
    end = -(-(weights + 2 * chans) // 16) * 16
    row_grad, bias_grad, copies = pl.pallas_call(
        lambda *refs: col_sum_kernel(n_row, n_col, cols, *refs),
        out_shape=(sds((16, CH)), sds((1, CH)), sds((n_row, end, LANES), BF16)),
        scratch_shapes=[pltpu.VMEM((end, LANES), F32)],
        compiler_params=PARAMS,
    )(got)
    got = lax.all_to_all(copies, "row", 0, 0)
    col_grad, one, two = pl.pallas_call(
        lambda *refs: spread_kernel(n_row, *refs),
        out_shape=(sds((CH, cols)), sds((9 * CH, CH)), sds((9 * CH, CH))),
        compiler_params=PARAMS,
    )(got)
    shape = conv_one.shape
    return row_grad, col_grad.T, one.reshape(shape), bias_grad[0], two.reshape(shape)


def solution(mesh):
    in_specs = (P(None, "row", "col"), P("row", None), P("col", None), P(), P(), P())
    out_specs = (P("row", None), P("col", None), P(), P(), P())
    n_row, n_col = mesh.shape["row"], mesh.shape["col"]
    return jax.shard_map(
        lambda *args: shards(n_row, n_col, *args), mesh=mesh, in_specs=in_specs, out_specs=out_specs, check_vma=False
    )
```

```python
import math

import jax
import jax.numpy as jnp
from jax import lax
from jax.experimental import pallas as pl
from jax.experimental.pallas import tpu as pltpu
from jax.sharding import PartitionSpec as P

F32, BF16 = jnp.float32, jnp.bfloat16
NN = (((1,), (0,)), ((), ()))
NT = (((1,), (1,)), ((), ()))
TN = (((0,), (0,)), ((), ()))
CH = 64
LANES = 128


def dot(x, y, dims):
    return lax.dot_general(x, y, dims, preferred_element_type=F32)


def dot_exact(x, y, dims):
    return lax.dot_general(
        x.astype(F32), y.astype(F32), dims, precision=lax.Precision.HIGHEST, preferred_element_type=F32
    )


def chunk_rows(n_row):
    weights, chans = 9 * CH // n_row, CH // n_row
    return weights, chans, weights + 3 * chans


def dot_split(x, y, dims):
    high = x.astype(BF16)
    low = (x - high.astype(F32)).astype(BF16)
    y = y.astype(BF16)
    return dot(high, y, dims) + dot(low, y, dims)


def pack_kernel(row_hbm, col_hbm, out_ref, row_ref, col_ref, row_sem, col_sem):
    row_copy = pltpu.make_async_copy(row_hbm, row_ref, row_sem)
    col_copy = pltpu.make_async_copy(col_hbm, col_ref, col_sem)
    row_copy.start()
    col_copy.start()
    row_copy.wait()
    col_copy.wait()
    rows = row_ref[...].astype(F32)
    out_ref[:16, :] = jnp.concatenate([rows, jnp.zeros_like(rows)], axis=1).astype(BF16)
    cols = col_ref.shape[1]
    lane = lax.broadcasted_iota(jnp.int32, (CH, LANES), 1)
    first, last = col_ref[:, :LANES].astype(F32), col_ref[:, cols - LANES :].astype(F32)
    out_ref[16:, :] = jnp.where(lane < LANES // 2, first, last).astype(BF16)


def off_edge(axis, index):
    return jnp.where(lax.axis_index(axis) == index, 0.0, 1.0).astype(F32)


def indicator(cols, n_col):
    lane = lax.broadcasted_iota(jnp.int32, (8, cols), 1)
    row = lax.broadcasted_iota(jnp.int32, (8, cols), 0)
    me = lax.axis_index("col")
    off_map = ((lane < 8) & (me == 0), lane < 0, (lane >= cols - 8) & (me == n_col - 1))
    edge_lane = lax.broadcasted_iota(jnp.int32, (8, LANES), 1)
    edge_row = lax.broadcasted_iota(jnp.int32, (8, LANES), 0)
    edge = jnp.where(edge_lane // 16 == edge_row, 1.0, 0.0)
    taps = []
    for tap in range(3):
        on_map = jnp.logical_not(off_map[tap])
        main = [jnp.where(on_map & (row == k), 1.0, 0.0) for k in range(8)]
        taps.append(jnp.concatenate(main + [edge], axis=1))
    return jnp.concatenate(taps, axis=0).astype(BF16)


def own_kernel(
    n_col, grad_hbm, one_hbm, two_hbm, bias_hbm, row_hbm, col_hbm,
    x_ref, back_ref, grad_rows_ref, grad_cols_ref, ind_ref, k1c_ref, k1f_ref, bias_col_ref, row_ref, col_ref,
    rows_scr, grad_ref, one_ref, two_ref, bias_ref, sems,
):
    cols = grad_ref.shape[2]
    pairs = (
        (one_hbm, one_ref), (two_hbm, two_ref), (bias_hbm, bias_ref), (row_hbm, row_ref), (col_hbm, col_ref),
        (grad_hbm, grad_ref),
    )
    copies = [pltpu.make_async_copy(source, target, sems.at[k]) for k, (source, target) in enumerate(pairs)]
    for copy in copies:
        copy.start()
    hits = indicator(cols, n_col)
    ind_ref[...] = hits
    for copy in copies[:-1]:
        copy.wait()
    one = [[one_ref[a, b].astype(F32) for b in range(3)] for a in range(3)]
    for k in range(3):
        rows = slice(CH * k, CH * (k + 1))
        k1c_ref[rows, :] = jnp.concatenate(one[k], axis=1).astype(BF16)
        k1f_ref[rows, :] = jnp.concatenate([one[a][k] for a in range(3)], axis=1).astype(BF16)
    nil = jnp.zeros((CH, CH), F32)
    two = [[two_ref[a, b].astype(F32) for b in range(3)] for a in range(3)]
    w2 = jnp.concatenate(
        [
            jnp.concatenate([two[eb - gb][b] if 0 <= eb - gb <= 2 else nil for eb in range(4)], axis=1)
            for b in range(3)
            for gb in range(2)
        ],
        axis=0,
    ).astype(BF16)
    bias = jnp.concatenate([bias_ref[...], jnp.zeros((1, LANES - CH), F32)], axis=1)
    bias_col_ref[...] = jnp.broadcast_to(bias, (8, LANES)).T[:CH, :]
    copies[-1].wait()
    lane = lax.broadcasted_iota(jnp.int32, (CH, cols), 1)
    edge_lane = lax.broadcasted_iota(jnp.int32, (CH, LANES), 1)
    for piece in range(cols // LANES):
        wide = grad_ref[:, :, LANES * piece : LANES * (piece + 1)]
        rows_scr[piece] = wide.astype(F32).reshape(CH * 16, LANES)
    col_sum = jnp.zeros((CH, cols), F32)
    for half in range(2):
        rows = slice(half * CH, (half + 1) * CH)
        left = right = jnp.zeros((CH, LANES), F32)
        for k in range(8):
            pieces = [rows_scr[p, pl.ds(half * 8 + k, CH, stride=16), :] for p in range(cols // LANES)]
            line = jnp.concatenate(pieces, axis=1)
            col_sum = col_sum + line
            span = slice(k * cols, (k + 1) * cols)
            x_ref[1, rows, span] = line.astype(BF16)
            x_ref[0, rows, span] = jnp.where(lane < cols - 8, pltpu.roll(line, cols - 8, 1), 0.0).astype(BF16)
            x_ref[2, rows, span] = jnp.where(lane >= 8, pltpu.roll(line, 8, 1), 0.0).astype(BF16)
            first = pltpu.roll(pieces[0], 16 * k, 1) if k else pieces[0]
            last = pltpu.roll(pieces[-1], 16 * k + 16, 1) if k < 7 else pieces[-1]
            here = edge_lane // 16 == k
            left = jnp.where(here & (edge_lane % 16 < 8), first, left)
            right = jnp.where(here & (edge_lane % 16 >= 8), last, right)
        x_ref[0, rows, 8 * cols :] = left.astype(BF16)
        x_ref[1, rows, 8 * cols :] = jnp.zeros((CH, LANES), BF16)
        x_ref[2, rows, 8 * cols :] = right.astype(BF16)
    grad_cols_ref[...] = col_sum
    row = lax.broadcasted_iota(jnp.int32, (8, 8 * cols), 0)
    span = lax.broadcasted_iota(jnp.int32, (8, 8 * cols), 1) // cols
    grad_rows_ref[...] = dot(jnp.where(row == span, 1.0, 0.0).astype(BF16), x_ref[1, :, : 8 * cols], NT)
    x_all = x_ref[...].reshape(6 * CH, x_ref.shape[2])
    back_ref[...] = dot(w2, x_all, TN)


def main_kernel(
    n_row, n_col, prev_ref, next_ref,
    x_ref, back_ref, grad_rows_ref, grad_cols_ref, ind_ref, k1c_ref, k1f_ref, bias_ref, row_ref, col_ref,
    out_ref, own_ref, pre_scr, act_scr, inner_scr, w_scr, chunk_scr,
):
    cols = col_ref.shape[1]
    top, bottom = off_edge("row", 0), off_edge("row", n_row - 1)
    left, right = off_edge("col", 0), off_edge("col", n_col - 1)
    edge_lane = lax.broadcasted_iota(jnp.int32, (CH, LANES), 1)
    row_ext = jnp.concatenate(
        [top * prev_ref[:16, :CH].astype(F32), row_ref[...].astype(F32), bottom * next_ref[:16, :CH].astype(F32)],
        axis=0,
    )
    row_cat = jnp.concatenate([row_ext[8 * a : 8 * a + 32] for a in range(3)], axis=1).astype(BF16)
    col_ext = jnp.concatenate(
        [left * prev_ref[16:, :].astype(F32), col_ref[...].astype(F32), right * next_ref[16:, :].astype(F32)], axis=1
    )
    taps = []
    for tap in range(3):
        moved = pltpu.roll(col_ext, (8 * (1 - tap)) % (cols + 2 * LANES), 1) if tap != 1 else col_ext
        low, high = pltpu.roll(moved[:, :LANES], 8, 1), pltpu.roll(moved[:, LANES + cols :], 8, 1)
        edge = jnp.where(edge_lane < 8, low, jnp.where(edge_lane < 16, high, 0.0))
        for width in (16, 32, 64):
            edge = edge + pltpu.roll(edge, width, 1)
        taps.append(jnp.concatenate([moved[:, LANES : LANES + cols], edge], axis=1))
    col_cat = jnp.concatenate(taps, axis=0).astype(BF16)
    terms = dot(k1c_ref[...], col_cat, NN)
    low, mid, high = (terms[CH * a : CH * (a + 1)] for a in range(3))
    mid = mid + bias_ref[:, :1]
    col_part = [low + mid + high, top * low + mid + high, low + mid + bottom * high, low + mid + high]
    row_terms = dot(k1f_ref[...], row_cat, NT)
    row_part = jnp.concatenate(
        [
            jnp.concatenate([row_terms[CH * b : CH * (b + 1), 8 * eb : 8 * eb + 8] for b in range(3)], axis=1)
            for eb in range(4)
        ],
        axis=0,
    )
    hits = ind_ref[...]
    pre_scr[...] = dot_split(row_part, hits, NN)
    on_map = jnp.where(edge_lane % 16 < 8, left, right)
    sums_of = []
    for eb in range(4):
        rows = slice(CH * eb, CH * (eb + 1))
        total = jnp.zeros((CH, cols), F32)
        for k in range(9):
            span = slice(k * cols, (k + 1) * cols) if k < 8 else slice(8 * cols, 8 * cols + LANES)
            pre = pre_scr[rows, span] + (col_part[eb][:, :cols] if k < 8 else col_part[eb][:, cols:])
            sig = 1.0 / (1.0 + jnp.exp(-pre))
            held = sig
            if eb == 0:
                held = held * top
            if eb == 3:
                held = held * bottom
            if k == 8:
                held = held * on_map
            act_scr[rows, span] = (pre * held).astype(BF16)
            inner = (back_ref[rows, span] * (held * (1.0 + pre * (1.0 - sig)))).astype(BF16)
            inner_scr[rows, span] = inner
            if k < 8:
                total = total + inner.astype(F32)
            else:
                total = jnp.concatenate([total, inner.astype(F32)], axis=1)
        sums_of.append(total)

    full = dot(x_ref[...].reshape(6 * CH, x_ref.shape[2]), act_scr[...], NT)
    sums = dot(hits, inner_scr[...], NT)
    row_sums = jnp.concatenate(
        [
            jnp.concatenate([sums[8 * b : 8 * b + 8, CH * eb : CH * (eb + 1)] for b in range(3)], axis=1)
            for eb in range(4)
        ],
        axis=0,
    )
    spread_row = dot_split(row_sums, k1f_ref[...], NN)

    def part(eb, a):
        return spread_row[8 * eb : 8 * eb + 8, CH * a : CH * (a + 1)]

    reached = [sum(part(eb, pb - eb) for eb in range(4) if 0 <= pb - eb <= 2) for pb in range(6)]
    above, mine, below = (jnp.concatenate(reached[2 * k : 2 * k + 2], axis=1) for k in range(3))
    own_ref[...] = grad_rows_ref[...] + mine
    whole = sums_of[0] + sums_of[1] + sums_of[2] + sums_of[3]
    col_sums = jnp.concatenate(
        [whole - (1.0 - top) * sums_of[1], whole, whole - (1.0 - bottom) * sums_of[2]], axis=0
    )
    high = col_sums.astype(BF16)
    rest = (col_sums - high.astype(F32)).astype(BF16)
    k1c = k1c_ref[...]
    spread_col = dot(k1c, high, TN) + dot(k1c, rest, TN)
    nothing = jnp.zeros((CH, LANES), F32)
    total = jnp.concatenate([nothing, grad_cols_ref[...], nothing], axis=1)
    for tap in range(3):
        piece = spread_col[CH * tap : CH * (tap + 1)]
        edge = piece[:, cols:]
        for width in (16, 32, 64):
            edge = edge + pltpu.roll(edge, width, 1)
        low = jnp.where(edge_lane >= LANES - 8, pltpu.roll(edge, LANES - 8, 1), 0.0)
        high_edge = jnp.where(edge_lane < 8, pltpu.roll(edge, LANES - 8, 1), 0.0)
        piece = jnp.concatenate([low, piece[:, :cols], high_edge], axis=1)
        total = total + (pltpu.roll(piece, (8 * (tap - 1)) % (cols + 2 * LANES), 1) if tap != 1 else piece)
    one_row = dot_split(row_sums, row_cat, TN)
    one_col = dot(high, col_cat, NT) + dot(rest, col_cat, NT)
    gap = jnp.zeros((32, cols + LANES), F32)
    bias_row = dot_exact(jnp.ones((8, cols + LANES), F32), jnp.concatenate([gap, whole, gap], axis=0), NT)
    for a in range(3):
        for b in range(3):
            one = one_row[CH * b : CH * (b + 1), CH * a : CH * (a + 1)]
            one = one + one_col[CH * a : CH * (a + 1), CH * b : CH * (b + 1)]
            two = [
                full[CH * (2 * b + gb) : CH * (2 * b + gb + 1), CH * (a + gb) : CH * (a + gb + 1)] for gb in range(2)
            ]
            w_scr[CH * (3 * a + b) : CH * (3 * a + b + 1), :] = jnp.concatenate([one, two[0] + two[1]], axis=1)

    weights, chans, sums_end = chunk_rows(n_row)
    tail = total[:, :LANES] + total[:, cols + LANES :] + bias_row[:1, :]
    before = lax.axis_index("row") - 1
    for j in range(n_row):
        chunk_scr[j, :weights, :] = w_scr[weights * j : weights * (j + 1), :]
        share = slice(chans * j, chans * (j + 1))
        chunk_scr[j, weights : weights + chans, :] = total[share, LANES : 2 * LANES]
        chunk_scr[j, weights + chans : weights + 2 * chans, :] = total[share, cols : cols + LANES]
        chunk_scr[j, weights + 2 * chans : sums_end, :] = tail[share]
        chunk_scr[j, sums_end:, :] = jnp.where(before == j, above, below)
    out_ref[...] = chunk_scr[...].astype(BF16)


def row_sum_kernel(n_row, n_col, got_ref, own_ref, out_ref):
    sums_end = chunk_rows(n_row)[2]
    me = lax.axis_index("row")
    total = got_ref[0].astype(F32)
    for j in range(1, n_row):
        total = total + got_ref[j].astype(F32)
    total = total[:sums_end]
    before = got_ref[jnp.maximum(me - 1, 0)].astype(F32)[sums_end:]
    after = got_ref[jnp.minimum(me + 1, n_row - 1)].astype(F32)[sums_end:]
    rows = own_ref[...] + off_edge("row", 0) * before + off_edge("row", n_row - 1) * after
    whole = jnp.concatenate([total, rows], axis=0).astype(BF16)
    for k in range(n_col):
        out_ref[k] = whole


def col_sum_kernel(n_row, n_col, cols, got_ref, row_ref, bias_ref, out_ref, scr):
    weights, chans, sums_end = chunk_rows(n_row)
    me = lax.axis_index("col")
    whole = math.sqrt(16 * n_row * cols * n_col)
    total = got_ref[0].astype(F32)
    for k in range(1, n_col):
        total = total + got_ref[k].astype(F32)
    rows = total[sums_end:, :] * (1.0 / math.sqrt(cols * n_col))
    row_ref[0:8, :] = rows[:, :CH]
    row_ref[8:16, :] = rows[:, CH:]
    bias_ref[...] = total[sums_end - 1 : sums_end, 32 : 32 + CH] * (1.0 / whole)
    before = got_ref[jnp.maximum(me - 1, 0)].astype(F32) * off_edge("col", 0)
    after = got_ref[jnp.minimum(me + 1, n_col - 1)].astype(F32) * off_edge("col", n_col - 1)
    mine = got_ref[me].astype(F32)
    edge = slice(weights + 2 * chans, sums_end)
    lane = lax.broadcasted_iota(jnp.int32, (chans, LANES), 1)
    low = mine[weights : weights + chans] + jnp.where(lane < 16, before[edge], 0.0)
    high = mine[weights + chans : weights + 2 * chans] + jnp.where(lane >= LANES - 16, after[edge], 0.0)
    scale = 1.0 / math.sqrt(16 * n_row)
    scr[...] = jnp.zeros(scr.shape, F32)
    scr[:weights, :] = total[:weights] * (1.0 / whole)
    scr[weights : weights + chans, :] = low * scale
    scr[weights + chans : weights + 2 * chans, :] = high * scale
    share = scr[...].astype(BF16)
    for j in range(n_row):
        out_ref[j] = share


def spread_kernel(n_row, got_ref, col_ref, one_ref, two_ref):
    weights, chans, _ = chunk_rows(n_row)
    for j in range(n_row):
        chunk = got_ref[j].astype(F32)
        one_ref[weights * j : weights * (j + 1), :] = chunk[:weights, :CH]
        two_ref[weights * j : weights * (j + 1), :] = chunk[:weights, CH:]
        col_ref[chans * j : chans * (j + 1), :LANES] = chunk[weights : weights + chans]
        col_ref[chans * j : chans * (j + 1), LANES:] = chunk[weights + chans : weights + 2 * chans]


PARAMS = pltpu.CompilerParams(vmem_limit_bytes=48 * 1024 * 1024)


def sds(shape, dtype=F32):
    return jax.ShapeDtypeStruct(shape, dtype)


def shards(n_row, n_col, grad_out, row_feat, col_feat, conv_one, bias_one, conv_two):
    cols = grad_out.shape[2]
    weights, chans, sums_end = chunk_rows(n_row)
    places = 8 * cols + LANES
    grad_out, row_feat, col_turned, conv_one, conv_two, bias_row = (
        pltpu.with_memory_space_constraint(x, pltpu.HBM)
        for x in (grad_out, row_feat, col_feat.T, conv_one, conv_two, bias_one.reshape(1, CH))
    )
    strip = pl.pallas_call(
        pack_kernel,
        out_shape=sds((16 + CH, LANES), BF16),
        in_specs=[pl.BlockSpec(memory_space=pltpu.HBM)] * 2,
        scratch_shapes=[
            pltpu.VMEM((16, CH), BF16),
            pltpu.VMEM((CH, cols), BF16),
            pltpu.SemaphoreType.DMA,
            pltpu.SemaphoreType.DMA,
        ],
        compiler_params=PARAMS,
    )(row_feat, col_turned)
    pairs = [
        (r * n_col + c, (r + 1) % n_row * n_col + (c + 1) % n_col) for r in range(n_row) for c in range(n_col)
    ]
    prev = lax.ppermute(strip, ("row", "col"), pairs)
    nxt = lax.ppermute(strip, ("row", "col"), [(target, source) for source, target in pairs])

    held = pl.pallas_call(
        lambda *refs: own_kernel(n_col, *refs),
        out_shape=(
            sds((3, 2 * CH, places), BF16), sds((4 * CH, places)), sds((8, 2 * CH)), sds((CH, cols)),
            sds((24, places), BF16), sds((3 * CH, 3 * CH), BF16), sds((3 * CH, 3 * CH), BF16), sds((CH, 8)),
            sds((16, CH), BF16), sds((CH, cols), BF16),
        ),
        in_specs=[pl.BlockSpec(memory_space=pltpu.HBM)] * 6,
        scratch_shapes=[
            pltpu.VMEM((cols // LANES, CH * 16, LANES), F32),
            pltpu.VMEM(grad_out.shape, BF16),
            pltpu.VMEM(conv_one.shape, BF16),
            pltpu.VMEM(conv_two.shape, BF16),
            pltpu.VMEM((1, CH), F32),
            pltpu.SemaphoreType.DMA((6,)),
        ],
        compiler_params=PARAMS,
    )(grad_out, conv_one, conv_two, bias_row, row_feat, col_turned)
    chunks, own = pl.pallas_call(
        lambda *refs: main_kernel(n_row, n_col, *refs),
        out_shape=(sds((n_row, sums_end + 8, LANES), BF16), sds((8, LANES))),
        scratch_shapes=[
            pltpu.VMEM((4 * CH, places), F32),
            pltpu.VMEM((4 * CH, places), BF16),
            pltpu.VMEM((4 * CH, places), BF16),
            pltpu.VMEM((9 * CH, LANES), F32),
            pltpu.VMEM((n_row, sums_end + 8, LANES), F32),
        ],
        compiler_params=PARAMS,
    )(prev, nxt, *held)
    got = lax.all_to_all(chunks, "row", 0, 0)
    copies = pl.pallas_call(
        lambda *refs: row_sum_kernel(n_row, n_col, *refs),
        out_shape=sds((n_col, sums_end + 8, LANES), BF16),
        compiler_params=PARAMS,
    )(got, own)
    got = lax.all_to_all(copies, "col", 0, 0)
    end = -(-(weights + 2 * chans) // 16) * 16
    row_grad, bias_grad, copies = pl.pallas_call(
        lambda *refs: col_sum_kernel(n_row, n_col, cols, *refs),
        out_shape=(sds((16, CH)), sds((1, CH)), sds((n_row, end, LANES), BF16)),
        scratch_shapes=[pltpu.VMEM((end, LANES), F32)],
        compiler_params=PARAMS,
    )(got)
    got = lax.all_to_all(copies, "row", 0, 0)
    col_grad, one, two = pl.pallas_call(
        lambda *refs: spread_kernel(n_row, *refs),
        out_shape=(sds((CH, cols)), sds((9 * CH, CH)), sds((9 * CH, CH))),
        compiler_params=PARAMS,
    )(got)
    shape = conv_one.shape
    return row_grad, col_grad.T, one.reshape(shape), bias_grad[0], two.reshape(shape)


def solution(mesh):
    in_specs = (P(None, "row", "col"), P("row", None), P("col", None), P(), P(), P())
    out_specs = (P("row", None), P("col", None), P(), P(), P())
    n_row, n_col = mesh.shape["row"], mesh.shape["col"]
    return jax.shard_map(
        lambda *args: shards(n_row, n_col, *args), mesh=mesh, in_specs=in_specs, out_specs=out_specs, check_vma=False
    )
```

```python
import math

import jax
import jax.numpy as jnp
from jax import lax
from jax.experimental import pallas as pl
from jax.experimental.pallas import tpu as pltpu
from jax.sharding import PartitionSpec as P

F32, BF16 = jnp.float32, jnp.bfloat16
NN = (((1,), (0,)), ((), ()))
NT = (((1,), (1,)), ((), ()))
TN = (((0,), (0,)), ((), ()))
CH = 64
LANES = 128


def dot(x, y, dims):
    return lax.dot_general(x, y, dims, preferred_element_type=F32)


def dot_exact(x, y, dims):
    return lax.dot_general(
        x.astype(F32), y.astype(F32), dims, precision=lax.Precision.HIGHEST, preferred_element_type=F32
    )


def chunk_rows(n_row):
    weights, chans = 9 * CH // n_row, CH // n_row
    return weights, chans, weights + 3 * chans


def dot_split(x, y, dims):
    high = x.astype(BF16)
    low = (x - high.astype(F32)).astype(BF16)
    y = y.astype(BF16)
    return dot(high, y, dims) + dot(low, y, dims)


def pack_kernel(row_hbm, col_hbm, out_ref, row_ref, col_ref, row_sem, col_sem):
    row_copy = pltpu.make_async_copy(row_hbm, row_ref, row_sem)
    col_copy = pltpu.make_async_copy(col_hbm, col_ref, col_sem)
    row_copy.start()
    col_copy.start()
    row_copy.wait()
    col_copy.wait()
    rows = row_ref[...].astype(F32)
    out_ref[:16, :] = jnp.concatenate([rows, jnp.zeros_like(rows)], axis=1).astype(BF16)
    cols = col_ref.shape[1]
    lane = lax.broadcasted_iota(jnp.int32, (CH, LANES), 1)
    first, last = col_ref[:, :LANES].astype(F32), col_ref[:, cols - LANES :].astype(F32)
    out_ref[16:, :] = jnp.where(lane < LANES // 2, first, last).astype(BF16)


def off_edge(axis, index):
    return jnp.where(lax.axis_index(axis) == index, 0.0, 1.0).astype(F32)


def indicator(cols, n_col):
    lane = lax.broadcasted_iota(jnp.int32, (8, cols), 1)
    row = lax.broadcasted_iota(jnp.int32, (8, cols), 0)
    me = lax.axis_index("col")
    off_map = ((lane < 8) & (me == 0), lane < 0, (lane >= cols - 8) & (me == n_col - 1))
    edge_lane = lax.broadcasted_iota(jnp.int32, (8, LANES), 1)
    edge_row = lax.broadcasted_iota(jnp.int32, (8, LANES), 0)
    edge = jnp.where(edge_lane // 16 == edge_row, 1.0, 0.0)
    taps = []
    for tap in range(3):
        on_map = jnp.logical_not(off_map[tap])
        main = [jnp.where(on_map & (row == k), 1.0, 0.0) for k in range(8)]
        taps.append(jnp.concatenate(main + [edge], axis=1))
    return jnp.concatenate(taps, axis=0).astype(BF16)


def own_kernel(
    n_col, grad_hbm, one_hbm, two_hbm, bias_hbm, row_hbm, col_hbm,
    x_ref, back_ref, grad_rows_ref, grad_cols_ref, ind_ref, k1c_ref, k1f_ref, bias_col_ref, row_ref, col_ref,
    rows_scr, grad_ref, one_ref, two_ref, bias_ref, sems,
):
    cols = grad_ref.shape[2]
    pairs = (
        (one_hbm, one_ref), (two_hbm, two_ref), (bias_hbm, bias_ref), (row_hbm, row_ref), (col_hbm, col_ref),
        (grad_hbm, grad_ref),
    )
    copies = [pltpu.make_async_copy(source, target, sems.at[k]) for k, (source, target) in enumerate(pairs)]
    for copy in copies:
        copy.start()
    hits = indicator(cols, n_col)
    ind_ref[...] = hits
    for copy in copies[:-1]:
        copy.wait()
    one = [[one_ref[a, b].astype(F32) for b in range(3)] for a in range(3)]
    for k in range(3):
        rows = slice(CH * k, CH * (k + 1))
        k1c_ref[rows, :] = jnp.concatenate(one[k], axis=1).astype(BF16)
        k1f_ref[rows, :] = jnp.concatenate([one[a][k] for a in range(3)], axis=1).astype(BF16)
    nil = jnp.zeros((CH, CH), F32)
    two = [[two_ref[a, b].astype(F32) for b in range(3)] for a in range(3)]
    w2 = jnp.concatenate(
        [
            jnp.concatenate([two[eb - gb][b] if 0 <= eb - gb <= 2 else nil for eb in range(4)], axis=1)
            for b in range(3)
            for gb in range(2)
        ],
        axis=0,
    ).astype(BF16)
    bias = jnp.concatenate([bias_ref[...], jnp.zeros((1, LANES - CH), F32)], axis=1)
    bias_col_ref[...] = jnp.broadcast_to(bias, (8, LANES)).T[:CH, :]
    copies[-1].wait()
    lane = lax.broadcasted_iota(jnp.int32, (CH, cols), 1)
    edge_lane = lax.broadcasted_iota(jnp.int32, (CH, LANES), 1)
    for piece in range(cols // LANES):
        wide = grad_ref[:, :, LANES * piece : LANES * (piece + 1)]
        rows_scr[piece] = wide.astype(F32).reshape(CH * 16, LANES)
    col_sum = jnp.zeros((CH, cols), F32)
    for half in range(2):
        rows = slice(half * CH, (half + 1) * CH)
        left = right = jnp.zeros((CH, LANES), F32)
        for k in range(8):
            pieces = [rows_scr[p, pl.ds(half * 8 + k, CH, stride=16), :] for p in range(cols // LANES)]
            line = jnp.concatenate(pieces, axis=1)
            col_sum = col_sum + line
            span = slice(k * cols, (k + 1) * cols)
            x_ref[1, rows, span] = line.astype(BF16)
            x_ref[0, rows, span] = jnp.where(lane < cols - 8, pltpu.roll(line, cols - 8, 1), 0.0).astype(BF16)
            x_ref[2, rows, span] = jnp.where(lane >= 8, pltpu.roll(line, 8, 1), 0.0).astype(BF16)
            first = pltpu.roll(pieces[0], 16 * k, 1) if k else pieces[0]
            last = pltpu.roll(pieces[-1], 16 * k + 16, 1) if k < 7 else pieces[-1]
            here = edge_lane // 16 == k
            left = jnp.where(here & (edge_lane % 16 < 8), first, left)
            right = jnp.where(here & (edge_lane % 16 >= 8), last, right)
        x_ref[0, rows, 8 * cols :] = left.astype(BF16)
        x_ref[1, rows, 8 * cols :] = jnp.zeros((CH, LANES), BF16)
        x_ref[2, rows, 8 * cols :] = right.astype(BF16)
    grad_cols_ref[...] = col_sum
    row = lax.broadcasted_iota(jnp.int32, (8, 8 * cols), 0)
    span = lax.broadcasted_iota(jnp.int32, (8, 8 * cols), 1) // cols
    grad_rows_ref[...] = dot(jnp.where(row == span, 1.0, 0.0).astype(BF16), x_ref[1, :, : 8 * cols], NT)
    x_all = x_ref[...].reshape(6 * CH, x_ref.shape[2])
    back_ref[...] = dot(w2, x_all, TN)


def main_kernel(
    n_row, n_col, twin_ref, row_side_ref, col_side_ref,
    x_ref, back_ref, grad_rows_ref, grad_cols_ref, ind_ref, k1c_ref, k1f_ref, bias_ref, row_ref, col_ref,
    out_ref, own_ref, pre_scr, act_scr, inner_scr, w_scr, chunk_scr,
):
    cols = col_ref.shape[1]
    top, bottom = off_edge("row", 0), off_edge("row", n_row - 1)
    left, right = off_edge("col", 0), off_edge("col", n_col - 1)
    edge_lane = lax.broadcasted_iota(jnp.int32, (CH, LANES), 1)
    odd_row, odd_col = lax.axis_index("row") % 2 == 1, lax.axis_index("col") % 2 == 1
    twin, other = twin_ref[:16, :CH].astype(F32), row_side_ref[:16, :CH].astype(F32)
    row_ext = jnp.concatenate(
        [jnp.where(odd_row, twin, other), row_ref[...].astype(F32), jnp.where(odd_row, other, twin)], axis=0
    )
    row_cat = jnp.concatenate([row_ext[8 * a : 8 * a + 32] for a in range(3)], axis=1).astype(BF16)
    twin, other = twin_ref[16:, :].astype(F32), col_side_ref[16:, :].astype(F32)
    col_ext = jnp.concatenate(
        [jnp.where(odd_col, twin, other), col_ref[...].astype(F32), jnp.where(odd_col, other, twin)], axis=1
    )
    taps = []
    for tap in range(3):
        moved = pltpu.roll(col_ext, (8 * (1 - tap)) % (cols + 2 * LANES), 1) if tap != 1 else col_ext
        low, high = pltpu.roll(moved[:, :LANES], 8, 1), pltpu.roll(moved[:, LANES + cols :], 8, 1)
        edge = jnp.where(edge_lane < 8, low, jnp.where(edge_lane < 16, high, 0.0))
        for width in (16, 32, 64):
            edge = edge + pltpu.roll(edge, width, 1)
        taps.append(jnp.concatenate([moved[:, LANES : LANES + cols], edge], axis=1))
    col_cat = jnp.concatenate(taps, axis=0).astype(BF16)
    terms = dot(k1c_ref[...], col_cat, NN)
    low, mid, high = (terms[CH * a : CH * (a + 1)] for a in range(3))
    mid = mid + bias_ref[:, :1]
    col_part = [low + mid + high, top * low + mid + high, low + mid + bottom * high, low + mid + high]
    row_terms = dot(k1f_ref[...], row_cat, NT)
    row_part = jnp.concatenate(
        [
            jnp.concatenate([row_terms[CH * b : CH * (b + 1), 8 * eb : 8 * eb + 8] for b in range(3)], axis=1)
            for eb in range(4)
        ],
        axis=0,
    )
    hits = ind_ref[...]
    pre_scr[...] = dot_split(row_part, hits, NN)
    on_map = jnp.where(edge_lane % 16 < 8, left, right)
    sums_of = []
    for eb in range(4):
        rows = slice(CH * eb, CH * (eb + 1))
        total = jnp.zeros((CH, cols), F32)
        for k in range(9):
            span = slice(k * cols, (k + 1) * cols) if k < 8 else slice(8 * cols, 8 * cols + LANES)
            pre = pre_scr[rows, span] + (col_part[eb][:, :cols] if k < 8 else col_part[eb][:, cols:])
            sig = 1.0 / (1.0 + jnp.exp(-pre))
            held = sig
            if eb == 0:
                held = held * top
            if eb == 3:
                held = held * bottom
            if k == 8:
                held = held * on_map
            act_scr[rows, span] = (pre * held).astype(BF16)
            inner = (back_ref[rows, span] * (held * (1.0 + pre * (1.0 - sig)))).astype(BF16)
            inner_scr[rows, span] = inner
            if k < 8:
                total = total + inner.astype(F32)
            else:
                total = jnp.concatenate([total, inner.astype(F32)], axis=1)
        sums_of.append(total)

    full = dot(x_ref[...].reshape(6 * CH, x_ref.shape[2]), act_scr[...], NT)
    sums = dot(hits, inner_scr[...], NT)
    row_sums = jnp.concatenate(
        [
            jnp.concatenate([sums[8 * b : 8 * b + 8, CH * eb : CH * (eb + 1)] for b in range(3)], axis=1)
            for eb in range(4)
        ],
        axis=0,
    )
    spread_row = dot_split(row_sums, k1f_ref[...], NN)

    def part(eb, a):
        return spread_row[8 * eb : 8 * eb + 8, CH * a : CH * (a + 1)]

    reached = [sum(part(eb, pb - eb) for eb in range(4) if 0 <= pb - eb <= 2) for pb in range(6)]
    above, mine, below = (jnp.concatenate(reached[2 * k : 2 * k + 2], axis=1) for k in range(3))
    own_ref[...] = grad_rows_ref[...] + mine
    whole = sums_of[0] + sums_of[1] + sums_of[2] + sums_of[3]
    col_sums = jnp.concatenate(
        [whole - (1.0 - top) * sums_of[1], whole, whole - (1.0 - bottom) * sums_of[2]], axis=0
    )
    high = col_sums.astype(BF16)
    rest = (col_sums - high.astype(F32)).astype(BF16)
    k1c = k1c_ref[...]
    spread_col = dot(k1c, high, TN) + dot(k1c, rest, TN)
    nothing = jnp.zeros((CH, LANES), F32)
    total = jnp.concatenate([nothing, grad_cols_ref[...], nothing], axis=1)
    for tap in range(3):
        piece = spread_col[CH * tap : CH * (tap + 1)]
        edge = piece[:, cols:]
        for width in (16, 32, 64):
            edge = edge + pltpu.roll(edge, width, 1)
        low = jnp.where(edge_lane >= LANES - 8, pltpu.roll(edge, LANES - 8, 1), 0.0)
        high_edge = jnp.where(edge_lane < 8, pltpu.roll(edge, LANES - 8, 1), 0.0)
        piece = jnp.concatenate([low, piece[:, :cols], high_edge], axis=1)
        total = total + (pltpu.roll(piece, (8 * (tap - 1)) % (cols + 2 * LANES), 1) if tap != 1 else piece)
    one_row = dot_split(row_sums, row_cat, TN)
    one_col = dot(high, col_cat, NT) + dot(rest, col_cat, NT)
    gap = jnp.zeros((32, cols + LANES), F32)
    bias_row = dot_exact(jnp.ones((8, cols + LANES), F32), jnp.concatenate([gap, whole, gap], axis=0), NT)
    for a in range(3):
        for b in range(3):
            one = one_row[CH * b : CH * (b + 1), CH * a : CH * (a + 1)]
            one = one + one_col[CH * a : CH * (a + 1), CH * b : CH * (b + 1)]
            two = [
                full[CH * (2 * b + gb) : CH * (2 * b + gb + 1), CH * (a + gb) : CH * (a + gb + 1)] for gb in range(2)
            ]
            w_scr[CH * (3 * a + b) : CH * (3 * a + b + 1), :] = jnp.concatenate([one, two[0] + two[1]], axis=1)

    weights, chans, sums_end = chunk_rows(n_row)
    tail = total[:, :LANES] + total[:, cols + LANES :] + bias_row[:1, :]
    before = lax.axis_index("row") - 1
    for j in range(n_row):
        chunk_scr[j, :weights, :] = w_scr[weights * j : weights * (j + 1), :]
        share = slice(chans * j, chans * (j + 1))
        chunk_scr[j, weights : weights + chans, :] = total[share, LANES : 2 * LANES]
        chunk_scr[j, weights + chans : weights + 2 * chans, :] = total[share, cols : cols + LANES]
        chunk_scr[j, weights + 2 * chans : sums_end, :] = tail[share]
        chunk_scr[j, sums_end:, :] = jnp.where(before == j, above, below)
    out_ref[...] = chunk_scr[...].astype(BF16)


def row_sum_kernel(n_row, n_col, got_ref, own_ref, out_ref):
    sums_end = chunk_rows(n_row)[2]
    me = lax.axis_index("row")
    total = got_ref[0].astype(F32)
    for j in range(1, n_row):
        total = total + got_ref[j].astype(F32)
    total = total[:sums_end]
    before = got_ref[jnp.maximum(me - 1, 0)].astype(F32)[sums_end:]
    after = got_ref[jnp.minimum(me + 1, n_row - 1)].astype(F32)[sums_end:]
    rows = own_ref[...] + off_edge("row", 0) * before + off_edge("row", n_row - 1) * after
    whole = jnp.concatenate([total, rows], axis=0).astype(BF16)
    for k in range(n_col):
        out_ref[k] = whole


def col_sum_kernel(n_row, n_col, cols, got_ref, row_ref, bias_ref, out_ref, scr):
    weights, chans, sums_end = chunk_rows(n_row)
    me = lax.axis_index("col")
    whole = math.sqrt(16 * n_row * cols * n_col)
    total = got_ref[0].astype(F32)
    for k in range(1, n_col):
        total = total + got_ref[k].astype(F32)
    rows = total[sums_end:, :] * (1.0 / math.sqrt(cols * n_col))
    row_ref[0:8, :] = rows[:, :CH]
    row_ref[8:16, :] = rows[:, CH:]
    bias_ref[...] = total[sums_end - 1 : sums_end, 32 : 32 + CH] * (1.0 / whole)
    before = got_ref[jnp.maximum(me - 1, 0)].astype(F32) * off_edge("col", 0)
    after = got_ref[jnp.minimum(me + 1, n_col - 1)].astype(F32) * off_edge("col", n_col - 1)
    mine = got_ref[me].astype(F32)
    edge = slice(weights + 2 * chans, sums_end)
    lane = lax.broadcasted_iota(jnp.int32, (chans, LANES), 1)
    low = mine[weights : weights + chans] + jnp.where(lane < 16, before[edge], 0.0)
    high = mine[weights + chans : weights + 2 * chans] + jnp.where(lane >= LANES - 16, after[edge], 0.0)
    scale = 1.0 / math.sqrt(16 * n_row)
    scr[...] = jnp.zeros(scr.shape, F32)
    scr[:weights, :] = total[:weights] * (1.0 / whole)
    scr[weights : weights + chans, :] = low * scale
    scr[weights + chans : weights + 2 * chans, :] = high * scale
    share = scr[...].astype(BF16)
    for j in range(n_row):
        out_ref[j] = share


def spread_kernel(n_row, got_ref, col_ref, one_ref, two_ref):
    weights, chans, _ = chunk_rows(n_row)
    for j in range(n_row):
        chunk = got_ref[j].astype(F32)
        one_ref[weights * j : weights * (j + 1), :] = chunk[:weights, :CH]
        two_ref[weights * j : weights * (j + 1), :] = chunk[:weights, CH:]
        col_ref[chans * j : chans * (j + 1), :LANES] = chunk[weights : weights + chans]
        col_ref[chans * j : chans * (j + 1), LANES:] = chunk[weights + chans : weights + 2 * chans]


PARAMS = pltpu.CompilerParams(vmem_limit_bytes=48 * 1024 * 1024)


def sds(shape, dtype=F32):
    return jax.ShapeDtypeStruct(shape, dtype)


def shards(n_row, n_col, grad_out, row_feat, col_feat, conv_one, bias_one, conv_two):
    cols = grad_out.shape[2]
    weights, chans, sums_end = chunk_rows(n_row)
    places = 8 * cols + LANES
    grad_out, row_feat, col_turned, conv_one, conv_two, bias_row = (
        pltpu.with_memory_space_constraint(x, pltpu.HBM)
        for x in (grad_out, row_feat, col_feat.T, conv_one, conv_two, bias_one.reshape(1, CH))
    )
    strip = pl.pallas_call(
        pack_kernel,
        out_shape=sds((16 + CH, LANES), BF16),
        in_specs=[pl.BlockSpec(memory_space=pltpu.HBM)] * 2,
        scratch_shapes=[
            pltpu.VMEM((16, CH), BF16),
            pltpu.VMEM((CH, cols), BF16),
            pltpu.SemaphoreType.DMA,
            pltpu.SemaphoreType.DMA,
        ],
        compiler_params=PARAMS,
    )(row_feat, col_turned)
    both = [(r * n_col + c, (r ^ 1) * n_col + (c ^ 1)) for r in range(n_row) for c in range(n_col)]

    def others(count):
        ups = [(k, k + 1) for k in range(1, count - 1, 2)]
        return ups + [(high, low) for low, high in ups]

    twin = lax.ppermute(strip, ("row", "col"), both)
    row_side = lax.ppermute(strip, "row", others(n_row))
    col_side = lax.ppermute(strip, "col", others(n_col))

    held = pl.pallas_call(
        lambda *refs: own_kernel(n_col, *refs),
        out_shape=(
            sds((3, 2 * CH, places), BF16), sds((4 * CH, places)), sds((8, 2 * CH)), sds((CH, cols)),
            sds((24, places), BF16), sds((3 * CH, 3 * CH), BF16), sds((3 * CH, 3 * CH), BF16), sds((CH, 8)),
            sds((16, CH), BF16), sds((CH, cols), BF16),
        ),
        in_specs=[pl.BlockSpec(memory_space=pltpu.HBM)] * 6,
        scratch_shapes=[
            pltpu.VMEM((cols // LANES, CH * 16, LANES), F32),
            pltpu.VMEM(grad_out.shape, BF16),
            pltpu.VMEM(conv_one.shape, BF16),
            pltpu.VMEM(conv_two.shape, BF16),
            pltpu.VMEM((1, CH), F32),
            pltpu.SemaphoreType.DMA((6,)),
        ],
        compiler_params=PARAMS,
    )(grad_out, conv_one, conv_two, bias_row, row_feat, col_turned)
    chunks, own = pl.pallas_call(
        lambda *refs: main_kernel(n_row, n_col, *refs),
        out_shape=(sds((n_row, sums_end + 8, LANES), BF16), sds((8, LANES))),
        scratch_shapes=[
            pltpu.VMEM((4 * CH, places), F32),
            pltpu.VMEM((4 * CH, places), BF16),
            pltpu.VMEM((4 * CH, places), BF16),
            pltpu.VMEM((9 * CH, LANES), F32),
            pltpu.VMEM((n_row, sums_end + 8, LANES), F32),
        ],
        compiler_params=PARAMS,
    )(twin, row_side, col_side, *held)
    got = lax.all_to_all(chunks, "row", 0, 0)
    copies = pl.pallas_call(
        lambda *refs: row_sum_kernel(n_row, n_col, *refs),
        out_shape=sds((n_col, sums_end + 8, LANES), BF16),
        compiler_params=PARAMS,
    )(got, own)
    got = lax.all_to_all(copies, "col", 0, 0)
    end = -(-(weights + 2 * chans) // 16) * 16
    row_grad, bias_grad, copies = pl.pallas_call(
        lambda *refs: col_sum_kernel(n_row, n_col, cols, *refs),
        out_shape=(sds((16, CH)), sds((1, CH)), sds((n_row, end, LANES), BF16)),
        scratch_shapes=[pltpu.VMEM((end, LANES), F32)],
        compiler_params=PARAMS,
    )(got)
    got = lax.all_to_all(copies, "row", 0, 0)
    col_grad, one, two = pl.pallas_call(
        lambda *refs: spread_kernel(n_row, *refs),
        out_shape=(sds((CH, cols)), sds((9 * CH, CH)), sds((9 * CH, CH))),
        compiler_params=PARAMS,
    )(got)
    shape = conv_one.shape
    return row_grad, col_grad.T, one.reshape(shape), bias_grad[0], two.reshape(shape)


def solution(mesh):
    in_specs = (P(None, "row", "col"), P("row", None), P("col", None), P(), P(), P())
    out_specs = (P("row", None), P("col", None), P(), P(), P())
    n_row, n_col = mesh.shape["row"], mesh.shape["col"]
    return jax.shard_map(
        lambda *args: shards(n_row, n_col, *args), mesh=mesh, in_specs=in_specs, out_specs=out_specs, check_vma=False
    )
```

```python
import math

import jax
import jax.numpy as jnp
from jax import lax
from jax.experimental import pallas as pl
from jax.experimental.pallas import tpu as pltpu
from jax.sharding import PartitionSpec as P

F32, BF16 = jnp.float32, jnp.bfloat16
NN = (((1,), (0,)), ((), ()))
NT = (((1,), (1,)), ((), ()))
TN = (((0,), (0,)), ((), ()))
CH = 64
LANES = 128


def dot(x, y, dims):
    return lax.dot_general(x, y, dims, preferred_element_type=F32)


def dot_exact(x, y, dims):
    return lax.dot_general(
        x.astype(F32), y.astype(F32), dims, precision=lax.Precision.HIGHEST, preferred_element_type=F32
    )


def chunk_rows(n_row):
    weights, chans = 9 * CH // n_row, CH // n_row
    return weights, chans, weights + 3 * chans


def dot_split(x, y, dims):
    high = x.astype(BF16)
    low = (x - high.astype(F32)).astype(BF16)
    y = y.astype(BF16)
    return dot(high, y, dims) + dot(low, y, dims)


def pack_kernel(row_hbm, col_hbm, out_ref, row_ref, col_ref, row_sem, col_sem):
    row_copy = pltpu.make_async_copy(row_hbm, row_ref, row_sem)
    col_copy = pltpu.make_async_copy(col_hbm, col_ref, col_sem)
    row_copy.start()
    col_copy.start()
    row_copy.wait()
    col_copy.wait()
    rows = row_ref[...].astype(F32)
    out_ref[:16, :] = jnp.concatenate([rows, jnp.zeros_like(rows)], axis=1).astype(BF16)
    cols = col_ref.shape[1]
    lane = lax.broadcasted_iota(jnp.int32, (CH, LANES), 1)
    first, last = col_ref[:, :LANES].astype(F32), col_ref[:, cols - LANES :].astype(F32)
    out_ref[16:, :] = jnp.where(lane < LANES // 2, first, last).astype(BF16)


def off_edge(axis, index):
    return jnp.where(lax.axis_index(axis) == index, 0.0, 1.0).astype(F32)


def indicator(cols, n_col):
    lane = lax.broadcasted_iota(jnp.int32, (8, cols), 1)
    row = lax.broadcasted_iota(jnp.int32, (8, cols), 0)
    me = lax.axis_index("col")
    off_map = ((lane < 8) & (me == 0), lane < 0, (lane >= cols - 8) & (me == n_col - 1))
    edge_lane = lax.broadcasted_iota(jnp.int32, (8, LANES), 1)
    edge_row = lax.broadcasted_iota(jnp.int32, (8, LANES), 0)
    edge = jnp.where(edge_lane // 16 == edge_row, 1.0, 0.0)
    taps = []
    for tap in range(3):
        on_map = jnp.logical_not(off_map[tap])
        main = [jnp.where(on_map & (row == k), 1.0, 0.0) for k in range(8)]
        taps.append(jnp.concatenate(main + [edge], axis=1))
    return jnp.concatenate(taps, axis=0).astype(BF16)


def own_kernel(
    n_col, grad_hbm, one_hbm, two_hbm, bias_hbm, row_hbm, col_hbm,
    x_ref, back_ref, grad_rows_ref, grad_cols_ref, ind_ref, k1c_ref, k1f_ref, bias_col_ref, row_ref, col_ref,
    rows_scr, grad_ref, one_ref, two_ref, bias_ref, sems,
):
    cols = grad_ref.shape[2]
    pairs = (
        (one_hbm, one_ref), (two_hbm, two_ref), (bias_hbm, bias_ref), (row_hbm, row_ref), (col_hbm, col_ref),
        (grad_hbm, grad_ref),
    )
    copies = [pltpu.make_async_copy(source, target, sems.at[k]) for k, (source, target) in enumerate(pairs)]
    for copy in copies:
        copy.start()
    hits = indicator(cols, n_col)
    ind_ref[...] = hits
    for copy in copies[:-1]:
        copy.wait()
    one = [[one_ref[a, b].astype(F32) for b in range(3)] for a in range(3)]
    for k in range(3):
        rows = slice(CH * k, CH * (k + 1))
        k1c_ref[rows, :] = jnp.concatenate(one[k], axis=1).astype(BF16)
        k1f_ref[rows, :] = jnp.concatenate([one[a][k] for a in range(3)], axis=1).astype(BF16)
    nil = jnp.zeros((CH, CH), F32)
    two = [[two_ref[a, b].astype(F32) for b in range(3)] for a in range(3)]
    w2 = jnp.concatenate(
        [
            jnp.concatenate([two[eb - gb][b] if 0 <= eb - gb <= 2 else nil for eb in range(4)], axis=1)
            for b in range(3)
            for gb in range(2)
        ],
        axis=0,
    ).astype(BF16)
    bias = jnp.concatenate([bias_ref[...], jnp.zeros((1, LANES - CH), F32)], axis=1)
    bias_col_ref[...] = jnp.broadcast_to(bias, (8, LANES)).T[:CH, :]
    copies[-1].wait()
    lane = lax.broadcasted_iota(jnp.int32, (CH, cols), 1)
    edge_lane = lax.broadcasted_iota(jnp.int32, (CH, LANES), 1)
    for piece in range(cols // LANES):
        wide = grad_ref[:, :, LANES * piece : LANES * (piece + 1)]
        rows_scr[piece] = wide.astype(F32).reshape(CH * 16, LANES)
    col_sum = jnp.zeros((CH, cols), F32)
    for half in range(2):
        rows = slice(half * CH, (half + 1) * CH)
        left = right = jnp.zeros((CH, LANES), F32)
        for k in range(8):
            pieces = [rows_scr[p, pl.ds(half * 8 + k, CH, stride=16), :] for p in range(cols // LANES)]
            line = jnp.concatenate(pieces, axis=1)
            col_sum = col_sum + line
            span = slice(k * cols, (k + 1) * cols)
            x_ref[1, rows, span] = line.astype(BF16)
            x_ref[0, rows, span] = jnp.where(lane < cols - 8, pltpu.roll(line, cols - 8, 1), 0.0).astype(BF16)
            x_ref[2, rows, span] = jnp.where(lane >= 8, pltpu.roll(line, 8, 1), 0.0).astype(BF16)
            first = pltpu.roll(pieces[0], 16 * k, 1) if k else pieces[0]
            last = pltpu.roll(pieces[-1], 16 * k + 16, 1) if k < 7 else pieces[-1]
            here = edge_lane // 16 == k
            left = jnp.where(here & (edge_lane % 16 < 8), first, left)
            right = jnp.where(here & (edge_lane % 16 >= 8), last, right)
        x_ref[0, rows, 8 * cols :] = left.astype(BF16)
        x_ref[1, rows, 8 * cols :] = jnp.zeros((CH, LANES), BF16)
        x_ref[2, rows, 8 * cols :] = right.astype(BF16)
    grad_cols_ref[...] = col_sum
    row = lax.broadcasted_iota(jnp.int32, (8, 8 * cols), 0)
    span = lax.broadcasted_iota(jnp.int32, (8, 8 * cols), 1) // cols
    grad_rows_ref[...] = dot(jnp.where(row == span, 1.0, 0.0).astype(BF16), x_ref[1, :, : 8 * cols], NT)
    x_all = x_ref[...].reshape(6 * CH, x_ref.shape[2])
    back_ref[...] = dot(w2, x_all, TN)


def main_kernel(
    n_row, n_col, twin_ref, far_ref,
    x_ref, back_ref, grad_rows_ref, grad_cols_ref, ind_ref, k1c_ref, k1f_ref, bias_ref, row_ref, col_ref,
    out_ref, own_ref, pre_scr, act_scr, inner_scr, w_scr, chunk_scr,
):
    cols = col_ref.shape[1]
    top, bottom = off_edge("row", 0), off_edge("row", n_row - 1)
    left, right = off_edge("col", 0), off_edge("col", n_col - 1)
    edge_lane = lax.broadcasted_iota(jnp.int32, (CH, LANES), 1)
    odd_row, odd_col = lax.axis_index("row") % 2 == 1, lax.axis_index("col") % 2 == 1
    twin, other = twin_ref[:16, :CH].astype(F32), far_ref[:16, :CH].astype(F32) * (top * bottom)
    row_ext = jnp.concatenate(
        [jnp.where(odd_row, twin, other), row_ref[...].astype(F32), jnp.where(odd_row, other, twin)], axis=0
    )
    row_cat = jnp.concatenate([row_ext[8 * a : 8 * a + 32] for a in range(3)], axis=1).astype(BF16)
    twin, other = twin_ref[16:, :].astype(F32), far_ref[16:, :].astype(F32) * (left * right)
    col_ext = jnp.concatenate(
        [jnp.where(odd_col, twin, other), col_ref[...].astype(F32), jnp.where(odd_col, other, twin)], axis=1
    )
    taps = []
    for tap in range(3):
        moved = pltpu.roll(col_ext, (8 * (1 - tap)) % (cols + 2 * LANES), 1) if tap != 1 else col_ext
        low, high = pltpu.roll(moved[:, :LANES], 8, 1), pltpu.roll(moved[:, LANES + cols :], 8, 1)
        edge = jnp.where(edge_lane < 8, low, jnp.where(edge_lane < 16, high, 0.0))
        for width in (16, 32, 64):
            edge = edge + pltpu.roll(edge, width, 1)
        taps.append(jnp.concatenate([moved[:, LANES : LANES + cols], edge], axis=1))
    col_cat = jnp.concatenate(taps, axis=0).astype(BF16)
    terms = dot(k1c_ref[...], col_cat, NN)
    low, mid, high = (terms[CH * a : CH * (a + 1)] for a in range(3))
    mid = mid + bias_ref[:, :1]
    col_part = [low + mid + high, top * low + mid + high, low + mid + bottom * high, low + mid + high]
    row_terms = dot(k1f_ref[...], row_cat, NT)
    row_part = jnp.concatenate(
        [
            jnp.concatenate([row_terms[CH * b : CH * (b + 1), 8 * eb : 8 * eb + 8] for b in range(3)], axis=1)
            for eb in range(4)
        ],
        axis=0,
    )
    hits = ind_ref[...]
    pre_scr[...] = dot_split(row_part, hits, NN)
    on_map = jnp.where(edge_lane % 16 < 8, left, right)
    sums_of = []
    for eb in range(4):
        rows = slice(CH * eb, CH * (eb + 1))
        total = jnp.zeros((CH, cols), F32)
        for k in range(9):
            span = slice(k * cols, (k + 1) * cols) if k < 8 else slice(8 * cols, 8 * cols + LANES)
            pre = pre_scr[rows, span] + (col_part[eb][:, :cols] if k < 8 else col_part[eb][:, cols:])
            sig = 1.0 / (1.0 + jnp.exp(-pre))
            held = sig
            if eb == 0:
                held = held * top
            if eb == 3:
                held = held * bottom
            if k == 8:
                held = held * on_map
            act_scr[rows, span] = (pre * held).astype(BF16)
            inner = (back_ref[rows, span] * (held * (1.0 + pre * (1.0 - sig)))).astype(BF16)
            inner_scr[rows, span] = inner
            if k < 8:
                total = total + inner.astype(F32)
            else:
                total = jnp.concatenate([total, inner.astype(F32)], axis=1)
        sums_of.append(total)

    full = dot(x_ref[...].reshape(6 * CH, x_ref.shape[2]), act_scr[...], NT)
    sums = dot(hits, inner_scr[...], NT)
    row_sums = jnp.concatenate(
        [
            jnp.concatenate([sums[8 * b : 8 * b + 8, CH * eb : CH * (eb + 1)] for b in range(3)], axis=1)
            for eb in range(4)
        ],
        axis=0,
    )
    spread_row = dot_split(row_sums, k1f_ref[...], NN)

    def part(eb, a):
        return spread_row[8 * eb : 8 * eb + 8, CH * a : CH * (a + 1)]

    reached = [sum(part(eb, pb - eb) for eb in range(4) if 0 <= pb - eb <= 2) for pb in range(6)]
    above, mine, below = (jnp.concatenate(reached[2 * k : 2 * k + 2], axis=1) for k in range(3))
    own_ref[...] = grad_rows_ref[...] + mine
    whole = sums_of[0] + sums_of[1] + sums_of[2] + sums_of[3]
    col_sums = jnp.concatenate(
        [whole - (1.0 - top) * sums_of[1], whole, whole - (1.0 - bottom) * sums_of[2]], axis=0
    )
    high = col_sums.astype(BF16)
    rest = (col_sums - high.astype(F32)).astype(BF16)
    k1c = k1c_ref[...]
    spread_col = dot(k1c, high, TN) + dot(k1c, rest, TN)
    nothing = jnp.zeros((CH, LANES), F32)
    total = jnp.concatenate([nothing, grad_cols_ref[...], nothing], axis=1)
    for tap in range(3):
        piece = spread_col[CH * tap : CH * (tap + 1)]
        edge = piece[:, cols:]
        for width in (16, 32, 64):
            edge = edge + pltpu.roll(edge, width, 1)
        low = jnp.where(edge_lane >= LANES - 8, pltpu.roll(edge, LANES - 8, 1), 0.0)
        high_edge = jnp.where(edge_lane < 8, pltpu.roll(edge, LANES - 8, 1), 0.0)
        piece = jnp.concatenate([low, piece[:, :cols], high_edge], axis=1)
        total = total + (pltpu.roll(piece, (8 * (tap - 1)) % (cols + 2 * LANES), 1) if tap != 1 else piece)
    one_row = dot_split(row_sums, row_cat, TN)
    one_col = dot(high, col_cat, NT) + dot(rest, col_cat, NT)
    gap = jnp.zeros((32, cols + LANES), F32)
    bias_row = dot_exact(jnp.ones((8, cols + LANES), F32), jnp.concatenate([gap, whole, gap], axis=0), NT)
    for a in range(3):
        for b in range(3):
            one = one_row[CH * b : CH * (b + 1), CH * a : CH * (a + 1)]
            one = one + one_col[CH * a : CH * (a + 1), CH * b : CH * (b + 1)]
            two = [
                full[CH * (2 * b + gb) : CH * (2 * b + gb + 1), CH * (a + gb) : CH * (a + gb + 1)] for gb in range(2)
            ]
            w_scr[CH * (3 * a + b) : CH * (3 * a + b + 1), :] = jnp.concatenate([one, two[0] + two[1]], axis=1)

    weights, chans, sums_end = chunk_rows(n_row)
    tail = total[:, :LANES] + total[:, cols + LANES :] + bias_row[:1, :]
    before = lax.axis_index("row") - 1
    for j in range(n_row):
        chunk_scr[j, :weights, :] = w_scr[weights * j : weights * (j + 1), :]
        share = slice(chans * j, chans * (j + 1))
        chunk_scr[j, weights : weights + chans, :] = total[share, LANES : 2 * LANES]
        chunk_scr[j, weights + chans : weights + 2 * chans, :] = total[share, cols : cols + LANES]
        chunk_scr[j, weights + 2 * chans : sums_end, :] = tail[share]
        chunk_scr[j, sums_end:, :] = jnp.where(before == j, above, below)
    out_ref[...] = chunk_scr[...].astype(BF16)


def row_sum_kernel(n_row, n_col, got_ref, own_ref, out_ref):
    sums_end = chunk_rows(n_row)[2]
    me = lax.axis_index("row")
    total = got_ref[0].astype(F32)
    for j in range(1, n_row):
        total = total + got_ref[j].astype(F32)
    total = total[:sums_end]
    before = got_ref[jnp.maximum(me - 1, 0)].astype(F32)[sums_end:]
    after = got_ref[jnp.minimum(me + 1, n_row - 1)].astype(F32)[sums_end:]
    rows = own_ref[...] + off_edge("row", 0) * before + off_edge("row", n_row - 1) * after
    whole = jnp.concatenate([total, rows], axis=0).astype(BF16)
    for k in range(n_col):
        out_ref[k] = whole


def col_sum_kernel(n_row, n_col, cols, got_ref, row_ref, bias_ref, out_ref, scr):
    weights, chans, sums_end = chunk_rows(n_row)
    me = lax.axis_index("col")
    whole = math.sqrt(16 * n_row * cols * n_col)
    total = got_ref[0].astype(F32)
    for k in range(1, n_col):
        total = total + got_ref[k].astype(F32)
    rows = total[sums_end:, :] * (1.0 / math.sqrt(cols * n_col))
    row_ref[0:8, :] = rows[:, :CH]
    row_ref[8:16, :] = rows[:, CH:]
    bias_ref[...] = total[sums_end - 1 : sums_end, 32 : 32 + CH] * (1.0 / whole)
    before = got_ref[jnp.maximum(me - 1, 0)].astype(F32) * off_edge("col", 0)
    after = got_ref[jnp.minimum(me + 1, n_col - 1)].astype(F32) * off_edge("col", n_col - 1)
    mine = got_ref[me].astype(F32)
    edge = slice(weights + 2 * chans, sums_end)
    lane = lax.broadcasted_iota(jnp.int32, (chans, LANES), 1)
    low = mine[weights : weights + chans] + jnp.where(lane < 16, before[edge], 0.0)
    high = mine[weights + chans : weights + 2 * chans] + jnp.where(lane >= LANES - 16, after[edge], 0.0)
    scale = 1.0 / math.sqrt(16 * n_row)
    scr[...] = jnp.zeros(scr.shape, F32)
    scr[:weights, :] = total[:weights] * (1.0 / whole)
    scr[weights : weights + chans, :] = low * scale
    scr[weights + chans : weights + 2 * chans, :] = high * scale
    share = scr[...].astype(BF16)
    for j in range(n_row):
        out_ref[j] = share


def spread_kernel(n_row, got_ref, col_ref, one_ref, two_ref):
    weights, chans, _ = chunk_rows(n_row)
    for j in range(n_row):
        chunk = got_ref[j].astype(F32)
        one_ref[weights * j : weights * (j + 1), :] = chunk[:weights, :CH]
        two_ref[weights * j : weights * (j + 1), :] = chunk[:weights, CH:]
        col_ref[chans * j : chans * (j + 1), :LANES] = chunk[weights : weights + chans]
        col_ref[chans * j : chans * (j + 1), LANES:] = chunk[weights + chans : weights + 2 * chans]


PARAMS = pltpu.CompilerParams(vmem_limit_bytes=48 * 1024 * 1024)


def sds(shape, dtype=F32):
    return jax.ShapeDtypeStruct(shape, dtype)


def shards(n_row, n_col, grad_out, row_feat, col_feat, conv_one, bias_one, conv_two):
    cols = grad_out.shape[2]
    weights, chans, sums_end = chunk_rows(n_row)
    places = 8 * cols + LANES
    grad_out, row_feat, col_turned, conv_one, conv_two, bias_row = (
        pltpu.with_memory_space_constraint(x, pltpu.HBM)
        for x in (grad_out, row_feat, col_feat.T, conv_one, conv_two, bias_one.reshape(1, CH))
    )
    strip = pl.pallas_call(
        pack_kernel,
        out_shape=sds((16 + CH, LANES), BF16),
        in_specs=[pl.BlockSpec(memory_space=pltpu.HBM)] * 2,
        scratch_shapes=[
            pltpu.VMEM((16, CH), BF16),
            pltpu.VMEM((CH, cols), BF16),
            pltpu.SemaphoreType.DMA,
            pltpu.SemaphoreType.DMA,
        ],
        compiler_params=PARAMS,
    )(row_feat, col_turned)
    both = [(r * n_col + c, (r ^ 1) * n_col + (c ^ 1)) for r in range(n_row) for c in range(n_col)]

    def other(index, count):
        return min(max(index + (1 if index % 2 else -1), 0), count - 1)

    rest = [
        (r * n_col + c, other(r, n_row) * n_col + other(c, n_col)) for r in range(n_row) for c in range(n_col)
    ]
    twin = lax.ppermute(strip, ("row", "col"), both)
    far = lax.ppermute(strip, ("row", "col"), rest)

    held = pl.pallas_call(
        lambda *refs: own_kernel(n_col, *refs),
        out_shape=(
            sds((3, 2 * CH, places), BF16), sds((4 * CH, places)), sds((8, 2 * CH)), sds((CH, cols)),
            sds((24, places), BF16), sds((3 * CH, 3 * CH), BF16), sds((3 * CH, 3 * CH), BF16), sds((CH, 8)),
            sds((16, CH), BF16), sds((CH, cols), BF16),
        ),
        in_specs=[pl.BlockSpec(memory_space=pltpu.HBM)] * 6,
        scratch_shapes=[
            pltpu.VMEM((cols // LANES, CH * 16, LANES), F32),
            pltpu.VMEM(grad_out.shape, BF16),
            pltpu.VMEM(conv_one.shape, BF16),
            pltpu.VMEM(conv_two.shape, BF16),
            pltpu.VMEM((1, CH), F32),
            pltpu.SemaphoreType.DMA((6,)),
        ],
        compiler_params=PARAMS,
    )(grad_out, conv_one, conv_two, bias_row, row_feat, col_turned)
    chunks, own = pl.pallas_call(
        lambda *refs: main_kernel(n_row, n_col, *refs),
        out_shape=(sds((n_row, sums_end + 8, LANES), BF16), sds((8, LANES))),
        scratch_shapes=[
            pltpu.VMEM((4 * CH, places), F32),
            pltpu.VMEM((4 * CH, places), BF16),
            pltpu.VMEM((4 * CH, places), BF16),
            pltpu.VMEM((9 * CH, LANES), F32),
            pltpu.VMEM((n_row, sums_end + 8, LANES), F32),
        ],
        compiler_params=PARAMS,
    )(twin, far, *held)
    got = lax.all_to_all(chunks, "row", 0, 0)
    copies = pl.pallas_call(
        lambda *refs: row_sum_kernel(n_row, n_col, *refs),
        out_shape=sds((n_col, sums_end + 8, LANES), BF16),
        compiler_params=PARAMS,
    )(got, own)
    got = lax.all_to_all(copies, "col", 0, 0)
    end = -(-(weights + 2 * chans) // 16) * 16
    row_grad, bias_grad, copies = pl.pallas_call(
        lambda *refs: col_sum_kernel(n_row, n_col, cols, *refs),
        out_shape=(sds((16, CH)), sds((1, CH)), sds((n_row, end, LANES), BF16)),
        scratch_shapes=[pltpu.VMEM((end, LANES), F32)],
        compiler_params=PARAMS,
    )(got)
    got = lax.all_to_all(copies, "row", 0, 0)
    col_grad, one, two = pl.pallas_call(
        lambda *refs: spread_kernel(n_row, *refs),
        out_shape=(sds((CH, cols)), sds((9 * CH, CH)), sds((9 * CH, CH))),
        compiler_params=PARAMS,
    )(got)
    shape = conv_one.shape
    return row_grad, col_grad.T, one.reshape(shape), bias_grad[0], two.reshape(shape)


def solution(mesh):
    in_specs = (P(None, "row", "col"), P("row", None), P("col", None), P(), P(), P())
    out_specs = (P("row", None), P("col", None), P(), P(), P())
    n_row, n_col = mesh.shape["row"], mesh.shape["col"]
    return jax.shard_map(
        lambda *args: shards(n_row, n_col, *args), mesh=mesh, in_specs=in_specs, out_specs=out_specs, check_vma=False
    )
```

```python
import math

import jax
import jax.numpy as jnp
from jax import lax
from jax.experimental import pallas as pl
from jax.experimental.pallas import tpu as pltpu
from jax.sharding import PartitionSpec as P

F32, BF16 = jnp.float32, jnp.bfloat16
NN = (((1,), (0,)), ((), ()))
NT = (((1,), (1,)), ((), ()))
TN = (((0,), (0,)), ((), ()))
CH = 64
LANES = 128


def dot(x, y, dims):
    return lax.dot_general(x, y, dims, preferred_element_type=F32)


def chunk_rows(n_row):
    weights, chans = 9 * CH // n_row, CH // n_row
    return weights, chans, weights + 3 * chans


def dot_split(x, y, dims):
    high = x.astype(BF16)
    low = (x - high.astype(F32)).astype(BF16)
    y = y.astype(BF16)
    return dot(high, y, dims) + dot(low, y, dims)


def pack_kernel(row_hbm, col_hbm, out_ref, row_ref, col_ref, row_sem, col_sem):
    row_copy = pltpu.make_async_copy(row_hbm, row_ref, row_sem)
    col_copy = pltpu.make_async_copy(col_hbm, col_ref, col_sem)
    row_copy.start()
    col_copy.start()
    row_copy.wait()
    col_copy.wait()
    rows = row_ref[...].astype(F32)
    out_ref[:16, :] = jnp.concatenate([rows, jnp.zeros_like(rows)], axis=1).astype(BF16)
    cols = col_ref.shape[1]
    lane = lax.broadcasted_iota(jnp.int32, (CH, LANES), 1)
    first, last = col_ref[:, :LANES].astype(F32), col_ref[:, cols - LANES :].astype(F32)
    out_ref[16:, :] = jnp.where(lane < LANES // 2, first, last).astype(BF16)


def off_edge(axis, index):
    return jnp.where(lax.axis_index(axis) == index, 0.0, 1.0).astype(F32)


def indicator(cols, n_col):
    lane = lax.broadcasted_iota(jnp.int32, (8, cols), 1)
    row = lax.broadcasted_iota(jnp.int32, (8, cols), 0)
    me = lax.axis_index("col")
    off_map = ((lane < 8) & (me == 0), lane < 0, (lane >= cols - 8) & (me == n_col - 1))
    edge_lane = lax.broadcasted_iota(jnp.int32, (8, LANES), 1)
    edge_row = lax.broadcasted_iota(jnp.int32, (8, LANES), 0)
    edge = jnp.where(edge_lane // 16 == edge_row, 1.0, 0.0)
    taps = []
    for tap in range(3):
        on_map = jnp.logical_not(off_map[tap])
        main = [jnp.where(on_map & (row == k), 1.0, 0.0) for k in range(8)]
        taps.append(jnp.concatenate(main + [edge], axis=1))
    return jnp.concatenate(taps, axis=0).astype(BF16)


def own_kernel(
    n_col, grad_hbm, one_hbm, two_hbm, bias_hbm, row_hbm, col_hbm,
    x_ref, back_ref, grad_rows_ref, grad_cols_ref, ind_ref, k1c_ref, k1f_ref, bias_col_ref, row_ref, col_ref,
    rows_scr, grad_ref, one_ref, two_ref, bias_ref, sems,
):
    cols = grad_ref.shape[2]
    pairs = (
        (one_hbm, one_ref), (two_hbm, two_ref), (bias_hbm, bias_ref), (row_hbm, row_ref), (col_hbm, col_ref),
        (grad_hbm, grad_ref),
    )
    copies = [pltpu.make_async_copy(source, target, sems.at[k]) for k, (source, target) in enumerate(pairs)]
    for copy in copies:
        copy.start()
    hits = indicator(cols, n_col)
    ind_ref[...] = hits
    for copy in copies[:-1]:
        copy.wait()
    one = [[one_ref[a, b].astype(F32) for b in range(3)] for a in range(3)]
    for k in range(3):
        rows = slice(CH * k, CH * (k + 1))
        k1c_ref[rows, :] = jnp.concatenate(one[k], axis=1).astype(BF16)
        k1f_ref[rows, :] = jnp.concatenate([one[a][k] for a in range(3)], axis=1).astype(BF16)
    nil = jnp.zeros((CH, CH), F32)
    two = [[two_ref[a, b].astype(F32) for b in range(3)] for a in range(3)]
    w2 = jnp.concatenate(
        [
            jnp.concatenate([two[eb - gb][b] if 0 <= eb - gb <= 2 else nil for eb in range(4)], axis=1)
            for b in range(3)
            for gb in range(2)
        ],
        axis=0,
    ).astype(BF16)
    bias = jnp.concatenate([bias_ref[...], jnp.zeros((1, LANES - CH), F32)], axis=1)
    bias_col_ref[...] = jnp.broadcast_to(bias, (8, LANES)).T[:CH, :]
    copies[-1].wait()
    lane = lax.broadcasted_iota(jnp.int32, (CH, cols), 1)
    edge_lane = lax.broadcasted_iota(jnp.int32, (CH, LANES), 1)
    for piece in range(cols // LANES):
        wide = grad_ref[:, :, LANES * piece : LANES * (piece + 1)]
        rows_scr[piece] = wide.astype(F32).reshape(CH * 16, LANES)
    col_sum = jnp.zeros((CH, cols), F32)
    for half in range(2):
        rows = slice(half * CH, (half + 1) * CH)
        left = right = jnp.zeros((CH, LANES), F32)
        for k in range(8):
            pieces = [rows_scr[p, pl.ds(half * 8 + k, CH, stride=16), :] for p in range(cols // LANES)]
            line = jnp.concatenate(pieces, axis=1)
            col_sum = col_sum + line
            span = slice(k * cols, (k + 1) * cols)
            x_ref[1, rows, span] = line.astype(BF16)
            x_ref[0, rows, span] = jnp.where(lane < cols - 8, pltpu.roll(line, cols - 8, 1), 0.0).astype(BF16)
            x_ref[2, rows, span] = jnp.where(lane >= 8, pltpu.roll(line, 8, 1), 0.0).astype(BF16)
            first = pltpu.roll(pieces[0], 16 * k, 1) if k else pieces[0]
            last = pltpu.roll(pieces[-1], 16 * k + 16, 1) if k < 7 else pieces[-1]
            here = edge_lane // 16 == k
            left = jnp.where(here & (edge_lane % 16 < 8), first, left)
            right = jnp.where(here & (edge_lane % 16 >= 8), last, right)
        x_ref[0, rows, 8 * cols :] = left.astype(BF16)
        x_ref[1, rows, 8 * cols :] = jnp.zeros((CH, LANES), BF16)
        x_ref[2, rows, 8 * cols :] = right.astype(BF16)
    grad_cols_ref[...] = col_sum
    row = lax.broadcasted_iota(jnp.int32, (8, 8 * cols), 0)
    span = lax.broadcasted_iota(jnp.int32, (8, 8 * cols), 1) // cols
    grad_rows_ref[...] = dot(jnp.where(row == span, 1.0, 0.0).astype(BF16), x_ref[1, :, : 8 * cols], NT)
    x_all = x_ref[...].reshape(6 * CH, x_ref.shape[2])
    back_ref[...] = dot(w2, x_all, TN)


def main_kernel(
    n_row, n_col, row_twin_ref, col_twin_ref,
    x_ref, back_ref, grad_rows_ref, grad_cols_ref, ind_ref, k1c_ref, k1f_ref, bias_ref, row_ref, col_ref,
    out_ref, own_ref, act_scr, inner_scr, w_scr, chunk_scr,
):
    cols = col_ref.shape[1]
    top, bottom = off_edge("row", 0), off_edge("row", n_row - 1)
    left, right = off_edge("col", 0), off_edge("col", n_col - 1)
    edge_lane = lax.broadcasted_iota(jnp.int32, (CH, LANES), 1)
    odd_row, odd_col = lax.axis_index("row") % 2 == 1, lax.axis_index("col") % 2 == 1
    twin, other = row_twin_ref[:16, :CH].astype(F32), col_twin_ref[:16, :CH].astype(F32) * (top * bottom)
    row_ext = jnp.concatenate(
        [jnp.where(odd_row, twin, other), row_ref[...].astype(F32), jnp.where(odd_row, other, twin)], axis=0
    )
    row_cat = jnp.concatenate([row_ext[8 * a : 8 * a + 32] for a in range(3)], axis=1).astype(BF16)
    twin, other = col_twin_ref[16:, :].astype(F32), row_twin_ref[16:, :].astype(F32) * (left * right)
    col_ext = jnp.concatenate(
        [jnp.where(odd_col, twin, other), col_ref[...].astype(F32), jnp.where(odd_col, other, twin)], axis=1
    )
    taps = []
    for tap in range(3):
        moved = pltpu.roll(col_ext, (8 * (1 - tap)) % (cols + 2 * LANES), 1) if tap != 1 else col_ext
        low, high = pltpu.roll(moved[:, :LANES], 8, 1), pltpu.roll(moved[:, LANES + cols :], 8, 1)
        edge = jnp.where(edge_lane < 8, low, jnp.where(edge_lane < 16, high, 0.0))
        for width in (16, 32, 64):
            edge = edge + pltpu.roll(edge, width, 1)
        taps.append(jnp.concatenate([moved[:, LANES : LANES + cols], edge], axis=1))
    col_cat = jnp.concatenate(taps, axis=0).astype(BF16)
    terms = dot(k1c_ref[...], col_cat, NN)
    low, mid, high = (terms[CH * a : CH * (a + 1)] for a in range(3))
    mid = mid + bias_ref[:, :1]
    col_part = [low + mid + high, top * low + mid + high, low + mid + bottom * high, low + mid + high]
    row_terms = dot(k1f_ref[...], row_cat, NT)
    by_tap = [row_terms[CH * b : CH * (b + 1)] for b in range(3)]
    row_part = by_tap[0] + by_tap[1] + by_tap[2]

    def spread_over(terms, k):
        return jnp.concatenate(
            [jnp.broadcast_to(terms[:, 8 * eb + k : 8 * eb + k + 1], (CH, LANES)) for eb in range(4)], axis=0
        )

    side_lane = lax.broadcasted_iota(jnp.int32, (4 * CH, LANES), 1)
    first_off = jnp.where(side_lane < 8, left - 1.0, 0.0)
    last_off = jnp.where(side_lane >= LANES - 8, right - 1.0, 0.0)
    edge_part = jnp.zeros((4 * CH, LANES), F32)
    on_map = jnp.where(side_lane % 16 < 8, left, right)
    col_part = jnp.concatenate(col_part, axis=0)
    main_sum = jnp.zeros((4 * CH, cols), F32)
    for k in range(9):
        span = slice(k * cols, (k + 1) * cols) if k < 8 else slice(8 * cols, 8 * cols + LANES)
        if k < 8:
            each = spread_over(row_part, k)
            edge_part = jnp.where(side_lane // 16 == k, each, edge_part)
            pieces = [each] * (cols // LANES)
            pieces[0] = pieces[0] + first_off * spread_over(by_tap[0], k)
            pieces[-1] = pieces[-1] + last_off * spread_over(by_tap[2], k)
            pre = jnp.concatenate(pieces, axis=1) + col_part[:, :cols]
        else:
            pre = edge_part + col_part[:, cols:]
        sig = 1.0 / (1.0 + jnp.exp(-pre))
        held = jnp.concatenate([sig[:CH] * top, sig[CH : 3 * CH], sig[3 * CH :] * bottom], axis=0)
        if k == 8:
            held = held * on_map
        act_scr[:, span] = (pre * held).astype(BF16)
        inner = (back_ref[:, span] * (held * (1.0 + pre * (1.0 - sig)))).astype(BF16)
        inner_scr[:, span] = inner
        if k < 8:
            main_sum = main_sum + inner.astype(F32)
    sums = jnp.concatenate([main_sum, inner.astype(F32)], axis=1)
    sums_of = [sums[CH * eb : CH * (eb + 1)] for eb in range(4)]

    full = dot(x_ref[...].reshape(6 * CH, x_ref.shape[2]), act_scr[...], NT)
    sums = dot(ind_ref[...], inner_scr[...], NT)
    row_sums = jnp.concatenate(
        [
            jnp.concatenate([sums[8 * b : 8 * b + 8, CH * eb : CH * (eb + 1)] for b in range(3)], axis=1)
            for eb in range(4)
        ],
        axis=0,
    )
    spread_row = dot_split(row_sums, k1f_ref[...], NN)

    def part(eb, a):
        return spread_row[8 * eb : 8 * eb + 8, CH * a : CH * (a + 1)]

    reached = [sum(part(eb, pb - eb) for eb in range(4) if 0 <= pb - eb <= 2) for pb in range(6)]
    above, mine, below = (jnp.concatenate(reached[2 * k : 2 * k + 2], axis=1) for k in range(3))
    own_ref[...] = grad_rows_ref[...] + mine
    whole = sums_of[0] + sums_of[1] + sums_of[2] + sums_of[3]
    col_sums = jnp.concatenate(
        [whole - (1.0 - top) * sums_of[1], whole, whole - (1.0 - bottom) * sums_of[2]], axis=0
    )
    high = col_sums.astype(BF16)
    rest = (col_sums - high.astype(F32)).astype(BF16)
    k1c = k1c_ref[...]
    spread_col = dot(k1c, high, TN) + dot(k1c, rest, TN)
    nothing = jnp.zeros((CH, LANES), F32)
    total = jnp.concatenate([nothing, grad_cols_ref[...], nothing], axis=1)
    for tap in range(3):
        piece = spread_col[CH * tap : CH * (tap + 1)]
        edge = piece[:, cols:]
        for width in (16, 32, 64):
            edge = edge + pltpu.roll(edge, width, 1)
        low = jnp.where(edge_lane >= LANES - 8, pltpu.roll(edge, LANES - 8, 1), 0.0)
        high_edge = jnp.where(edge_lane < 8, pltpu.roll(edge, LANES - 8, 1), 0.0)
        piece = jnp.concatenate([low, piece[:, :cols], high_edge], axis=1)
        total = total + (pltpu.roll(piece, (8 * (tap - 1)) % (cols + 2 * LANES), 1) if tap != 1 else piece)
    one_row = dot_split(row_sums, row_cat, TN)
    one_col = dot(high, col_cat, NT) + dot(rest, col_cat, NT)
    bias_row = jnp.sum(row_sums[:, :LANES], axis=0, keepdims=True)
    bias_row = pltpu.roll(jnp.where(lax.broadcasted_iota(jnp.int32, (8, LANES), 1) >= CH, bias_row, 0.0), 96, 1)
    for a in range(3):
        for b in range(3):
            one = one_row[CH * b : CH * (b + 1), CH * a : CH * (a + 1)]
            one = one + one_col[CH * a : CH * (a + 1), CH * b : CH * (b + 1)]
            two = [
                full[CH * (2 * b + gb) : CH * (2 * b + gb + 1), CH * (a + gb) : CH * (a + gb + 1)] for gb in range(2)
            ]
            w_scr[CH * (3 * a + b) : CH * (3 * a + b + 1), :] = jnp.concatenate([one, two[0] + two[1]], axis=1)

    weights, chans, sums_end = chunk_rows(n_row)
    tail = total[:, :LANES] + total[:, cols + LANES :] + bias_row[:1, :]
    before = lax.axis_index("row") - 1
    for j in range(n_row):
        chunk_scr[j, :weights, :] = w_scr[weights * j : weights * (j + 1), :]
        share = slice(chans * j, chans * (j + 1))
        chunk_scr[j, weights : weights + chans, :] = total[share, LANES : 2 * LANES]
        chunk_scr[j, weights + chans : weights + 2 * chans, :] = total[share, cols : cols + LANES]
        chunk_scr[j, weights + 2 * chans : sums_end, :] = tail[share]
        chunk_scr[j, sums_end:, :] = jnp.where(before == j, above, below)
    out_ref[...] = chunk_scr[...].astype(BF16)


def row_sum_kernel(n_row, n_col, got_ref, own_ref, out_ref):
    sums_end = chunk_rows(n_row)[2]
    me = lax.axis_index("row")
    total = got_ref[0].astype(F32)
    for j in range(1, n_row):
        total = total + got_ref[j].astype(F32)
    total = total[:sums_end]
    before = got_ref[jnp.maximum(me - 1, 0)].astype(F32)[sums_end:]
    after = got_ref[jnp.minimum(me + 1, n_row - 1)].astype(F32)[sums_end:]
    rows = own_ref[...] + off_edge("row", 0) * before + off_edge("row", n_row - 1) * after
    whole = jnp.concatenate([total, rows], axis=0).astype(BF16)
    for k in range(n_col):
        out_ref[k] = whole


def col_sum_kernel(n_row, n_col, cols, got_ref, row_ref, bias_ref, out_ref, scr):
    weights, chans, sums_end = chunk_rows(n_row)
    me = lax.axis_index("col")
    whole = math.sqrt(16 * n_row * cols * n_col)
    total = got_ref[0].astype(F32)
    for k in range(1, n_col):
        total = total + got_ref[k].astype(F32)
    rows = total[sums_end:, :] * (1.0 / math.sqrt(cols * n_col))
    row_ref[0:8, :] = rows[:, :CH]
    row_ref[8:16, :] = rows[:, CH:]
    bias_ref[...] = total[sums_end - 1 : sums_end, 32 : 32 + CH] * (1.0 / whole)
    before = got_ref[jnp.maximum(me - 1, 0)].astype(F32) * off_edge("col", 0)
    after = got_ref[jnp.minimum(me + 1, n_col - 1)].astype(F32) * off_edge("col", n_col - 1)
    mine = got_ref[me].astype(F32)
    edge = slice(weights + 2 * chans, sums_end)
    lane = lax.broadcasted_iota(jnp.int32, (chans, LANES), 1)
    low = mine[weights : weights + chans] + jnp.where(lane < 16, before[edge], 0.0)
    high = mine[weights + chans : weights + 2 * chans] + jnp.where(lane >= LANES - 16, after[edge], 0.0)
    scale = 1.0 / math.sqrt(16 * n_row)
    scr[...] = jnp.zeros(scr.shape, F32)
    scr[:weights, :] = total[:weights] * (1.0 / whole)
    scr[weights : weights + chans, :] = low * scale
    scr[weights + chans : weights + 2 * chans, :] = high * scale
    share = scr[...].astype(BF16)
    for j in range(n_row):
        out_ref[j] = share


def spread_kernel(n_row, got_ref, col_ref, one_ref, two_ref):
    weights, chans, _ = chunk_rows(n_row)
    for j in range(n_row):
        chunk = got_ref[j].astype(F32)
        one_ref[weights * j : weights * (j + 1), :] = chunk[:weights, :CH]
        two_ref[weights * j : weights * (j + 1), :] = chunk[:weights, CH:]
        col_ref[chans * j : chans * (j + 1), :LANES] = chunk[weights : weights + chans]
        col_ref[chans * j : chans * (j + 1), LANES:] = chunk[weights + chans : weights + 2 * chans]


PARAMS = pltpu.CompilerParams(vmem_limit_bytes=48 * 1024 * 1024)


def sds(shape, dtype=F32):
    return jax.ShapeDtypeStruct(shape, dtype)


def shards(n_row, n_col, grad_out, row_feat, col_feat, conv_one, bias_one, conv_two):
    cols = grad_out.shape[2]
    weights, chans, sums_end = chunk_rows(n_row)
    places = 8 * cols + LANES
    grad_out, row_feat, col_turned, conv_one, conv_two, bias_row = (
        pltpu.with_memory_space_constraint(x, pltpu.HBM)
        for x in (grad_out, row_feat, col_feat.T, conv_one, conv_two, bias_one.reshape(1, CH))
    )
    strip = pl.pallas_call(
        pack_kernel,
        out_shape=sds((16 + CH, LANES), BF16),
        in_specs=[pl.BlockSpec(memory_space=pltpu.HBM)] * 2,
        scratch_shapes=[
            pltpu.VMEM((16, CH), BF16),
            pltpu.VMEM((CH, cols), BF16),
            pltpu.SemaphoreType.DMA,
            pltpu.SemaphoreType.DMA,
        ],
        compiler_params=PARAMS,
    )(row_feat, col_turned)

    def twin(index, count):
        return index ^ 1

    def other(index, count):
        return min(max(index + (1 if index % 2 else -1), 0), count - 1)

    def swap(along_row, along_col):
        pairs = [
            (r * n_col + c, along_row(r, n_row) * n_col + along_col(c, n_col))
            for r in range(n_row)
            for c in range(n_col)
        ]
        return lax.ppermute(strip, ("row", "col"), pairs)

    row_twin = swap(twin, other)
    col_twin = swap(other, twin)

    held = pl.pallas_call(
        lambda *refs: own_kernel(n_col, *refs),
        out_shape=(
            sds((3, 2 * CH, places), BF16), sds((4 * CH, places)), sds((8, 2 * CH)), sds((CH, cols)),
            sds((24, places), BF16), sds((3 * CH, 3 * CH), BF16), sds((3 * CH, 3 * CH), BF16), sds((CH, 8)),
            sds((16, CH), BF16), sds((CH, cols), BF16),
        ),
        in_specs=[pl.BlockSpec(memory_space=pltpu.HBM)] * 6,
        scratch_shapes=[
            pltpu.VMEM((cols // LANES, CH * 16, LANES), F32),
            pltpu.VMEM(grad_out.shape, BF16),
            pltpu.VMEM(conv_one.shape, BF16),
            pltpu.VMEM(conv_two.shape, BF16),
            pltpu.VMEM((1, CH), F32),
            pltpu.SemaphoreType.DMA((6,)),
        ],
        compiler_params=PARAMS,
    )(grad_out, conv_one, conv_two, bias_row, row_feat, col_turned)
    chunks, own = pl.pallas_call(
        lambda *refs: main_kernel(n_row, n_col, *refs),
        out_shape=(sds((n_row, sums_end + 8, LANES), BF16), sds((8, LANES))),
        scratch_shapes=[
            pltpu.VMEM((4 * CH, places), BF16),
            pltpu.VMEM((4 * CH, places), BF16),
            pltpu.VMEM((9 * CH, LANES), F32),
            pltpu.VMEM((n_row, sums_end + 8, LANES), F32),
        ],
        compiler_params=PARAMS,
    )(row_twin, col_twin, *held)
    got = lax.all_to_all(chunks, "row", 0, 0)
    copies = pl.pallas_call(
        lambda *refs: row_sum_kernel(n_row, n_col, *refs),
        out_shape=sds((n_col, sums_end + 8, LANES), BF16),
        compiler_params=PARAMS,
    )(got, own)
    got = lax.all_to_all(copies, "col", 0, 0)
    end = -(-(weights + 2 * chans) // 16) * 16
    row_grad, bias_grad, copies = pl.pallas_call(
        lambda *refs: col_sum_kernel(n_row, n_col, cols, *refs),
        out_shape=(sds((16, CH)), sds((1, CH)), sds((n_row, end, LANES), BF16)),
        scratch_shapes=[pltpu.VMEM((end, LANES), F32)],
        compiler_params=PARAMS,
    )(got)
    got = lax.all_to_all(copies, "row", 0, 0)
    col_grad, one, two = pl.pallas_call(
        lambda *refs: spread_kernel(n_row, *refs),
        out_shape=(sds((CH, cols)), sds((9 * CH, CH)), sds((9 * CH, CH))),
        compiler_params=PARAMS,
    )(got)
    shape = conv_one.shape
    return row_grad, col_grad.T, one.reshape(shape), bias_grad[0], two.reshape(shape)


def solution(mesh):
    in_specs = (P(None, "row", "col"), P("row", None), P("col", None), P(), P(), P())
    out_specs = (P("row", None), P("col", None), P(), P(), P())
    n_row, n_col = mesh.shape["row"], mesh.shape["col"]
    return jax.shard_map(
        lambda *args: shards(n_row, n_col, *args), mesh=mesh, in_specs=in_specs, out_specs=out_specs, check_vma=False
    )
```

```python
import math

import jax
import jax.numpy as jnp
from jax import lax
from jax.experimental import pallas as pl
from jax.experimental.pallas import tpu as pltpu
from jax.sharding import PartitionSpec as P

F32, BF16 = jnp.float32, jnp.bfloat16
NN = (((1,), (0,)), ((), ()))
NT = (((1,), (1,)), ((), ()))
TN = (((0,), (0,)), ((), ()))
CH = 64
LANES = 128
GRAD_COPIES = 1


def dot(x, y, dims):
    return lax.dot_general(x, y, dims, preferred_element_type=F32)


def chunk_rows(n_row):
    weights, chans = 9 * CH // n_row, CH // n_row
    return weights, chans, weights + 3 * chans


def dot_split(x, y, dims):
    high = x.astype(BF16)
    low = (x - high.astype(F32)).astype(BF16)
    y = y.astype(BF16)
    return dot(high, y, dims) + dot(low, y, dims)


def shares(n_row, j):
    weights = 9 * CH // n_row
    main = weights // 8 * 8
    pieces = [(slice(0, main), slice(main * j, main * (j + 1)))]
    if main < weights:
        rest = weights - main
        pieces.append((slice(main, weights), slice(main * n_row + rest * j, main * n_row + rest * (j + 1))))
    return pieces


def pack_kernel(
    n_col, row_hbm, col_hbm, one_hbm, two_hbm, bias_hbm, grad_hbm,
    out_ref, row_ref, col_ref, grad_ref, ind_ref, k1c_ref, k1f_ref, w2_ref, bias_col_ref,
    one_ref, two_ref, bias_ref, sems,
):
    pairs = [
        (row_hbm, row_ref), (col_hbm, col_ref), (one_hbm, one_ref), (two_hbm, two_ref), (bias_hbm, bias_ref),
    ]
    step = CH // GRAD_COPIES
    for k in range(GRAD_COPIES):
        part = slice(step * k, step * (k + 1))
        pairs.append((grad_hbm.at[part], grad_ref.at[part]))
    copies = [pltpu.make_async_copy(x, y, sems.at[k]) for k, (x, y) in enumerate(pairs)]
    for copy in copies:
        copy.start()
    for copy in copies[:2]:
        copy.wait()
    rows = row_ref[...].astype(F32)
    out_ref[:16, :] = jnp.concatenate([rows, jnp.zeros_like(rows)], axis=1).astype(BF16)
    cols = col_ref.shape[1]
    lane = lax.broadcasted_iota(jnp.int32, (CH, LANES), 1)
    first, last = col_ref[:, :LANES].astype(F32), col_ref[:, cols - LANES :].astype(F32)
    out_ref[16:, :] = jnp.where(lane < LANES // 2, first, last).astype(BF16)
    ind_ref[...] = indicator(cols, n_col)
    for copy in copies[2:5]:
        copy.wait()
    one = [[one_ref[a, b].astype(F32) for b in range(3)] for a in range(3)]
    for k in range(3):
        rows = slice(CH * k, CH * (k + 1))
        k1c_ref[rows, :] = jnp.concatenate(one[k], axis=1).astype(BF16)
        k1f_ref[rows, :] = jnp.concatenate([one[a][k] for a in range(3)], axis=1).astype(BF16)
    nil = jnp.zeros((CH, CH), F32)
    two = [[two_ref[a, b].astype(F32) for b in range(3)] for a in range(3)]
    for b in range(3):
        for gb in range(2):
            blocks = [two[eb - gb][b] if 0 <= eb - gb <= 2 else nil for eb in range(4)]
            at = CH * (2 * b + gb)
            w2_ref[at : at + CH, :] = jnp.concatenate(blocks, axis=1).astype(BF16)
    bias = jnp.concatenate([bias_ref[...], jnp.zeros((1, LANES - CH), F32)], axis=1)
    bias_col_ref[...] = jnp.broadcast_to(bias, (8, LANES)).T[:CH, :]
    for copy in copies[5:]:
        copy.wait()


def off_edge(axis, index):
    return jnp.where(lax.axis_index(axis) == index, 0.0, 1.0).astype(F32)


def indicator(cols, n_col):
    lane = lax.broadcasted_iota(jnp.int32, (8, cols), 1)
    row = lax.broadcasted_iota(jnp.int32, (8, cols), 0)
    me = lax.axis_index("col")
    off_map = ((lane < 8) & (me == 0), lane < 0, (lane >= cols - 8) & (me == n_col - 1))
    edge_lane = lax.broadcasted_iota(jnp.int32, (8, LANES), 1)
    edge_row = lax.broadcasted_iota(jnp.int32, (8, LANES), 0)
    edge = jnp.where(edge_lane // 16 == edge_row, 1.0, 0.0)
    taps = []
    for tap in range(3):
        on_map = jnp.logical_not(off_map[tap])
        main = [jnp.where(on_map & (row == k), 1.0, 0.0) for k in range(8)]
        taps.append(jnp.concatenate(main + [edge], axis=1))
    return jnp.concatenate(taps, axis=0).astype(BF16)


def own_kernel(grad_ref, w2_ref, x_ref, back_ref, grad_rows_ref, grad_cols_ref, rows_scr):
    cols = grad_ref.shape[2]
    lane = lax.broadcasted_iota(jnp.int32, (CH, cols), 1)
    edge_lane = lax.broadcasted_iota(jnp.int32, (CH, LANES), 1)
    for piece in range(cols // LANES):
        wide = grad_ref[:, :, LANES * piece : LANES * (piece + 1)]
        rows_scr[piece] = wide.astype(F32).reshape(CH * 16, LANES)
    col_sum = jnp.zeros((CH, cols), F32)
    for half in range(2):
        rows = slice(half * CH, (half + 1) * CH)
        left = right = jnp.zeros((CH, LANES), F32)
        for k in range(8):
            pieces = [rows_scr[p, pl.ds(half * 8 + k, CH, stride=16), :] for p in range(cols // LANES)]
            line = jnp.concatenate(pieces, axis=1)
            col_sum = col_sum + line
            span = slice(k * cols, (k + 1) * cols)
            x_ref[1, rows, span] = line.astype(BF16)
            x_ref[0, rows, span] = jnp.where(lane < cols - 8, pltpu.roll(line, cols - 8, 1), 0.0).astype(BF16)
            x_ref[2, rows, span] = jnp.where(lane >= 8, pltpu.roll(line, 8, 1), 0.0).astype(BF16)
            first = pltpu.roll(pieces[0], 16 * k, 1) if k else pieces[0]
            last = pltpu.roll(pieces[-1], 16 * k + 16, 1) if k < 7 else pieces[-1]
            here = edge_lane // 16 == k
            left = jnp.where(here & (edge_lane % 16 < 8), first, left)
            right = jnp.where(here & (edge_lane % 16 >= 8), last, right)
        x_ref[0, rows, 8 * cols :] = left.astype(BF16)
        x_ref[1, rows, 8 * cols :] = jnp.zeros((CH, LANES), BF16)
        x_ref[2, rows, 8 * cols :] = right.astype(BF16)
    grad_cols_ref[...] = col_sum
    row = lax.broadcasted_iota(jnp.int32, (8, 8 * cols), 0)
    span = lax.broadcasted_iota(jnp.int32, (8, 8 * cols), 1) // cols
    grad_rows_ref[...] = dot(jnp.where(row == span, 1.0, 0.0).astype(BF16), x_ref[1, :, : 8 * cols], NT)
    x_all = x_ref[...].reshape(6 * CH, x_ref.shape[2])
    back_ref[...] = dot(w2_ref[...], x_all, TN)


def main_kernel(
    n_row, n_col, row_twin_ref, col_twin_ref, row_ref, col_ref,
    x_ref, back_ref, grad_rows_ref, grad_cols_ref, ind_ref, k1c_ref, k1f_ref, bias_ref,
    out_ref, own_ref, act_scr, inner_scr, w_scr, chunk_scr,
):
    cols = col_ref.shape[1]
    top, bottom = off_edge("row", 0), off_edge("row", n_row - 1)
    left, right = off_edge("col", 0), off_edge("col", n_col - 1)
    edge_lane = lax.broadcasted_iota(jnp.int32, (CH, LANES), 1)
    odd_row, odd_col = lax.axis_index("row") % 2 == 1, lax.axis_index("col") % 2 == 1
    twin, other = row_twin_ref[:16, :CH].astype(F32), col_twin_ref[:16, :CH].astype(F32) * (top * bottom)
    row_ext = jnp.concatenate(
        [jnp.where(odd_row, twin, other), row_ref[...].astype(F32), jnp.where(odd_row, other, twin)], axis=0
    )
    row_cat = jnp.concatenate([row_ext[8 * a : 8 * a + 32] for a in range(3)], axis=1).astype(BF16)
    twin, other = col_twin_ref[16:, :].astype(F32), row_twin_ref[16:, :].astype(F32) * (left * right)
    col_ext = jnp.concatenate(
        [jnp.where(odd_col, twin, other), col_ref[...].astype(F32), jnp.where(odd_col, other, twin)], axis=1
    )
    taps = []
    for tap in range(3):
        moved = pltpu.roll(col_ext, (8 * (1 - tap)) % (cols + 2 * LANES), 1) if tap != 1 else col_ext
        low, high = pltpu.roll(moved[:, :LANES], 8, 1), pltpu.roll(moved[:, LANES + cols :], 8, 1)
        edge = jnp.where(edge_lane < 8, low, jnp.where(edge_lane < 16, high, 0.0))
        for width in (16, 32, 64):
            edge = edge + pltpu.roll(edge, width, 1)
        taps.append(jnp.concatenate([moved[:, LANES : LANES + cols], edge], axis=1))
    col_cat = jnp.concatenate(taps, axis=0).astype(BF16)
    terms = dot(k1c_ref[...], col_cat, NN)
    low, mid, high = (terms[CH * a : CH * (a + 1)] for a in range(3))
    mid = mid + bias_ref[:, :1]
    col_part = [low + mid + high, top * low + mid + high, low + mid + bottom * high, low + mid + high]
    row_terms = dot(k1f_ref[...], row_cat, NT)
    by_tap = [row_terms[CH * b : CH * (b + 1)] for b in range(3)]
    row_part = by_tap[0] + by_tap[1] + by_tap[2]

    def spread_over(terms, k):
        return jnp.concatenate(
            [jnp.broadcast_to(terms[:, 8 * eb + k : 8 * eb + k + 1], (CH, LANES)) for eb in range(4)], axis=0
        )

    side_lane = lax.broadcasted_iota(jnp.int32, (4 * CH, LANES), 1)
    first_off = jnp.where(side_lane < 8, left - 1.0, 0.0)
    last_off = jnp.where(side_lane >= LANES - 8, right - 1.0, 0.0)
    edge_part = jnp.zeros((4 * CH, LANES), F32)
    on_map = jnp.where(side_lane % 16 < 8, left, right)
    col_part = jnp.concatenate(col_part, axis=0)
    main_sum = jnp.zeros((4 * CH, cols), F32)
    for k in range(9):
        span = slice(k * cols, (k + 1) * cols) if k < 8 else slice(8 * cols, 8 * cols + LANES)
        if k < 8:
            each = spread_over(row_part, k)
            edge_part = jnp.where(side_lane // 16 == k, each, edge_part)
            pieces = [each] * (cols // LANES)
            pieces[0] = pieces[0] + first_off * spread_over(by_tap[0], k)
            pieces[-1] = pieces[-1] + last_off * spread_over(by_tap[2], k)
            pre = jnp.concatenate(pieces, axis=1) + col_part[:, :cols]
        else:
            pre = edge_part + col_part[:, cols:]
        sig = 1.0 / (1.0 + jnp.exp(-pre))
        held = jnp.concatenate([sig[:CH] * top, sig[CH : 3 * CH], sig[3 * CH :] * bottom], axis=0)
        if k == 8:
            held = held * on_map
        act_scr[:, span] = (pre * held).astype(BF16)
        inner = (back_ref[:, span] * (held * (1.0 + pre * (1.0 - sig)))).astype(BF16)
        inner_scr[:, span] = inner
        if k < 8:
            main_sum = main_sum + inner.astype(F32)
    sums = jnp.concatenate([main_sum, inner.astype(F32)], axis=1)
    sums_of = [sums[CH * eb : CH * (eb + 1)] for eb in range(4)]

    full = dot(x_ref[...].reshape(6 * CH, x_ref.shape[2]), act_scr[...], NT)
    sums = dot(ind_ref[...], inner_scr[...], NT)
    row_sums = jnp.concatenate(
        [
            jnp.concatenate([sums[8 * b : 8 * b + 8, CH * eb : CH * (eb + 1)] for b in range(3)], axis=1)
            for eb in range(4)
        ],
        axis=0,
    )
    spread_row = dot_split(row_sums, k1f_ref[...], NN)

    def part(eb, a):
        return spread_row[8 * eb : 8 * eb + 8, CH * a : CH * (a + 1)]

    reached = [sum(part(eb, pb - eb) for eb in range(4) if 0 <= pb - eb <= 2) for pb in range(6)]
    above, mine, below = (jnp.concatenate(reached[2 * k : 2 * k + 2], axis=1) for k in range(3))
    own_ref[...] = grad_rows_ref[...] + mine
    whole = sums_of[0] + sums_of[1] + sums_of[2] + sums_of[3]
    col_sums = jnp.concatenate(
        [whole - (1.0 - top) * sums_of[1], whole, whole - (1.0 - bottom) * sums_of[2]], axis=0
    )
    high = col_sums.astype(BF16)
    rest = (col_sums - high.astype(F32)).astype(BF16)
    k1c = k1c_ref[...]
    spread_col = dot(k1c, high, TN) + dot(k1c, rest, TN)
    nothing = jnp.zeros((CH, LANES), F32)
    total = jnp.concatenate([nothing, grad_cols_ref[...], nothing], axis=1)
    for tap in range(3):
        piece = spread_col[CH * tap : CH * (tap + 1)]
        edge = piece[:, cols:]
        for width in (16, 32, 64):
            edge = edge + pltpu.roll(edge, width, 1)
        low = jnp.where(edge_lane >= LANES - 8, pltpu.roll(edge, LANES - 8, 1), 0.0)
        high_edge = jnp.where(edge_lane < 8, pltpu.roll(edge, LANES - 8, 1), 0.0)
        piece = jnp.concatenate([low, piece[:, :cols], high_edge], axis=1)
        total = total + (pltpu.roll(piece, (8 * (tap - 1)) % (cols + 2 * LANES), 1) if tap != 1 else piece)
    one_row = dot_split(row_sums, row_cat, TN)
    one_col = dot(high, col_cat, NT) + dot(rest, col_cat, NT)
    bias_row = jnp.sum(row_sums[:, :LANES], axis=0, keepdims=True)
    bias_row = pltpu.roll(jnp.where(lax.broadcasted_iota(jnp.int32, (8, LANES), 1) >= CH, bias_row, 0.0), 96, 1)
    for a in range(3):
        for b in range(3):
            one = one_row[CH * b : CH * (b + 1), CH * a : CH * (a + 1)]
            one = one + one_col[CH * a : CH * (a + 1), CH * b : CH * (b + 1)]
            two = [
                full[CH * (2 * b + gb) : CH * (2 * b + gb + 1), CH * (a + gb) : CH * (a + gb + 1)] for gb in range(2)
            ]
            w_scr[CH * (3 * a + b) : CH * (3 * a + b + 1), :] = jnp.concatenate([one, two[0] + two[1]], axis=1)

    weights, chans, sums_end = chunk_rows(n_row)
    tail = total[:, :LANES] + total[:, cols + LANES :] + bias_row[:1, :]
    before = lax.axis_index("row") - 1
    for j in range(n_row):
        for there, here in shares(n_row, j):
            chunk_scr[j, there, :] = w_scr[here, :]
        share = slice(chans * j, chans * (j + 1))
        chunk_scr[j, weights : weights + chans, :] = total[share, LANES : 2 * LANES]
        chunk_scr[j, weights + chans : weights + 2 * chans, :] = total[share, cols : cols + LANES]
        chunk_scr[j, weights + 2 * chans : sums_end, :] = tail[share]
        chunk_scr[j, sums_end:, :] = jnp.where(before == j, above, below)
    out_ref[...] = chunk_scr[...].astype(BF16)


def row_sum_kernel(n_row, n_col, got_ref, own_ref, out_ref):
    sums_end = chunk_rows(n_row)[2]
    me = lax.axis_index("row")
    total = got_ref[0].astype(F32)
    for j in range(1, n_row):
        total = total + got_ref[j].astype(F32)
    total = total[:sums_end]
    before = got_ref[jnp.maximum(me - 1, 0)].astype(F32)[sums_end:]
    after = got_ref[jnp.minimum(me + 1, n_row - 1)].astype(F32)[sums_end:]
    rows = own_ref[...] + off_edge("row", 0) * before + off_edge("row", n_row - 1) * after
    whole = jnp.concatenate([total, rows], axis=0).astype(BF16)
    for k in range(n_col):
        out_ref[k] = whole


def col_sum_kernel(n_row, n_col, cols, got_ref, kept_ref, out_ref, scr):
    weights, chans, sums_end = chunk_rows(n_row)
    me = lax.axis_index("col")
    whole = math.sqrt(16 * n_row * cols * n_col)
    total = got_ref[0].astype(F32)
    for k in range(1, n_col):
        total = total + got_ref[k].astype(F32)
    kept_ref[:8, :] = total[sums_end:, :] * (1.0 / math.sqrt(cols * n_col))
    kept_ref[8:, :] = total[sums_end - 8 : sums_end, :] * (1.0 / whole)
    before = got_ref[jnp.maximum(me - 1, 0)].astype(F32) * off_edge("col", 0)
    after = got_ref[jnp.minimum(me + 1, n_col - 1)].astype(F32) * off_edge("col", n_col - 1)
    mine = got_ref[me].astype(F32)
    edge = slice(weights + 2 * chans, sums_end)
    lane = lax.broadcasted_iota(jnp.int32, (chans, LANES), 1)
    low = mine[weights : weights + chans] + jnp.where(lane < 16, before[edge], 0.0)
    high = mine[weights + chans : weights + 2 * chans] + jnp.where(lane >= LANES - 16, after[edge], 0.0)
    scale = 1.0 / math.sqrt(16 * n_row)
    scr[...] = jnp.zeros(scr.shape, F32)
    scr[:weights, :] = total[:weights] * (1.0 / whole)
    scr[weights : weights + chans, :] = low * scale
    scr[weights + chans : weights + 2 * chans, :] = high * scale
    share = scr[...].astype(BF16)
    for j in range(n_row):
        out_ref[j] = share


def spread_kernel(n_row, got_ref, kept_ref, row_ref, col_ref, one_ref, bias_ref, two_ref):
    weights, chans, _ = chunk_rows(n_row)
    row_ref[:8, :] = kept_ref[:8, :CH]
    row_ref[8:, :] = kept_ref[:8, CH:]
    bias_ref[...] = kept_ref[15:, 32 : 32 + CH]
    for j in range(n_row):
        chunk = got_ref[j].astype(F32)
        for there, here in shares(n_row, j):
            one_ref[here, :] = chunk[there, :CH]
            two_ref[here, :] = chunk[there, CH:]
        col_ref[chans * j : chans * (j + 1), :LANES] = chunk[weights : weights + chans]
        col_ref[chans * j : chans * (j + 1), LANES:] = chunk[weights + chans : weights + 2 * chans]


PARAMS = pltpu.CompilerParams(vmem_limit_bytes=48 * 1024 * 1024)


def sds(shape, dtype=F32):
    return jax.ShapeDtypeStruct(shape, dtype)


def shards(n_row, n_col, grad_out, row_feat, col_feat, conv_one, bias_one, conv_two):
    cols = grad_out.shape[2]
    weights, chans, sums_end = chunk_rows(n_row)
    places = 8 * cols + LANES
    grad_out, row_feat, col_turned, conv_one, conv_two, bias_row = (
        pltpu.with_memory_space_constraint(x, pltpu.HBM)
        for x in (grad_out, row_feat, col_feat.T, conv_one, conv_two, bias_one.reshape(1, CH))
    )
    square = (3 * CH, 3 * CH)
    strip, row_feat, col_turned, grad_out, hits, k1c, k1f, w2, bias_col = pl.pallas_call(
        lambda *refs: pack_kernel(n_col, *refs),
        out_shape=(
            sds((16 + CH, LANES), BF16), sds(row_feat.shape, BF16), sds(col_turned.shape, BF16),
            sds(grad_out.shape, BF16), sds((24, places), BF16), sds(square, BF16), sds(square, BF16),
            sds((6 * CH, 4 * CH), BF16), sds((CH, 8)),
        ),
        in_specs=[pl.BlockSpec(memory_space=pltpu.HBM)] * 6,
        scratch_shapes=[
            pltpu.VMEM(conv_one.shape, BF16),
            pltpu.VMEM(conv_two.shape, BF16),
            pltpu.VMEM((1, CH), F32),
            pltpu.SemaphoreType.DMA((5 + GRAD_COPIES,)),
        ],
        compiler_params=PARAMS,
    )(row_feat, col_turned, conv_one, conv_two, bias_row, grad_out)

    def twin(index, count):
        return index ^ 1

    def other(index, count):
        return min(max(index + (1 if index % 2 else -1), 0), count - 1)

    def swap(along_row, along_col):
        pairs = [
            (r * n_col + c, along_row(r, n_row) * n_col + along_col(c, n_col))
            for r in range(n_row)
            for c in range(n_col)
        ]
        return lax.ppermute(strip, ("row", "col"), pairs)

    row_twin = swap(twin, other)
    col_twin = swap(other, twin)

    x, back, grad_rows, grad_cols = pl.pallas_call(
        own_kernel,
        out_shape=(sds((3, 2 * CH, places), BF16), sds((4 * CH, places)), sds((8, 2 * CH)), sds((CH, cols))),
        scratch_shapes=[pltpu.VMEM((cols // LANES, CH * 16, LANES), F32)],
        compiler_params=PARAMS,
    )(grad_out, w2)
    chunks, own = pl.pallas_call(
        lambda *refs: main_kernel(n_row, n_col, *refs),
        out_shape=(sds((n_row, sums_end + 8, LANES), BF16), sds((8, LANES))),
        scratch_shapes=[
            pltpu.VMEM((4 * CH, places), BF16),
            pltpu.VMEM((4 * CH, places), BF16),
            pltpu.VMEM((9 * CH, LANES), F32),
            pltpu.VMEM((n_row, sums_end + 8, LANES), F32),
        ],
        compiler_params=PARAMS,
    )(row_twin, col_twin, row_feat, col_turned, x, back, grad_rows, grad_cols, hits, k1c, k1f, bias_col)
    got = lax.all_to_all(chunks, "row", 0, 0)
    copies = pl.pallas_call(
        lambda *refs: row_sum_kernel(n_row, n_col, *refs),
        out_shape=sds((n_col, sums_end + 8, LANES), BF16),
        compiler_params=PARAMS,
    )(got, own)
    got = lax.all_to_all(copies, "col", 0, 0)
    end = -(-(weights + 2 * chans) // 16) * 16
    kept, copies = pl.pallas_call(
        lambda *refs: col_sum_kernel(n_row, n_col, cols, *refs),
        out_shape=(sds((16, LANES)), sds((n_row, end, LANES), BF16)),
        scratch_shapes=[pltpu.VMEM((end, LANES), F32)],
        compiler_params=PARAMS,
    )(got)
    got = lax.all_to_all(copies, "row", 0, 0)
    row_grad, col_grad, one, bias_grad, two = pl.pallas_call(
        lambda *refs: spread_kernel(n_row, *refs),
        out_shape=(sds((16, CH)), sds((CH, cols)), sds((9 * CH, CH)), sds((1, CH)), sds((9 * CH, CH))),
        compiler_params=PARAMS,
    )(got, kept)
    shape = conv_one.shape
    return row_grad, col_grad.T, one.reshape(shape), bias_grad[0], two.reshape(shape)


def solution(mesh):
    in_specs = (P(None, "row", "col"), P("row", None), P("col", None), P(), P(), P())
    out_specs = (P("row", None), P("col", None), P(), P(), P())
    n_row, n_col = mesh.shape["row"], mesh.shape["col"]
    return jax.shard_map(
        lambda *args: shards(n_row, n_col, *args), mesh=mesh, in_specs=in_specs, out_specs=out_specs, check_vma=False
    )
```

```python
import math

import jax
import jax.numpy as jnp
from jax import lax
from jax.experimental import pallas as pl
from jax.experimental.pallas import tpu as pltpu
from jax.sharding import PartitionSpec as P

F32, BF16 = jnp.float32, jnp.bfloat16
NN = (((1,), (0,)), ((), ()))
NT = (((1,), (1,)), ((), ()))
TN = (((0,), (0,)), ((), ()))
CH = 64
LANES = 128
GRAD_COPIES = 1


def dot(x, y, dims):
    return lax.dot_general(x, y, dims, preferred_element_type=F32)


def chunk_rows(n_row):
    weights, chans = 9 * CH // n_row, CH // n_row
    return weights, chans, weights + 3 * chans


def dot_split(x, y, dims):
    high = x.astype(BF16)
    low = (x - high.astype(F32)).astype(BF16)
    y = y.astype(BF16)
    return dot(high, y, dims) + dot(low, y, dims)


def shares(n_row, j):
    weights = 9 * CH // n_row
    main = weights // 8 * 8
    pieces = [(slice(0, main), slice(main * j, main * (j + 1)))]
    if main < weights:
        rest = weights - main
        pieces.append((slice(main, weights), slice(main * n_row + rest * j, main * n_row + rest * (j + 1))))
    return pieces


def pack_kernel(
    n_col, row_hbm, col_hbm, one_hbm, two_hbm, bias_hbm, grad_hbm,
    out_ref, row_ref, col_ref, grad_ref, ind_ref, k1c_ref, k1f_ref, w2_ref, bias_col_ref,
    one_ref, two_ref, bias_ref, sems,
):
    pairs = [
        (row_hbm, row_ref), (col_hbm, col_ref), (one_hbm, one_ref), (two_hbm, two_ref), (bias_hbm, bias_ref),
    ]
    step = CH // GRAD_COPIES
    for k in range(GRAD_COPIES):
        part = slice(step * k, step * (k + 1))
        pairs.append((grad_hbm.at[part], grad_ref.at[part]))
    copies = [pltpu.make_async_copy(x, y, sems.at[k]) for k, (x, y) in enumerate(pairs)]
    for copy in copies:
        copy.start()
    for copy in copies[:2]:
        copy.wait()
    rows = row_ref[...].astype(F32)
    out_ref[:16, :] = jnp.concatenate([rows, jnp.zeros_like(rows)], axis=1).astype(BF16)
    cols = col_ref.shape[1]
    lane = lax.broadcasted_iota(jnp.int32, (CH, LANES), 1)
    first, last = col_ref[:, :LANES].astype(F32), col_ref[:, cols - LANES :].astype(F32)
    out_ref[16:, :] = jnp.where(lane < LANES // 2, first, last).astype(BF16)
    ind_ref[...] = indicator(cols, n_col)
    for copy in copies[2:5]:
        copy.wait()
    one = [[one_ref[a, b].astype(F32) for b in range(3)] for a in range(3)]
    for k in range(3):
        rows = slice(CH * k, CH * (k + 1))
        k1c_ref[rows, :] = jnp.concatenate(one[k], axis=1).astype(BF16)
        k1f_ref[rows, :] = jnp.concatenate([one[a][k] for a in range(3)], axis=1).astype(BF16)
    nil = jnp.zeros((CH, CH), F32)
    two = [[two_ref[a, b].astype(F32) for b in range(3)] for a in range(3)]
    for b in range(3):
        for gb in range(2):
            blocks = [two[eb - gb][b] if 0 <= eb - gb <= 2 else nil for eb in range(4)]
            at = CH * (2 * b + gb)
            w2_ref[at : at + CH, :] = jnp.concatenate(blocks, axis=1).astype(BF16)
    bias = jnp.concatenate([bias_ref[...], jnp.zeros((1, LANES - CH), F32)], axis=1)
    bias_col_ref[...] = jnp.broadcast_to(bias, (8, LANES)).T[:CH, :]
    for copy in copies[5:]:
        copy.wait()


def off_edge(axis, index):
    return jnp.where(lax.axis_index(axis) == index, 0.0, 1.0).astype(F32)


def indicator(cols, n_col):
    lane = lax.broadcasted_iota(jnp.int32, (8, cols), 1)
    row = lax.broadcasted_iota(jnp.int32, (8, cols), 0)
    me = lax.axis_index("col")
    off_map = ((lane < 8) & (me == 0), lane < 0, (lane >= cols - 8) & (me == n_col - 1))
    edge_lane = lax.broadcasted_iota(jnp.int32, (8, LANES), 1)
    edge_row = lax.broadcasted_iota(jnp.int32, (8, LANES), 0)
    edge = jnp.where(edge_lane // 16 == edge_row, 1.0, 0.0)
    taps = []
    for tap in range(3):
        on_map = jnp.logical_not(off_map[tap])
        main = [jnp.where(on_map & (row == k), 1.0, 0.0) for k in range(8)]
        taps.append(jnp.concatenate(main + [edge], axis=1))
    return jnp.concatenate(taps, axis=0).astype(BF16)


def own_kernel(grad_ref, w2_ref, x_ref, back_ref, grad_rows_ref, grad_cols_ref, rows_scr):
    cols = grad_ref.shape[2]
    lane = lax.broadcasted_iota(jnp.int32, (CH, cols), 1)
    edge_lane = lax.broadcasted_iota(jnp.int32, (CH, LANES), 1)
    for piece in range(cols // LANES):
        wide = grad_ref[:, :, LANES * piece : LANES * (piece + 1)]
        rows_scr[piece] = wide.astype(F32).reshape(CH * 16, LANES)
    col_sum = jnp.zeros((CH, cols), F32)
    for half in range(2):
        rows = slice(half * CH, (half + 1) * CH)
        left = right = jnp.zeros((CH, LANES), F32)
        for k in range(8):
            pieces = [rows_scr[p, pl.ds(half * 8 + k, CH, stride=16), :] for p in range(cols // LANES)]
            line = jnp.concatenate(pieces, axis=1)
            col_sum = col_sum + line
            span = slice(k * cols, (k + 1) * cols)
            x_ref[1, rows, span] = line.astype(BF16)
            x_ref[0, rows, span] = jnp.where(lane < cols - 8, pltpu.roll(line, cols - 8, 1), 0.0).astype(BF16)
            x_ref[2, rows, span] = jnp.where(lane >= 8, pltpu.roll(line, 8, 1), 0.0).astype(BF16)
            first = pltpu.roll(pieces[0], 16 * k, 1) if k else pieces[0]
            last = pltpu.roll(pieces[-1], 16 * k + 16, 1) if k < 7 else pieces[-1]
            here = edge_lane // 16 == k
            left = jnp.where(here & (edge_lane % 16 < 8), first, left)
            right = jnp.where(here & (edge_lane % 16 >= 8), last, right)
        x_ref[0, rows, 8 * cols :] = left.astype(BF16)
        x_ref[1, rows, 8 * cols :] = jnp.zeros((CH, LANES), BF16)
        x_ref[2, rows, 8 * cols :] = right.astype(BF16)
    grad_cols_ref[...] = col_sum
    row = lax.broadcasted_iota(jnp.int32, (8, 8 * cols), 0)
    span = lax.broadcasted_iota(jnp.int32, (8, 8 * cols), 1) // cols
    grad_rows_ref[...] = dot(jnp.where(row == span, 1.0, 0.0).astype(BF16), x_ref[1, :, : 8 * cols], NT)
    x_all = x_ref[...].reshape(6 * CH, x_ref.shape[2])
    back_ref[...] = dot(w2_ref[...], x_all, TN)


def main_kernel(
    n_row, n_col, col_twin_ref, row_twin_ref, row_ref, col_ref,
    x_ref, back_ref, grad_rows_ref, grad_cols_ref, ind_ref, k1c_ref, k1f_ref, bias_ref,
    out_ref, own_ref, act_scr, inner_scr, w_scr, chunk_scr,
):
    cols = col_ref.shape[1]
    top, bottom = off_edge("row", 0), off_edge("row", n_row - 1)
    left, right = off_edge("col", 0), off_edge("col", n_col - 1)
    edge_lane = lax.broadcasted_iota(jnp.int32, (CH, LANES), 1)
    odd_row, odd_col = lax.axis_index("row") % 2 == 1, lax.axis_index("col") % 2 == 1
    twin, other = row_twin_ref[:16, :CH].astype(F32), col_twin_ref[:16, :CH].astype(F32) * (top * bottom)
    row_ext = jnp.concatenate(
        [jnp.where(odd_row, twin, other), row_ref[...].astype(F32), jnp.where(odd_row, other, twin)], axis=0
    )
    row_cat = jnp.concatenate([row_ext[8 * a : 8 * a + 32] for a in range(3)], axis=1).astype(BF16)
    twin, other = col_twin_ref[16:, :].astype(F32), row_twin_ref[16:, :].astype(F32) * (left * right)
    col_ext = jnp.concatenate(
        [jnp.where(odd_col, twin, other), col_ref[...].astype(F32), jnp.where(odd_col, other, twin)], axis=1
    )
    taps = []
    for tap in range(3):
        moved = pltpu.roll(col_ext, (8 * (1 - tap)) % (cols + 2 * LANES), 1) if tap != 1 else col_ext
        low, high = pltpu.roll(moved[:, :LANES], 8, 1), pltpu.roll(moved[:, LANES + cols :], 8, 1)
        edge = jnp.where(edge_lane < 8, low, jnp.where(edge_lane < 16, high, 0.0))
        for width in (16, 32, 64):
            edge = edge + pltpu.roll(edge, width, 1)
        taps.append(jnp.concatenate([moved[:, LANES : LANES + cols], edge], axis=1))
    col_cat = jnp.concatenate(taps, axis=0).astype(BF16)
    terms = dot(k1c_ref[...], col_cat, NN)
    low, mid, high = (terms[CH * a : CH * (a + 1)] for a in range(3))
    mid = mid + bias_ref[:, :1]
    col_part = [low + mid + high, top * low + mid + high, low + mid + bottom * high, low + mid + high]
    row_terms = dot(k1f_ref[...], row_cat, NT)
    by_tap = [row_terms[CH * b : CH * (b + 1)] for b in range(3)]
    row_part = by_tap[0] + by_tap[1] + by_tap[2]

    def spread_over(terms, k):
        return jnp.concatenate(
            [jnp.broadcast_to(terms[:, 8 * eb + k : 8 * eb + k + 1], (CH, LANES)) for eb in range(4)], axis=0
        )

    side_lane = lax.broadcasted_iota(jnp.int32, (4 * CH, LANES), 1)
    first_off = jnp.where(side_lane < 8, left - 1.0, 0.0)
    last_off = jnp.where(side_lane >= LANES - 8, right - 1.0, 0.0)
    edge_part = jnp.zeros((4 * CH, LANES), F32)
    on_map = jnp.where(side_lane % 16 < 8, left, right)
    col_part = jnp.concatenate(col_part, axis=0)
    main_sum = jnp.zeros((4 * CH, cols), F32)
    for k in range(9):
        span = slice(k * cols, (k + 1) * cols) if k < 8 else slice(8 * cols, 8 * cols + LANES)
        if k < 8:
            each = spread_over(row_part, k)
            edge_part = jnp.where(side_lane // 16 == k, each, edge_part)
            pieces = [each] * (cols // LANES)
            pieces[0] = pieces[0] + first_off * spread_over(by_tap[0], k)
            pieces[-1] = pieces[-1] + last_off * spread_over(by_tap[2], k)
            pre = jnp.concatenate(pieces, axis=1) + col_part[:, :cols]
        else:
            pre = edge_part + col_part[:, cols:]
        sig = 1.0 / (1.0 + jnp.exp(-pre))
        held = jnp.concatenate([sig[:CH] * top, sig[CH : 3 * CH], sig[3 * CH :] * bottom], axis=0)
        if k == 8:
            held = held * on_map
        act_scr[:, span] = (pre * held).astype(BF16)
        inner = (back_ref[:, span] * (held * (1.0 + pre * (1.0 - sig)))).astype(BF16)
        inner_scr[:, span] = inner
        if k < 8:
            main_sum = main_sum + inner.astype(F32)
    sums = jnp.concatenate([main_sum, inner.astype(F32)], axis=1)
    sums_of = [sums[CH * eb : CH * (eb + 1)] for eb in range(4)]

    full = dot(x_ref[...].reshape(6 * CH, x_ref.shape[2]), act_scr[...], NT)
    sums = dot(ind_ref[...], inner_scr[...], NT)
    row_sums = jnp.concatenate(
        [
            jnp.concatenate([sums[8 * b : 8 * b + 8, CH * eb : CH * (eb + 1)] for b in range(3)], axis=1)
            for eb in range(4)
        ],
        axis=0,
    )
    spread_row = dot_split(row_sums, k1f_ref[...], NN)

    def part(eb, a):
        return spread_row[8 * eb : 8 * eb + 8, CH * a : CH * (a + 1)]

    reached = [sum(part(eb, pb - eb) for eb in range(4) if 0 <= pb - eb <= 2) for pb in range(6)]
    above, mine, below = (jnp.concatenate(reached[2 * k : 2 * k + 2], axis=1) for k in range(3))
    own_ref[...] = grad_rows_ref[...] + mine
    whole = sums_of[0] + sums_of[1] + sums_of[2] + sums_of[3]
    col_sums = jnp.concatenate(
        [whole - (1.0 - top) * sums_of[1], whole, whole - (1.0 - bottom) * sums_of[2]], axis=0
    )
    high = col_sums.astype(BF16)
    rest = (col_sums - high.astype(F32)).astype(BF16)
    k1c = k1c_ref[...]
    spread_col = dot(k1c, high, TN) + dot(k1c, rest, TN)
    nothing = jnp.zeros((CH, LANES), F32)
    total = jnp.concatenate([nothing, grad_cols_ref[...], nothing], axis=1)
    for tap in range(3):
        piece = spread_col[CH * tap : CH * (tap + 1)]
        edge = piece[:, cols:]
        for width in (16, 32, 64):
            edge = edge + pltpu.roll(edge, width, 1)
        low = jnp.where(edge_lane >= LANES - 8, pltpu.roll(edge, LANES - 8, 1), 0.0)
        high_edge = jnp.where(edge_lane < 8, pltpu.roll(edge, LANES - 8, 1), 0.0)
        piece = jnp.concatenate([low, piece[:, :cols], high_edge], axis=1)
        total = total + (pltpu.roll(piece, (8 * (tap - 1)) % (cols + 2 * LANES), 1) if tap != 1 else piece)
    one_row = dot_split(row_sums, row_cat, TN)
    one_col = dot(high, col_cat, NT) + dot(rest, col_cat, NT)
    bias_row = jnp.sum(row_sums[:, :LANES], axis=0, keepdims=True)
    bias_row = pltpu.roll(jnp.where(lax.broadcasted_iota(jnp.int32, (8, LANES), 1) >= CH, bias_row, 0.0), 96, 1)
    for a in range(3):
        for b in range(3):
            one = one_row[CH * b : CH * (b + 1), CH * a : CH * (a + 1)]
            one = one + one_col[CH * a : CH * (a + 1), CH * b : CH * (b + 1)]
            two = [
                full[CH * (2 * b + gb) : CH * (2 * b + gb + 1), CH * (a + gb) : CH * (a + gb + 1)] for gb in range(2)
            ]
            w_scr[CH * (3 * a + b) : CH * (3 * a + b + 1), :] = jnp.concatenate([one, two[0] + two[1]], axis=1)

    weights, chans, sums_end = chunk_rows(n_row)
    tail = total[:, :LANES] + total[:, cols + LANES :] + bias_row[:1, :]
    before = lax.axis_index("row") - 1
    for j in range(n_row):
        for there, here in shares(n_row, j):
            chunk_scr[j, there, :] = w_scr[here, :]
        share = slice(chans * j, chans * (j + 1))
        chunk_scr[j, weights : weights + chans, :] = total[share, LANES : 2 * LANES]
        chunk_scr[j, weights + chans : weights + 2 * chans, :] = total[share, cols : cols + LANES]
        chunk_scr[j, weights + 2 * chans : sums_end, :] = tail[share]
        chunk_scr[j, sums_end:, :] = jnp.where(before == j, above, below)
    out_ref[...] = chunk_scr[...].astype(BF16)


def row_sum_kernel(n_row, n_col, got_ref, own_ref, out_ref):
    sums_end = chunk_rows(n_row)[2]
    me = lax.axis_index("row")
    total = got_ref[0].astype(F32)
    for j in range(1, n_row):
        total = total + got_ref[j].astype(F32)
    total = total[:sums_end]
    before = got_ref[jnp.maximum(me - 1, 0)].astype(F32)[sums_end:]
    after = got_ref[jnp.minimum(me + 1, n_row - 1)].astype(F32)[sums_end:]
    rows = own_ref[...] + off_edge("row", 0) * before + off_edge("row", n_row - 1) * after
    whole = jnp.concatenate([total, rows], axis=0).astype(BF16)
    for k in range(n_col):
        out_ref[k] = whole


def col_sum_kernel(n_row, n_col, cols, got_ref, kept_ref, out_ref, scr):
    weights, chans, sums_end = chunk_rows(n_row)
    me = lax.axis_index("col")
    whole = math.sqrt(16 * n_row * cols * n_col)
    total = got_ref[0].astype(F32)
    for k in range(1, n_col):
        total = total + got_ref[k].astype(F32)
    kept_ref[:8, :] = total[sums_end:, :] * (1.0 / math.sqrt(cols * n_col))
    kept_ref[8:, :] = total[sums_end - 8 : sums_end, :] * (1.0 / whole)
    before = got_ref[jnp.maximum(me - 1, 0)].astype(F32) * off_edge("col", 0)
    after = got_ref[jnp.minimum(me + 1, n_col - 1)].astype(F32) * off_edge("col", n_col - 1)
    mine = got_ref[me].astype(F32)
    edge = slice(weights + 2 * chans, sums_end)
    lane = lax.broadcasted_iota(jnp.int32, (chans, LANES), 1)
    low = mine[weights : weights + chans] + jnp.where(lane < 16, before[edge], 0.0)
    high = mine[weights + chans : weights + 2 * chans] + jnp.where(lane >= LANES - 16, after[edge], 0.0)
    scale = 1.0 / math.sqrt(16 * n_row)
    scr[...] = jnp.zeros(scr.shape, F32)
    scr[:weights, :] = total[:weights] * (1.0 / whole)
    scr[weights : weights + chans, :] = low * scale
    scr[weights + chans : weights + 2 * chans, :] = high * scale
    share = scr[...].astype(BF16)
    for j in range(n_row):
        out_ref[j] = share


def spread_kernel(n_row, got_ref, kept_ref, row_ref, col_ref, one_ref, bias_ref, two_ref):
    weights, chans, _ = chunk_rows(n_row)
    row_ref[:8, :] = kept_ref[:8, :CH]
    row_ref[8:, :] = kept_ref[:8, CH:]
    bias_ref[...] = kept_ref[15:, 32 : 32 + CH]
    for j in range(n_row):
        chunk = got_ref[j].astype(F32)
        for there, here in shares(n_row, j):
            one_ref[here, :] = chunk[there, :CH]
            two_ref[here, :] = chunk[there, CH:]
        col_ref[chans * j : chans * (j + 1), :LANES] = chunk[weights : weights + chans]
        col_ref[chans * j : chans * (j + 1), LANES:] = chunk[weights + chans : weights + 2 * chans]


PARAMS = pltpu.CompilerParams(vmem_limit_bytes=48 * 1024 * 1024)


def sds(shape, dtype=F32):
    return jax.ShapeDtypeStruct(shape, dtype)


def shards(n_row, n_col, grad_out, row_feat, col_feat, conv_one, bias_one, conv_two):
    cols = grad_out.shape[2]
    weights, chans, sums_end = chunk_rows(n_row)
    places = 8 * cols + LANES
    grad_out, row_feat, col_turned, conv_one, conv_two, bias_row = (
        pltpu.with_memory_space_constraint(x, pltpu.HBM)
        for x in (grad_out, row_feat, col_feat.T, conv_one, conv_two, bias_one.reshape(1, CH))
    )
    square = (3 * CH, 3 * CH)
    strip, row_feat, col_turned, grad_out, hits, k1c, k1f, w2, bias_col = pl.pallas_call(
        lambda *refs: pack_kernel(n_col, *refs),
        out_shape=(
            sds((16 + CH, LANES), BF16), sds(row_feat.shape, BF16), sds(col_turned.shape, BF16),
            sds(grad_out.shape, BF16), sds((24, places), BF16), sds(square, BF16), sds(square, BF16),
            sds((6 * CH, 4 * CH), BF16), sds((CH, 8)),
        ),
        in_specs=[pl.BlockSpec(memory_space=pltpu.HBM)] * 6,
        scratch_shapes=[
            pltpu.VMEM(conv_one.shape, BF16),
            pltpu.VMEM(conv_two.shape, BF16),
            pltpu.VMEM((1, CH), F32),
            pltpu.SemaphoreType.DMA((5 + GRAD_COPIES,)),
        ],
        compiler_params=PARAMS,
    )(row_feat, col_turned, conv_one, conv_two, bias_row, grad_out)

    def twin(index, count):
        return index ^ 1

    def other(index, count):
        return min(max(index + (1 if index % 2 else -1), 0), count - 1)

    def swap(along_row, along_col):
        pairs = [
            (r * n_col + c, along_row(r, n_row) * n_col + along_col(c, n_col))
            for r in range(n_row)
            for c in range(n_col)
        ]
        return lax.ppermute(strip, ("row", "col"), pairs)

    col_twin = swap(other, twin)
    row_twin = swap(twin, other)

    x, back, grad_rows, grad_cols = pl.pallas_call(
        own_kernel,
        out_shape=(sds((3, 2 * CH, places), BF16), sds((4 * CH, places)), sds((8, 2 * CH)), sds((CH, cols))),
        scratch_shapes=[pltpu.VMEM((cols // LANES, CH * 16, LANES), F32)],
        compiler_params=PARAMS,
    )(grad_out, w2)
    chunks, own = pl.pallas_call(
        lambda *refs: main_kernel(n_row, n_col, *refs),
        out_shape=(sds((n_row, sums_end + 8, LANES), BF16), sds((8, LANES))),
        scratch_shapes=[
            pltpu.VMEM((4 * CH, places), BF16),
            pltpu.VMEM((4 * CH, places), BF16),
            pltpu.VMEM((9 * CH, LANES), F32),
            pltpu.VMEM((n_row, sums_end + 8, LANES), F32),
        ],
        compiler_params=PARAMS,
    )(col_twin, row_twin, row_feat, col_turned, x, back, grad_rows, grad_cols, hits, k1c, k1f, bias_col)
    got = lax.all_to_all(chunks, "row", 0, 0)
    copies = pl.pallas_call(
        lambda *refs: row_sum_kernel(n_row, n_col, *refs),
        out_shape=sds((n_col, sums_end + 8, LANES), BF16),
        compiler_params=PARAMS,
    )(got, own)
    got = lax.all_to_all(copies, "col", 0, 0)
    end = -(-(weights + 2 * chans) // 16) * 16
    kept, copies = pl.pallas_call(
        lambda *refs: col_sum_kernel(n_row, n_col, cols, *refs),
        out_shape=(sds((16, LANES)), sds((n_row, end, LANES), BF16)),
        scratch_shapes=[pltpu.VMEM((end, LANES), F32)],
        compiler_params=PARAMS,
    )(got)
    got = lax.all_to_all(copies, "row", 0, 0)
    row_grad, col_grad, one, bias_grad, two = pl.pallas_call(
        lambda *refs: spread_kernel(n_row, *refs),
        out_shape=(sds((16, CH)), sds((CH, cols)), sds((9 * CH, CH)), sds((1, CH)), sds((9 * CH, CH))),
        compiler_params=PARAMS,
    )(got, kept)
    shape = conv_one.shape
    return row_grad, col_grad.T, one.reshape(shape), bias_grad[0], two.reshape(shape)


def solution(mesh):
    in_specs = (P(None, "row", "col"), P("row", None), P("col", None), P(), P(), P())
    out_specs = (P("row", None), P("col", None), P(), P(), P())
    n_row, n_col = mesh.shape["row"], mesh.shape["col"]
    return jax.shard_map(
        lambda *args: shards(n_row, n_col, *args), mesh=mesh, in_specs=in_specs, out_specs=out_specs, check_vma=False
    )
```

```python
import math

import jax
import jax.numpy as jnp
from jax import lax
from jax.experimental import pallas as pl
from jax.experimental.pallas import tpu as pltpu
from jax.sharding import PartitionSpec as P

F32, BF16 = jnp.float32, jnp.bfloat16
NN = (((1,), (0,)), ((), ()))
NT = (((1,), (1,)), ((), ()))
TN = (((0,), (0,)), ((), ()))
CH = 64
LANES = 128


def dot(x, y, dims):
    return lax.dot_general(x, y, dims, preferred_element_type=F32)


def chunk_rows(n_row):
    weights, chans = 9 * CH // n_row, CH // n_row
    return weights, chans, weights + 3 * chans


def split(x):
    high = x.astype(BF16)
    return high, (x - high.astype(F32)).astype(BF16)


def shares(n_row, j):
    weights = 9 * CH // n_row
    main = weights // 8 * 8
    pieces = [(slice(0, main), slice(main * j, main * (j + 1)))]
    if main < weights:
        rest = weights - main
        pieces.append((slice(main, weights), slice(main * n_row + rest * j, main * n_row + rest * (j + 1))))
    return pieces


def start_copies(sources, targets, sems):
    copies = [pltpu.make_async_copy(x, y, sems.at[k]) for k, (x, y) in enumerate(zip(sources, targets, strict=True))]
    for copy in copies:
        copy.start()
    return copies


def pack_kernel(row_hbm, col_hbm, out_ref, row_ref, col_ref, sems):
    for copy in start_copies((row_hbm, col_hbm), (row_ref, col_ref), sems):
        copy.wait()
    rows = row_ref[...].astype(F32)
    out_ref[:16, :] = jnp.concatenate([rows, jnp.zeros_like(rows)], axis=1).astype(BF16)
    cols = col_ref.shape[1]
    lane = lax.broadcasted_iota(jnp.int32, (CH, LANES), 1)
    first, last = col_ref[:, :LANES].astype(F32), col_ref[:, cols - LANES :].astype(F32)
    out_ref[16:, :] = jnp.where(lane < LANES // 2, first, last).astype(BF16)


def off_edge(axis, index):
    return jnp.where(lax.axis_index(axis) == index, 0.0, 1.0).astype(F32)


def indicator(cols, n_col):
    lane = lax.broadcasted_iota(jnp.int32, (8, cols), 1)
    row = lax.broadcasted_iota(jnp.int32, (8, cols), 0)
    me = lax.axis_index("col")
    off_map = ((lane < 8) & (me == 0), lane < 0, (lane >= cols - 8) & (me == n_col - 1))
    edge_lane = lax.broadcasted_iota(jnp.int32, (8, LANES), 1)
    edge_row = lax.broadcasted_iota(jnp.int32, (8, LANES), 0)
    edge = jnp.where(edge_lane // 16 == edge_row, 1.0, 0.0)
    taps = []
    for tap in range(3):
        on_map = jnp.logical_not(off_map[tap])
        main = [jnp.where(on_map & (row == k), 1.0, 0.0) for k in range(8)]
        taps.append(jnp.concatenate(main + [edge], axis=1))
    return jnp.concatenate(taps, axis=0).astype(BF16)


def own_kernel(
    n_col, one_hbm, two_hbm, bias_hbm, grad_hbm,
    x_ref, back_ref, grad_rows_ref, grad_cols_ref, ind_ref, k1c_ref, k1ct_ref, k1f_ref, bias_col_ref,
    rows_scr, one_ref, two_ref, bias_ref, grad_ref, sems,
):
    copies = start_copies((one_hbm, two_hbm, bias_hbm, grad_hbm), (one_ref, two_ref, bias_ref, grad_ref), sems)
    cols = grad_ref.shape[2]
    ind_ref[...] = indicator(cols, n_col)
    for copy in copies[:3]:
        copy.wait()
    one = [[one_ref[a, b].astype(F32) for b in range(3)] for a in range(3)]
    for k in range(3):
        rows = slice(CH * k, CH * (k + 1))
        k1c_ref[rows, :] = jnp.concatenate(one[k], axis=1).astype(BF16)
        k1f_ref[rows, :] = jnp.concatenate([one[a][k] for a in range(3)], axis=1).astype(BF16)
        k1ct_ref[rows, :] = jnp.concatenate([one[a][k].T for a in range(3)], axis=1).astype(BF16)
    nil = jnp.zeros((CH, CH), F32)
    two = [[two_ref[a, b].astype(F32) for b in range(3)] for a in range(3)]
    w2 = jnp.concatenate(
        [
            jnp.concatenate([two[eb - gb][b] if 0 <= eb - gb <= 2 else nil for eb in range(4)], axis=1)
            for b in range(3)
            for gb in range(2)
        ],
        axis=0,
    ).astype(BF16)
    bias = jnp.concatenate([bias_ref[...], jnp.zeros((1, LANES - CH), F32)], axis=1)
    bias_col_ref[...] = jnp.broadcast_to(bias, (8, LANES)).T[:CH, :]
    copies[3].wait()
    lane = lax.broadcasted_iota(jnp.int32, (CH, cols), 1)
    edge_lane = lax.broadcasted_iota(jnp.int32, (CH, LANES), 1)
    for piece in range(cols // LANES):
        wide = grad_ref[:, :, LANES * piece : LANES * (piece + 1)]
        rows_scr[piece] = wide.astype(F32).reshape(CH * 16, LANES)
    col_sum = jnp.zeros((CH, cols), F32)
    for half in range(2):
        rows = slice(half * CH, (half + 1) * CH)
        left = right = jnp.zeros((CH, LANES), F32)
        for k in range(8):
            pieces = [rows_scr[p, pl.ds(half * 8 + k, CH, stride=16), :] for p in range(cols // LANES)]
            line = jnp.concatenate(pieces, axis=1)
            col_sum = col_sum + line
            span = slice(k * cols, (k + 1) * cols)
            x_ref[1, rows, span] = line.astype(BF16)
            x_ref[0, rows, span] = jnp.where(lane < cols - 8, pltpu.roll(line, cols - 8, 1), 0.0).astype(BF16)
            x_ref[2, rows, span] = jnp.where(lane >= 8, pltpu.roll(line, 8, 1), 0.0).astype(BF16)
            first = pltpu.roll(pieces[0], 16 * k, 1) if k else pieces[0]
            last = pltpu.roll(pieces[-1], 16 * k + 16, 1) if k < 7 else pieces[-1]
            here = edge_lane // 16 == k
            left = jnp.where(here & (edge_lane % 16 < 8), first, left)
            right = jnp.where(here & (edge_lane % 16 >= 8), last, right)
        x_ref[0, rows, 8 * cols :] = left.astype(BF16)
        x_ref[1, rows, 8 * cols :] = jnp.zeros((CH, LANES), BF16)
        x_ref[2, rows, 8 * cols :] = right.astype(BF16)
    grad_cols_ref[...] = col_sum
    row = lax.broadcasted_iota(jnp.int32, (8, 8 * cols), 0)
    span = lax.broadcasted_iota(jnp.int32, (8, 8 * cols), 1) // cols
    grad_rows_ref[...] = dot(jnp.where(row == span, 1.0, 0.0).astype(BF16), x_ref[1, :, : 8 * cols], NT)
    x_all = x_ref[...].reshape(6 * CH, x_ref.shape[2])
    back_ref[...] = dot(w2, x_all, TN)


def main_kernel(
    n_row, n_col, row_twin_ref, col_twin_ref, row_ref, col_ref,
    x_ref, back_ref, grad_rows_ref, grad_cols_ref, ind_ref, k1c_ref, k1ct_ref, k1f_ref, bias_ref,
    out_ref, own_ref, w_scr, chunk_scr,
):
    cols = col_ref.shape[1]
    top, bottom = off_edge("row", 0), off_edge("row", n_row - 1)
    left, right = off_edge("col", 0), off_edge("col", n_col - 1)
    edge_lane = lax.broadcasted_iota(jnp.int32, (CH, LANES), 1)
    odd_row, odd_col = lax.axis_index("row") % 2 == 1, lax.axis_index("col") % 2 == 1
    twin, other = row_twin_ref[:16, :CH].astype(F32), col_twin_ref[:16, :CH].astype(F32) * (top * bottom)
    row_ext = jnp.concatenate(
        [jnp.where(odd_row, twin, other), row_ref[...].astype(F32), jnp.where(odd_row, other, twin)], axis=0
    )
    row_taps = [row_ext[8 * a : 8 * a + 32].astype(BF16) for a in range(3)]
    row_cat = jnp.concatenate([row_ext[8 * a : 8 * a + 32] for a in range(3)], axis=1).astype(BF16)
    twin, other = col_twin_ref[16:, :].astype(F32), row_twin_ref[16:, :].astype(F32) * (left * right)
    col_ext = jnp.concatenate(
        [jnp.where(odd_col, twin, other), col_ref[...].astype(F32), jnp.where(odd_col, other, twin)], axis=1
    )
    taps = []
    for tap in range(3):
        moved = pltpu.roll(col_ext, (8 * (1 - tap)) % (cols + 2 * LANES), 1) if tap != 1 else col_ext
        low, high = pltpu.roll(moved[:, :LANES], 8, 1), pltpu.roll(moved[:, LANES + cols :], 8, 1)
        edge = jnp.where(edge_lane < 8, low, jnp.where(edge_lane < 16, high, 0.0))
        for width in (16, 32, 64):
            edge = edge + pltpu.roll(edge, width, 1)
        taps.append(jnp.concatenate([moved[:, LANES : LANES + cols], edge], axis=1).astype(BF16))
    col_cat = jnp.concatenate(taps, axis=0)
    terms = dot(k1c_ref[...], col_cat, NN)
    low, mid, high = (terms[CH * a : CH * (a + 1)] for a in range(3))
    mid = mid + bias_ref[:, :1]
    col_part = [low + mid + high, top * low + mid + high, low + mid + bottom * high, low + mid + high]
    row_terms = dot(k1f_ref[...], row_cat, NT)
    by_tap = [row_terms[CH * b : CH * (b + 1)] for b in range(3)]
    row_part = by_tap[0] + by_tap[1] + by_tap[2]

    def spread_over(terms, k):
        return jnp.concatenate(
            [jnp.broadcast_to(terms[:, 8 * eb + k : 8 * eb + k + 1], (CH, LANES)) for eb in range(4)], axis=0
        )

    side_lane = lax.broadcasted_iota(jnp.int32, (4 * CH, LANES), 1)
    first_off = jnp.where(side_lane < 8, left - 1.0, 0.0)
    last_off = jnp.where(side_lane >= LANES - 8, right - 1.0, 0.0)
    edge_part = jnp.zeros((4 * CH, LANES), F32)
    on_map = jnp.where(side_lane % 16 < 8, left, right)
    col_part = jnp.concatenate(col_part, axis=0)
    main_sum = jnp.zeros((4 * CH, cols), F32)
    full = jnp.zeros((6 * CH, 4 * CH), F32)
    row_of = jnp.zeros((24, 4 * CH), F32)
    x_all = x_ref[...].reshape(6 * CH, x_ref.shape[2])
    for k in range(9):
        span = slice(k * cols, (k + 1) * cols) if k < 8 else slice(8 * cols, 8 * cols + LANES)
        if k < 8:
            each = spread_over(row_part, k)
            edge_part = jnp.where(side_lane // 16 == k, each, edge_part)
            pieces = [each] * (cols // LANES)
            pieces[0] = pieces[0] + first_off * spread_over(by_tap[0], k)
            pieces[-1] = pieces[-1] + last_off * spread_over(by_tap[2], k)
            pre = jnp.concatenate(pieces, axis=1) + col_part[:, :cols]
        else:
            pre = edge_part + col_part[:, cols:]
        sig = 1.0 / (1.0 + jnp.exp(-pre))
        held = jnp.concatenate([sig[:CH] * top, sig[CH : 3 * CH], sig[3 * CH :] * bottom], axis=0)
        if k == 8:
            held = held * on_map
        full = full + dot(x_all[:, span], (pre * held).astype(BF16), NT)
        inner = (back_ref[:, span] * (held * (1.0 + pre * (1.0 - sig)))).astype(BF16)
        row_of = row_of + dot(ind_ref[:, span], inner, NT)
        if k < 8:
            main_sum = main_sum + inner.astype(F32)
    sums = jnp.concatenate([main_sum, inner.astype(F32)], axis=1)
    sums_of = [sums[CH * eb : CH * (eb + 1)] for eb in range(4)]

    row_sums = jnp.concatenate(
        [
            jnp.concatenate([row_of[8 * b : 8 * b + 8, CH * eb : CH * (eb + 1)] for b in range(3)], axis=1)
            for eb in range(4)
        ],
        axis=0,
    )
    row_split = jnp.concatenate(split(row_sums), axis=0)
    spread_row = dot(row_split, k1f_ref[...], NN)
    spread_row = spread_row[:32] + spread_row[32:]

    def part(eb, a):
        return spread_row[8 * eb : 8 * eb + 8, CH * a : CH * (a + 1)]

    reached = [sum(part(eb, pb - eb) for eb in range(4) if 0 <= pb - eb <= 2) for pb in range(6)]
    above, mine, below = (jnp.concatenate(reached[2 * k : 2 * k + 2], axis=1) for k in range(3))
    own_ref[...] = grad_rows_ref[...] + mine
    whole = sums_of[0] + sums_of[1] + sums_of[2] + sums_of[3]
    col_sums = jnp.concatenate(
        [whole - (1.0 - top) * sums_of[1], whole, whole - (1.0 - bottom) * sums_of[2]], axis=0
    )
    col_split = jnp.concatenate(split(col_sums), axis=1)
    spread_col = dot(k1ct_ref[...], col_split, NN)
    spread_col = spread_col[:, : cols + LANES] + spread_col[:, cols + LANES :]
    nothing = jnp.zeros((CH, LANES), F32)
    total = jnp.concatenate([nothing, grad_cols_ref[...], nothing], axis=1)
    for tap in range(3):
        piece = spread_col[CH * tap : CH * (tap + 1)]
        edge = piece[:, cols:]
        for width in (16, 32, 64):
            edge = edge + pltpu.roll(edge, width, 1)
        low = jnp.where(edge_lane >= LANES - 8, pltpu.roll(edge, LANES - 8, 1), 0.0)
        high_edge = jnp.where(edge_lane < 8, pltpu.roll(edge, LANES - 8, 1), 0.0)
        piece = jnp.concatenate([low, piece[:, :cols], high_edge], axis=1)
        total = total + (pltpu.roll(piece, (8 * (tap - 1)) % (cols + 2 * LANES), 1) if tap != 1 else piece)
    one_row = [dot(row_split, jnp.concatenate([piece, piece], axis=0), TN) for piece in row_taps]
    one_col = [dot(col_split, jnp.concatenate([piece, piece], axis=1), NT) for piece in taps]
    bias_row = jnp.sum(row_sums[:, :LANES], axis=0, keepdims=True)
    bias_row = pltpu.roll(jnp.where(lax.broadcasted_iota(jnp.int32, (8, LANES), 1) >= CH, bias_row, 0.0), 96, 1)
    for a in range(3):
        for b in range(3):
            one = one_row[a][CH * b : CH * (b + 1)] + one_col[b][CH * a : CH * (a + 1)]
            two = [
                full[CH * (2 * b + gb) : CH * (2 * b + gb + 1), CH * (a + gb) : CH * (a + gb + 1)] for gb in range(2)
            ]
            w_scr[CH * (3 * a + b) : CH * (3 * a + b + 1), :] = jnp.concatenate([one, two[0] + two[1]], axis=1)

    weights, chans, sums_end = chunk_rows(n_row)
    tail = total[:, :LANES] + total[:, cols + LANES :] + bias_row[:1, :]
    before = lax.axis_index("row") - 1
    for j in range(n_row):
        for there, here in shares(n_row, j):
            chunk_scr[j, there, :] = w_scr[here, :]
        share = slice(chans * j, chans * (j + 1))
        chunk_scr[j, weights : weights + chans, :] = total[share, LANES : 2 * LANES]
        chunk_scr[j, weights + chans : weights + 2 * chans, :] = total[share, cols : cols + LANES]
        chunk_scr[j, weights + 2 * chans : sums_end, :] = tail[share]
        chunk_scr[j, sums_end:, :] = jnp.where(before == j, above, below)
    out_ref[...] = chunk_scr[...].astype(BF16)


def row_sum_kernel(n_row, n_col, got_ref, own_ref, out_ref):
    sums_end = chunk_rows(n_row)[2]
    me = lax.axis_index("row")
    total = got_ref[0].astype(F32)
    for j in range(1, n_row):
        total = total + got_ref[j].astype(F32)
    total = total[:sums_end]
    before = got_ref[jnp.maximum(me - 1, 0)].astype(F32)[sums_end:]
    after = got_ref[jnp.minimum(me + 1, n_row - 1)].astype(F32)[sums_end:]
    rows = own_ref[...] + off_edge("row", 0) * before + off_edge("row", n_row - 1) * after
    whole = jnp.concatenate([total, rows], axis=0).astype(BF16)
    for k in range(n_col):
        out_ref[k] = whole


def col_sum_kernel(n_row, n_col, cols, got_ref, kept_ref, out_ref, scr):
    weights, chans, sums_end = chunk_rows(n_row)
    me = lax.axis_index("col")
    whole = math.sqrt(16 * n_row * cols * n_col)
    total = got_ref[0].astype(F32)
    for k in range(1, n_col):
        total = total + got_ref[k].astype(F32)
    kept_ref[:8, :] = total[sums_end:, :] * (1.0 / math.sqrt(cols * n_col))
    kept_ref[8:, :] = total[sums_end - 8 : sums_end, :] * (1.0 / whole)
    before = got_ref[jnp.maximum(me - 1, 0)].astype(F32) * off_edge("col", 0)
    after = got_ref[jnp.minimum(me + 1, n_col - 1)].astype(F32) * off_edge("col", n_col - 1)
    mine = got_ref[me].astype(F32)
    edge = slice(weights + 2 * chans, sums_end)
    lane = lax.broadcasted_iota(jnp.int32, (chans, LANES), 1)
    low = mine[weights : weights + chans] + jnp.where(lane < 16, before[edge], 0.0)
    high = mine[weights + chans : weights + 2 * chans] + jnp.where(lane >= LANES - 16, after[edge], 0.0)
    scale = 1.0 / math.sqrt(16 * n_row)
    scr[...] = jnp.zeros(scr.shape, F32)
    scr[:weights, :] = total[:weights] * (1.0 / whole)
    scr[weights : weights + chans, :] = low * scale
    scr[weights + chans : weights + 2 * chans, :] = high * scale
    share = scr[...].astype(BF16)
    for j in range(n_row):
        out_ref[j] = share


def spread_kernel(n_row, got_ref, kept_ref, row_ref, col_ref, one_ref, bias_ref, two_ref):
    weights, chans, _ = chunk_rows(n_row)
    row_ref[:8, :] = kept_ref[:8, :CH]
    row_ref[8:, :] = kept_ref[:8, CH:]
    bias_ref[...] = kept_ref[15:, 32 : 32 + CH]
    for j in range(n_row):
        chunk = got_ref[j].astype(F32)
        for there, here in shares(n_row, j):
            one_ref[here, :] = chunk[there, :CH]
            two_ref[here, :] = chunk[there, CH:]
        col_ref[chans * j : chans * (j + 1), :LANES] = chunk[weights : weights + chans]
        col_ref[chans * j : chans * (j + 1), LANES:] = chunk[weights + chans : weights + 2 * chans]


PARAMS = pltpu.CompilerParams(vmem_limit_bytes=48 * 1024 * 1024)


def sds(shape, dtype=F32):
    return jax.ShapeDtypeStruct(shape, dtype)


def shards(n_row, n_col, grad_out, row_feat, col_feat, conv_one, bias_one, conv_two):
    cols = grad_out.shape[2]
    weights, chans, sums_end = chunk_rows(n_row)
    places = 8 * cols + LANES
    grad_out, row_feat, col_turned, conv_one, conv_two, bias_row = (
        pltpu.with_memory_space_constraint(x, pltpu.HBM)
        for x in (grad_out, row_feat, col_feat.T, conv_one, conv_two, bias_one.reshape(1, CH))
    )
    strip, *feats = pl.pallas_call(
        pack_kernel,
        out_shape=(sds((16 + CH, LANES), BF16), sds(row_feat.shape, BF16), sds(col_turned.shape, BF16)),
        in_specs=[pl.BlockSpec(memory_space=pltpu.HBM)] * 2,
        scratch_shapes=[pltpu.SemaphoreType.DMA((2,))],
        compiler_params=PARAMS,
    )(row_feat, col_turned)

    def twin(index, count):
        return index ^ 1

    def other(index, count):
        return min(max(index + (1 if index % 2 else -1), 0), count - 1)

    def swap(along_row, along_col):
        pairs = [
            (r * n_col + c, along_row(r, n_row) * n_col + along_col(c, n_col))
            for r in range(n_row)
            for c in range(n_col)
        ]
        return lax.ppermute(strip, ("row", "col"), pairs)

    col_twin = swap(other, twin)
    row_twin = swap(twin, other)

    square = sds((3 * CH, 3 * CH), BF16)
    held = pl.pallas_call(
        lambda *refs: own_kernel(n_col, *refs),
        out_shape=(
            sds((3, 2 * CH, places), BF16), sds((4 * CH, places)), sds((8, 2 * CH)), sds((CH, cols)),
            sds((24, places), BF16), square, square, square, sds((CH, 8)),
        ),
        in_specs=[pl.BlockSpec(memory_space=pltpu.HBM)] * 4,
        scratch_shapes=[
            pltpu.VMEM((cols // LANES, CH * 16, LANES), F32),
            pltpu.VMEM(conv_one.shape, BF16),
            pltpu.VMEM(conv_two.shape, BF16),
            pltpu.VMEM((1, CH), F32),
            pltpu.VMEM(grad_out.shape, BF16),
            pltpu.SemaphoreType.DMA((4,)),
        ],
        compiler_params=PARAMS,
    )(conv_one, conv_two, bias_row, grad_out)
    chunks, own = pl.pallas_call(
        lambda *refs: main_kernel(n_row, n_col, *refs),
        out_shape=(sds((n_row, sums_end + 8, LANES), BF16), sds((8, LANES))),
        scratch_shapes=[
            pltpu.VMEM((9 * CH, LANES), F32),
            pltpu.VMEM((n_row, sums_end + 8, LANES), F32),
        ],
        compiler_params=PARAMS,
    )(row_twin, col_twin, *feats, *held)
    got = lax.all_to_all(chunks, "row", 0, 0)
    copies = pl.pallas_call(
        lambda *refs: row_sum_kernel(n_row, n_col, *refs),
        out_shape=sds((n_col, sums_end + 8, LANES), BF16),
        compiler_params=PARAMS,
    )(got, own)
    got = lax.all_to_all(copies, "col", 0, 0)
    end = -(-(weights + 2 * chans) // 16) * 16
    kept, copies = pl.pallas_call(
        lambda *refs: col_sum_kernel(n_row, n_col, cols, *refs),
        out_shape=(sds((16, LANES)), sds((n_row, end, LANES), BF16)),
        scratch_shapes=[pltpu.VMEM((end, LANES), F32)],
        compiler_params=PARAMS,
    )(got)
    got = lax.all_to_all(copies, "row", 0, 0)
    row_grad, col_grad, one, bias_grad, two = pl.pallas_call(
        lambda *refs: spread_kernel(n_row, *refs),
        out_shape=(sds((16, CH)), sds((CH, cols)), sds((9 * CH, CH)), sds((1, CH)), sds((9 * CH, CH))),
        compiler_params=PARAMS,
    )(got, kept)
    shape = conv_one.shape
    return row_grad, col_grad.T, one.reshape(shape), bias_grad[0], two.reshape(shape)


def solution(mesh):
    in_specs = (P(None, "row", "col"), P("row", None), P("col", None), P(), P(), P())
    out_specs = (P("row", None), P("col", None), P(), P(), P())
    n_row, n_col = mesh.shape["row"], mesh.shape["col"]
    return jax.shard_map(
        lambda *args: shards(n_row, n_col, *args), mesh=mesh, in_specs=in_specs, out_specs=out_specs, check_vma=False
    )
```

```python
import math

import jax
import jax.numpy as jnp
from jax import lax
from jax.experimental import pallas as pl
from jax.experimental.pallas import tpu as pltpu
from jax.sharding import PartitionSpec as P

F32, BF16 = jnp.float32, jnp.bfloat16
NN = (((1,), (0,)), ((), ()))
NT = (((1,), (1,)), ((), ()))
TN = (((0,), (0,)), ((), ()))
CH = 64
LANES = 128


def dot(x, y, dims):
    return lax.dot_general(x, y, dims, preferred_element_type=F32)


def chunk_rows(n_row):
    weights, chans = 9 * CH // n_row, CH // n_row
    return weights, chans, weights + 3 * chans


def split(x):
    high = x.astype(BF16)
    return high, (x - high.astype(F32)).astype(BF16)


def shares(n_row, j):
    weights = 9 * CH // n_row
    main = weights // 8 * 8
    pieces = [(slice(0, main), slice(main * j, main * (j + 1)))]
    if main < weights:
        rest = weights - main
        pieces.append((slice(main, weights), slice(main * n_row + rest * j, main * n_row + rest * (j + 1))))
    return pieces


def start_copies(sources, targets, sems):
    copies = [pltpu.make_async_copy(x, y, sems.at[k]) for k, (x, y) in enumerate(zip(sources, targets, strict=True))]
    for copy in copies:
        copy.start()
    return copies


def off_edge(axis, index):
    return jnp.where(lax.axis_index(axis) == index, 0.0, 1.0).astype(F32)


def indicator(cols, n_col):
    lane = lax.broadcasted_iota(jnp.int32, (8, cols), 1)
    row = lax.broadcasted_iota(jnp.int32, (8, cols), 0)
    me = lax.axis_index("col")
    off_map = ((lane < 8) & (me == 0), lane < 0, (lane >= cols - 8) & (me == n_col - 1))
    edge_lane = lax.broadcasted_iota(jnp.int32, (8, LANES), 1)
    edge_row = lax.broadcasted_iota(jnp.int32, (8, LANES), 0)
    edge = jnp.where(edge_lane // 16 == edge_row, 1.0, 0.0)
    taps = []
    for tap in range(3):
        on_map = jnp.logical_not(off_map[tap])
        main = [jnp.where(on_map & (row == k), 1.0, 0.0) for k in range(8)]
        taps.append(jnp.concatenate(main + [edge], axis=1))
    return jnp.concatenate(taps, axis=0).astype(BF16)


def own_kernel(
    n_col, one_hbm, two_hbm, bias_hbm, row_hbm, col_hbm, grad_hbm,
    x_ref, back_ref, grad_rows_ref, grad_cols_ref, ind_ref, k1c_ref, k1ct_ref, k1f_ref, bias_col_ref, row_ref, col_ref,
    rows_scr, one_ref, two_ref, bias_ref, grad_ref, sems,
):
    copies = start_copies(
        (one_hbm, two_hbm, bias_hbm, row_hbm, col_hbm, grad_hbm),
        (one_ref, two_ref, bias_ref, row_ref, col_ref, grad_ref),
        sems,
    )
    cols = grad_ref.shape[2]
    ind_ref[...] = indicator(cols, n_col)
    for copy in copies[:5]:
        copy.wait()
    one = [[one_ref[a, b].astype(F32) for b in range(3)] for a in range(3)]
    for k in range(3):
        rows = slice(CH * k, CH * (k + 1))
        k1c_ref[rows, :] = jnp.concatenate(one[k], axis=1).astype(BF16)
        k1f_ref[rows, :] = jnp.concatenate([one[a][k] for a in range(3)], axis=1).astype(BF16)
        k1ct_ref[rows, :] = jnp.concatenate([one[a][k].T for a in range(3)], axis=1).astype(BF16)
    nil = jnp.zeros((CH, CH), F32)
    two = [[two_ref[a, b].astype(F32) for b in range(3)] for a in range(3)]
    w2 = jnp.concatenate(
        [
            jnp.concatenate([two[eb - gb][b] if 0 <= eb - gb <= 2 else nil for eb in range(4)], axis=1)
            for b in range(3)
            for gb in range(2)
        ],
        axis=0,
    ).astype(BF16)
    bias = jnp.concatenate([bias_ref[...], jnp.zeros((1, LANES - CH), F32)], axis=1)
    bias_col_ref[...] = jnp.broadcast_to(bias, (8, LANES)).T[:CH, :]
    copies[5].wait()
    lane = lax.broadcasted_iota(jnp.int32, (CH, cols), 1)
    edge_lane = lax.broadcasted_iota(jnp.int32, (CH, LANES), 1)
    for piece in range(cols // LANES):
        wide = grad_ref[:, :, LANES * piece : LANES * (piece + 1)]
        rows_scr[piece] = wide.astype(F32).reshape(CH * 16, LANES)
    col_sum = jnp.zeros((CH, cols), F32)
    for half in range(2):
        rows = slice(half * CH, (half + 1) * CH)
        left = right = jnp.zeros((CH, LANES), F32)
        for k in range(8):
            pieces = [rows_scr[p, pl.ds(half * 8 + k, CH, stride=16), :] for p in range(cols // LANES)]
            line = jnp.concatenate(pieces, axis=1)
            col_sum = col_sum + line
            span = slice(k * cols, (k + 1) * cols)
            x_ref[1, rows, span] = line.astype(BF16)
            x_ref[0, rows, span] = jnp.where(lane < cols - 8, pltpu.roll(line, cols - 8, 1), 0.0).astype(BF16)
            x_ref[2, rows, span] = jnp.where(lane >= 8, pltpu.roll(line, 8, 1), 0.0).astype(BF16)
            first = pltpu.roll(pieces[0], 16 * k, 1) if k else pieces[0]
            last = pltpu.roll(pieces[-1], 16 * k + 16, 1) if k < 7 else pieces[-1]
            here = edge_lane // 16 == k
            left = jnp.where(here & (edge_lane % 16 < 8), first, left)
            right = jnp.where(here & (edge_lane % 16 >= 8), last, right)
        x_ref[0, rows, 8 * cols :] = left.astype(BF16)
        x_ref[1, rows, 8 * cols :] = jnp.zeros((CH, LANES), BF16)
        x_ref[2, rows, 8 * cols :] = right.astype(BF16)
    grad_cols_ref[...] = col_sum
    row = lax.broadcasted_iota(jnp.int32, (8, 8 * cols), 0)
    span = lax.broadcasted_iota(jnp.int32, (8, 8 * cols), 1) // cols
    grad_rows_ref[...] = dot(jnp.where(row == span, 1.0, 0.0).astype(BF16), x_ref[1, :, : 8 * cols], NT)
    x_all = x_ref[...].reshape(6 * CH, x_ref.shape[2])
    back_ref[...] = dot(w2, x_all, TN)


def main_kernel(
    n_row, n_col, row_twin_ref, row_other_ref, col_other_ref, col_twin_ref,
    x_ref, back_ref, grad_rows_ref, grad_cols_ref, ind_ref, k1c_ref, k1ct_ref, k1f_ref, bias_ref,
    row_ref, col_ref, out_ref, own_ref, w_scr, chunk_scr,
):
    cols = col_ref.shape[1]
    top, bottom = off_edge("row", 0), off_edge("row", n_row - 1)
    left, right = off_edge("col", 0), off_edge("col", n_col - 1)
    edge_lane = lax.broadcasted_iota(jnp.int32, (CH, LANES), 1)
    odd_row, odd_col = lax.axis_index("row") % 2 == 1, lax.axis_index("col") % 2 == 1
    twin, other = row_twin_ref[...].astype(F32), row_other_ref[...].astype(F32) * (top * bottom)
    row_ext = jnp.concatenate(
        [jnp.where(odd_row, twin, other), row_ref[...].astype(F32), jnp.where(odd_row, other, twin)], axis=0
    )
    row_taps = [row_ext[8 * a : 8 * a + 32].astype(BF16) for a in range(3)]
    row_cat = jnp.concatenate([row_ext[8 * a : 8 * a + 32] for a in range(3)], axis=1).astype(BF16)
    twin, other = col_twin_ref[...].astype(F32), col_other_ref[...].astype(F32) * (left * right)
    before = jnp.where(odd_col, twin[:, cols - LANES :], other[:, cols - LANES :])
    after = jnp.where(odd_col, other[:, :LANES], twin[:, :LANES])
    col_ext = jnp.concatenate([before, col_ref[...].astype(F32), after], axis=1)
    taps = []
    for tap in range(3):
        moved = pltpu.roll(col_ext, (8 * (1 - tap)) % (cols + 2 * LANES), 1) if tap != 1 else col_ext
        low, high = pltpu.roll(moved[:, :LANES], 8, 1), pltpu.roll(moved[:, LANES + cols :], 8, 1)
        edge = jnp.where(edge_lane < 8, low, jnp.where(edge_lane < 16, high, 0.0))
        for width in (16, 32, 64):
            edge = edge + pltpu.roll(edge, width, 1)
        taps.append(jnp.concatenate([moved[:, LANES : LANES + cols], edge], axis=1).astype(BF16))
    col_cat = jnp.concatenate(taps, axis=0)
    terms = dot(k1c_ref[...], col_cat, NN)
    low, mid, high = (terms[CH * a : CH * (a + 1)] for a in range(3))
    mid = mid + bias_ref[:, :1]
    col_part = [low + mid + high, top * low + mid + high, low + mid + bottom * high, low + mid + high]
    row_terms = dot(k1f_ref[...], row_cat, NT)
    by_tap = [row_terms[CH * b : CH * (b + 1)] for b in range(3)]
    row_part = by_tap[0] + by_tap[1] + by_tap[2]

    def spread_over(terms, k):
        return jnp.concatenate(
            [jnp.broadcast_to(terms[:, 8 * eb + k : 8 * eb + k + 1], (CH, LANES)) for eb in range(4)], axis=0
        )

    side_lane = lax.broadcasted_iota(jnp.int32, (4 * CH, LANES), 1)
    first_off = jnp.where(side_lane < 8, left - 1.0, 0.0)
    last_off = jnp.where(side_lane >= LANES - 8, right - 1.0, 0.0)
    edge_part = jnp.zeros((4 * CH, LANES), F32)
    on_map = jnp.where(side_lane % 16 < 8, left, right)
    col_part = jnp.concatenate(col_part, axis=0)
    main_sum = jnp.zeros((4 * CH, cols), F32)
    two = jnp.zeros((3 * CH, 3 * CH), F32)
    row_of = jnp.zeros((24, 4 * CH), F32)
    x_half = [jnp.concatenate([x_ref[b, CH * gb : CH * (gb + 1), :] for b in range(3)], axis=0) for gb in range(2)]
    for k in range(9):
        span = slice(k * cols, (k + 1) * cols) if k < 8 else slice(8 * cols, 8 * cols + LANES)
        if k < 8:
            each = spread_over(row_part, k)
            edge_part = jnp.where(side_lane // 16 == k, each, edge_part)
            pieces = [each] * (cols // LANES)
            pieces[0] = pieces[0] + first_off * spread_over(by_tap[0], k)
            pieces[-1] = pieces[-1] + last_off * spread_over(by_tap[2], k)
            pre = jnp.concatenate(pieces, axis=1) + col_part[:, :cols]
        else:
            pre = edge_part + col_part[:, cols:]
        sig = 1.0 / (1.0 + jnp.exp(-pre))
        held = jnp.concatenate([sig[:CH] * top, sig[CH : 3 * CH], sig[3 * CH :] * bottom], axis=0)
        if k == 8:
            held = held * on_map
        act = (pre * held).astype(BF16)
        two = two + dot(x_half[0][:, span], act[: 3 * CH], NT) + dot(x_half[1][:, span], act[CH:], NT)
        inner = (back_ref[:, span] * (held * (1.0 + pre * (1.0 - sig)))).astype(BF16)
        row_of = row_of + dot(ind_ref[:, span], inner, NT)
        if k < 8:
            main_sum = main_sum + inner.astype(F32)
    sums = jnp.concatenate([main_sum, inner.astype(F32)], axis=1)
    sums_of = [sums[CH * eb : CH * (eb + 1)] for eb in range(4)]

    row_sums = jnp.concatenate(
        [
            jnp.concatenate([row_of[8 * b : 8 * b + 8, CH * eb : CH * (eb + 1)] for b in range(3)], axis=1)
            for eb in range(4)
        ],
        axis=0,
    )
    row_split = jnp.concatenate(split(row_sums), axis=0)
    spread_row = dot(row_split, k1f_ref[...], NN)
    spread_row = spread_row[:32] + spread_row[32:]

    def part(eb, a):
        return spread_row[8 * eb : 8 * eb + 8, CH * a : CH * (a + 1)]

    reached = [sum(part(eb, pb - eb) for eb in range(4) if 0 <= pb - eb <= 2) for pb in range(6)]
    above, mine, below = (jnp.concatenate(reached[2 * k : 2 * k + 2], axis=1) for k in range(3))
    own_ref[...] = grad_rows_ref[...] + mine
    whole = sums_of[0] + sums_of[1] + sums_of[2] + sums_of[3]
    col_sums = jnp.concatenate(
        [whole - (1.0 - top) * sums_of[1], whole, whole - (1.0 - bottom) * sums_of[2]], axis=0
    )
    col_split = jnp.concatenate(split(col_sums), axis=1)
    spread_col = dot(k1ct_ref[...], col_split, NN)
    spread_col = spread_col[:, : cols + LANES] + spread_col[:, cols + LANES :]
    nothing = jnp.zeros((CH, LANES), F32)
    total = jnp.concatenate([nothing, grad_cols_ref[...], nothing], axis=1)
    for tap in range(3):
        piece = spread_col[CH * tap : CH * (tap + 1)]
        edge = piece[:, cols:]
        for width in (16, 32, 64):
            edge = edge + pltpu.roll(edge, width, 1)
        low = jnp.where(edge_lane >= LANES - 8, pltpu.roll(edge, LANES - 8, 1), 0.0)
        high_edge = jnp.where(edge_lane < 8, pltpu.roll(edge, LANES - 8, 1), 0.0)
        piece = jnp.concatenate([low, piece[:, :cols], high_edge], axis=1)
        total = total + (pltpu.roll(piece, (8 * (tap - 1)) % (cols + 2 * LANES), 1) if tap != 1 else piece)
    one_row = [dot(row_split, jnp.concatenate([piece, piece], axis=0), TN) for piece in row_taps]
    one_col = [dot(col_split, jnp.concatenate([piece, piece], axis=1), NT) for piece in taps]
    bias_row = jnp.sum(row_sums[:, :LANES], axis=0, keepdims=True)
    bias_row = pltpu.roll(jnp.where(lax.broadcasted_iota(jnp.int32, (8, LANES), 1) >= CH, bias_row, 0.0), 96, 1)
    for a in range(3):
        for b in range(3):
            one = one_row[a][CH * b : CH * (b + 1)] + one_col[b][CH * a : CH * (a + 1)]
            pair = jnp.concatenate([one, two[CH * b : CH * (b + 1), CH * a : CH * (a + 1)]], axis=1)
            w_scr[CH * (3 * a + b) : CH * (3 * a + b + 1), :] = pair

    weights, chans, sums_end = chunk_rows(n_row)
    tail = total[:, :LANES] + total[:, cols + LANES :] + bias_row[:1, :]
    before = lax.axis_index("row") - 1
    for j in range(n_row):
        for there, here in shares(n_row, j):
            chunk_scr[j, there, :] = w_scr[here, :]
        share = slice(chans * j, chans * (j + 1))
        chunk_scr[j, weights : weights + chans, :] = total[share, LANES : 2 * LANES]
        chunk_scr[j, weights + chans : weights + 2 * chans, :] = total[share, cols : cols + LANES]
        chunk_scr[j, weights + 2 * chans : sums_end, :] = tail[share]
        chunk_scr[j, sums_end:, :] = jnp.where(before == j, above, below)
    out_ref[...] = chunk_scr[...].astype(BF16)


def row_sum_kernel(n_row, n_col, got_ref, own_ref, out_ref):
    sums_end = chunk_rows(n_row)[2]
    me = lax.axis_index("row")
    total = got_ref[0].astype(F32)
    for j in range(1, n_row):
        total = total + got_ref[j].astype(F32)
    total = total[:sums_end]
    before = got_ref[jnp.maximum(me - 1, 0)].astype(F32)[sums_end:]
    after = got_ref[jnp.minimum(me + 1, n_row - 1)].astype(F32)[sums_end:]
    rows = own_ref[...] + off_edge("row", 0) * before + off_edge("row", n_row - 1) * after
    whole = jnp.concatenate([total, rows], axis=0).astype(BF16)
    for k in range(n_col):
        out_ref[k] = whole


def col_sum_kernel(n_row, n_col, cols, got_ref, kept_ref, out_ref, scr):
    weights, chans, sums_end = chunk_rows(n_row)
    me = lax.axis_index("col")
    whole = math.sqrt(16 * n_row * cols * n_col)
    total = got_ref[0].astype(F32)
    for k in range(1, n_col):
        total = total + got_ref[k].astype(F32)
    kept_ref[:8, :] = total[sums_end:, :] * (1.0 / math.sqrt(cols * n_col))
    kept_ref[8:, :] = total[sums_end - 8 : sums_end, :] * (1.0 / whole)
    before = got_ref[jnp.maximum(me - 1, 0)].astype(F32) * off_edge("col", 0)
    after = got_ref[jnp.minimum(me + 1, n_col - 1)].astype(F32) * off_edge("col", n_col - 1)
    mine = got_ref[me].astype(F32)
    edge = slice(weights + 2 * chans, sums_end)
    lane = lax.broadcasted_iota(jnp.int32, (chans, LANES), 1)
    low = mine[weights : weights + chans] + jnp.where(lane < 16, before[edge], 0.0)
    high = mine[weights + chans : weights + 2 * chans] + jnp.where(lane >= LANES - 16, after[edge], 0.0)
    scale = 1.0 / math.sqrt(16 * n_row)
    scr[...] = jnp.zeros(scr.shape, F32)
    scr[:weights, :] = total[:weights] * (1.0 / whole)
    scr[weights : weights + chans, :] = low * scale
    scr[weights + chans : weights + 2 * chans, :] = high * scale
    share = scr[...].astype(BF16)
    for j in range(n_row):
        out_ref[j] = share


def spread_kernel(n_row, got_ref, kept_ref, row_ref, col_ref, one_ref, bias_ref, two_ref):
    weights, chans, _ = chunk_rows(n_row)
    row_ref[:8, :] = kept_ref[:8, :CH]
    row_ref[8:, :] = kept_ref[:8, CH:]
    bias_ref[...] = kept_ref[15:, 32 : 32 + CH]
    for j in range(n_row):
        chunk = got_ref[j].astype(F32)
        for there, here in shares(n_row, j):
            one_ref[here, :] = chunk[there, :CH]
            two_ref[here, :] = chunk[there, CH:]
        col_ref[chans * j : chans * (j + 1), :LANES] = chunk[weights : weights + chans]
        col_ref[chans * j : chans * (j + 1), LANES:] = chunk[weights + chans : weights + 2 * chans]


PARAMS = pltpu.CompilerParams(vmem_limit_bytes=48 * 1024 * 1024)


def sds(shape, dtype=F32):
    return jax.ShapeDtypeStruct(shape, dtype)


def shards(n_row, n_col, grad_out, row_feat, col_feat, conv_one, bias_one, conv_two):
    cols = grad_out.shape[2]
    weights, chans, sums_end = chunk_rows(n_row)
    places = 8 * cols + LANES
    rows, columns = row_feat, col_feat.T
    grad_out, row_feat, col_turned, conv_one, conv_two, bias_row = (
        pltpu.with_memory_space_constraint(x, pltpu.HBM)
        for x in (grad_out, row_feat, col_feat.T, conv_one, conv_two, bias_one.reshape(1, CH))
    )

    def twin(index, count):
        return index ^ 1

    def other(index, count):
        return min(max(index + (1 if index % 2 else -1), 0), count - 1)

    def swap(x, along_row, along_col):
        pairs = [
            (r * n_col + c, along_row(r, n_row) * n_col + along_col(c, n_col))
            for r in range(n_row)
            for c in range(n_col)
        ]
        return lax.ppermute(x, ("row", "col"), pairs)

    row_other, row_twin = swap(rows, other, twin), swap(rows, twin, other)
    col_twin, col_other = swap(columns, other, twin), swap(columns, twin, other)

    square = sds((3 * CH, 3 * CH), BF16)
    held = pl.pallas_call(
        lambda *refs: own_kernel(n_col, *refs),
        out_shape=(
            sds((3, 2 * CH, places), BF16), sds((4 * CH, places)), sds((8, 2 * CH)), sds((CH, cols)),
            sds((24, places), BF16), square, square, square, sds((CH, 8)),
            sds(row_feat.shape, BF16), sds(col_turned.shape, BF16),
        ),
        in_specs=[pl.BlockSpec(memory_space=pltpu.HBM)] * 6,
        scratch_shapes=[
            pltpu.VMEM((cols // LANES, CH * 16, LANES), F32),
            pltpu.VMEM(conv_one.shape, BF16),
            pltpu.VMEM(conv_two.shape, BF16),
            pltpu.VMEM((1, CH), F32),
            pltpu.VMEM(grad_out.shape, BF16),
            pltpu.SemaphoreType.DMA((6,)),
        ],
        compiler_params=PARAMS,
    )(conv_one, conv_two, bias_row, row_feat, col_turned, grad_out)
    chunks, own = pl.pallas_call(
        lambda *refs: main_kernel(n_row, n_col, *refs),
        out_shape=(sds((n_row, sums_end + 8, LANES), BF16), sds((8, LANES))),
        scratch_shapes=[
            pltpu.VMEM((9 * CH, LANES), F32),
            pltpu.VMEM((n_row, sums_end + 8, LANES), F32),
        ],
        compiler_params=PARAMS,
    )(row_twin, row_other, col_other, col_twin, *held)
    got = lax.all_to_all(chunks, "row", 0, 0)
    copies = pl.pallas_call(
        lambda *refs: row_sum_kernel(n_row, n_col, *refs),
        out_shape=sds((n_col, sums_end + 8, LANES), BF16),
        compiler_params=PARAMS,
    )(got, own)
    got = lax.all_to_all(copies, "col", 0, 0)
    end = -(-(weights + 2 * chans) // 16) * 16
    kept, copies = pl.pallas_call(
        lambda *refs: col_sum_kernel(n_row, n_col, cols, *refs),
        out_shape=(sds((16, LANES)), sds((n_row, end, LANES), BF16)),
        scratch_shapes=[pltpu.VMEM((end, LANES), F32)],
        compiler_params=PARAMS,
    )(got)
    got = lax.all_to_all(copies, "row", 0, 0)
    row_grad, col_grad, one, bias_grad, two = pl.pallas_call(
        lambda *refs: spread_kernel(n_row, *refs),
        out_shape=(sds((16, CH)), sds((CH, cols)), sds((9 * CH, CH)), sds((1, CH)), sds((9 * CH, CH))),
        compiler_params=PARAMS,
    )(got, kept)
    shape = conv_one.shape
    return row_grad, col_grad.T, one.reshape(shape), bias_grad[0], two.reshape(shape)


def solution(mesh):
    in_specs = (P(None, "row", "col"), P("row", None), P("col", None), P(), P(), P())
    out_specs = (P("row", None), P("col", None), P(), P(), P())
    n_row, n_col = mesh.shape["row"], mesh.shape["col"]
    return jax.shard_map(
        lambda *args: shards(n_row, n_col, *args), mesh=mesh, in_specs=in_specs, out_specs=out_specs, check_vma=False
    )
```

```python
import math

import jax
import jax.numpy as jnp
from jax import lax
from jax.experimental import pallas as pl
from jax.experimental.pallas import tpu as pltpu
from jax.sharding import PartitionSpec as P

F32, BF16 = jnp.float32, jnp.bfloat16
NN = (((1,), (0,)), ((), ()))
NT = (((1,), (1,)), ((), ()))
TN = (((0,), (0,)), ((), ()))
CH = 64
LANES = 128


def dot(x, y, dims):
    return lax.dot_general(x, y, dims, preferred_element_type=F32)


def chunk_rows(n_row):
    weights, chans = 9 * CH // n_row, CH // n_row
    return weights, chans, weights + 3 * chans


def split(x):
    high = x.astype(BF16)
    return high, (x - high.astype(F32)).astype(BF16)


def shares(n_row, j):
    weights = 9 * CH // n_row
    main = weights // 8 * 8
    pieces = [(slice(0, main), slice(main * j, main * (j + 1)))]
    if main < weights:
        rest = weights - main
        pieces.append((slice(main, weights), slice(main * n_row + rest * j, main * n_row + rest * (j + 1))))
    return pieces


def start_copies(sources, targets, sems):
    copies = [pltpu.make_async_copy(x, y, sems.at[k]) for k, (x, y) in enumerate(zip(sources, targets, strict=True))]
    for copy in copies:
        copy.start()
    return copies


def pack_kernel(row_hbm, col_hbm, out_ref, row_ref, col_ref, sems):
    for copy in start_copies((row_hbm, col_hbm), (row_ref, col_ref), sems):
        copy.wait()
    rows = row_ref[...].astype(F32)
    out_ref[:16, :] = jnp.concatenate([rows, jnp.zeros_like(rows)], axis=1).astype(BF16)
    cols = col_ref.shape[1]
    lane = lax.broadcasted_iota(jnp.int32, (CH, LANES), 1)
    first, last = col_ref[:, :LANES].astype(F32), col_ref[:, cols - LANES :].astype(F32)
    out_ref[16:, :] = jnp.where(lane < LANES // 2, first, last).astype(BF16)


def off_edge(axis, index):
    return jnp.where(lax.axis_index(axis) == index, 0.0, 1.0).astype(F32)


def indicator(cols, n_col):
    lane = lax.broadcasted_iota(jnp.int32, (8, cols), 1)
    row = lax.broadcasted_iota(jnp.int32, (8, cols), 0)
    me = lax.axis_index("col")
    off_map = ((lane < 8) & (me == 0), lane < 0, (lane >= cols - 8) & (me == n_col - 1))
    edge_lane = lax.broadcasted_iota(jnp.int32, (8, LANES), 1)
    edge_row = lax.broadcasted_iota(jnp.int32, (8, LANES), 0)
    edge = jnp.where(edge_lane // 16 == edge_row, 1.0, 0.0)
    taps = []
    for tap in range(3):
        on_map = jnp.logical_not(off_map[tap])
        main = [jnp.where(on_map & (row == k), 1.0, 0.0) for k in range(8)]
        taps.append(jnp.concatenate(main + [edge], axis=1))
    return jnp.concatenate(taps, axis=0).astype(BF16)


def own_kernel(
    n_col, one_hbm, two_hbm, bias_hbm, grad_hbm,
    x_ref, back_ref, grad_rows_ref, grad_cols_ref, ind_ref, k1c_ref, k1ct_ref, k1f_ref, bias_col_ref,
    rows_scr, one_ref, two_ref, bias_ref, grad_ref, sems,
):
    copies = start_copies((one_hbm, two_hbm, bias_hbm, grad_hbm), (one_ref, two_ref, bias_ref, grad_ref), sems)
    cols = grad_ref.shape[2]
    ind_ref[...] = indicator(cols, n_col)
    for copy in copies[:3]:
        copy.wait()
    one = [[one_ref[a, b].astype(F32) for b in range(3)] for a in range(3)]
    for k in range(3):
        rows = slice(CH * k, CH * (k + 1))
        k1c_ref[rows, :] = jnp.concatenate(one[k], axis=1).astype(BF16)
        k1f_ref[rows, :] = jnp.concatenate([one[a][k] for a in range(3)], axis=1).astype(BF16)
        k1ct_ref[rows, :] = jnp.concatenate([one[a][k].T for a in range(3)], axis=1).astype(BF16)
    nil = jnp.zeros((CH, CH), F32)
    two = [[two_ref[a, b].astype(F32) for b in range(3)] for a in range(3)]
    w2 = jnp.concatenate(
        [
            jnp.concatenate([two[eb - gb][b] if 0 <= eb - gb <= 2 else nil for eb in range(4)], axis=1)
            for b in range(3)
            for gb in range(2)
        ],
        axis=0,
    ).astype(BF16)
    bias = jnp.concatenate([bias_ref[...], jnp.zeros((1, LANES - CH), F32)], axis=1)
    bias_col_ref[...] = jnp.broadcast_to(bias, (8, LANES)).T[:CH, :]
    copies[3].wait()
    lane = lax.broadcasted_iota(jnp.int32, (CH, cols), 1)
    edge_lane = lax.broadcasted_iota(jnp.int32, (CH, LANES), 1)
    for piece in range(cols // LANES):
        wide = grad_ref[:, :, LANES * piece : LANES * (piece + 1)]
        rows_scr[piece] = wide.astype(F32).reshape(CH * 16, LANES)
    col_sum = jnp.zeros((CH, cols), F32)
    for half in range(2):
        rows = slice(half * CH, (half + 1) * CH)
        left = right = jnp.zeros((CH, LANES), F32)
        for k in range(8):
            pieces = [rows_scr[p, pl.ds(half * 8 + k, CH, stride=16), :] for p in range(cols // LANES)]
            line = jnp.concatenate(pieces, axis=1)
            col_sum = col_sum + line
            span = slice(k * cols, (k + 1) * cols)
            x_ref[1, rows, span] = line.astype(BF16)
            x_ref[0, rows, span] = jnp.where(lane < cols - 8, pltpu.roll(line, cols - 8, 1), 0.0).astype(BF16)
            x_ref[2, rows, span] = jnp.where(lane >= 8, pltpu.roll(line, 8, 1), 0.0).astype(BF16)
            first = pltpu.roll(pieces[0], 16 * k, 1) if k else pieces[0]
            last = pltpu.roll(pieces[-1], 16 * k + 16, 1) if k < 7 else pieces[-1]
            here = edge_lane // 16 == k
            left = jnp.where(here & (edge_lane % 16 < 8), first, left)
            right = jnp.where(here & (edge_lane % 16 >= 8), last, right)
        x_ref[0, rows, 8 * cols :] = left.astype(BF16)
        x_ref[1, rows, 8 * cols :] = jnp.zeros((CH, LANES), BF16)
        x_ref[2, rows, 8 * cols :] = right.astype(BF16)
    grad_cols_ref[...] = col_sum
    row = lax.broadcasted_iota(jnp.int32, (8, 8 * cols), 0)
    span = lax.broadcasted_iota(jnp.int32, (8, 8 * cols), 1) // cols
    grad_rows_ref[...] = dot(jnp.where(row == span, 1.0, 0.0).astype(BF16), x_ref[1, :, : 8 * cols], NT)
    x_all = x_ref[...].reshape(6 * CH, x_ref.shape[2])
    back_ref[...] = dot(w2, x_all, TN)


def main_kernel(
    n_row, n_col, row_twin_ref, col_twin_ref, row_ref, col_ref,
    x_ref, back_ref, grad_rows_ref, grad_cols_ref, ind_ref, k1c_ref, k1ct_ref, k1f_ref, bias_ref,
    out_ref, own_ref, w_scr, chunk_scr,
):
    cols = col_ref.shape[1]
    top, bottom = off_edge("row", 0), off_edge("row", n_row - 1)
    left, right = off_edge("col", 0), off_edge("col", n_col - 1)
    edge_lane = lax.broadcasted_iota(jnp.int32, (CH, LANES), 1)
    odd_row, odd_col = lax.axis_index("row") % 2 == 1, lax.axis_index("col") % 2 == 1
    twin, other = row_twin_ref[:16, :CH].astype(F32), col_twin_ref[:16, :CH].astype(F32) * (top * bottom)
    row_ext = jnp.concatenate(
        [jnp.where(odd_row, twin, other), row_ref[...].astype(F32), jnp.where(odd_row, other, twin)], axis=0
    )
    row_taps = [row_ext[8 * a : 8 * a + 32].astype(BF16) for a in range(3)]
    row_cat = jnp.concatenate([row_ext[8 * a : 8 * a + 32] for a in range(3)], axis=1).astype(BF16)
    twin, other = col_twin_ref[16:, :].astype(F32), row_twin_ref[16:, :].astype(F32) * (left * right)
    col_ext = jnp.concatenate(
        [jnp.where(odd_col, twin, other), col_ref[...].astype(F32), jnp.where(odd_col, other, twin)], axis=1
    )
    taps = []
    for tap in range(3):
        moved = pltpu.roll(col_ext, (8 * (1 - tap)) % (cols + 2 * LANES), 1) if tap != 1 else col_ext
        low, high = pltpu.roll(moved[:, :LANES], 8, 1), pltpu.roll(moved[:, LANES + cols :], 8, 1)
        edge = jnp.where(edge_lane < 8, low, jnp.where(edge_lane < 16, high, 0.0))
        for width in (16, 32, 64):
            edge = edge + pltpu.roll(edge, width, 1)
        taps.append(jnp.concatenate([moved[:, LANES : LANES + cols], edge], axis=1).astype(BF16))
    col_cat = jnp.concatenate(taps, axis=0)
    terms = dot(k1c_ref[...], col_cat, NN)
    low, mid, high = (terms[CH * a : CH * (a + 1)] for a in range(3))
    mid = mid + bias_ref[:, :1]
    col_part = [low + mid + high, top * low + mid + high, low + mid + bottom * high, low + mid + high]
    row_terms = dot(k1f_ref[...], row_cat, NT)
    by_tap = [row_terms[CH * b : CH * (b + 1)] for b in range(3)]
    row_part = by_tap[0] + by_tap[1] + by_tap[2]

    def spread_over(terms, k):
        return jnp.concatenate(
            [jnp.broadcast_to(terms[:, 8 * eb + k : 8 * eb + k + 1], (CH, LANES)) for eb in range(4)], axis=0
        )

    side_lane = lax.broadcasted_iota(jnp.int32, (4 * CH, LANES), 1)
    first_off = jnp.where(side_lane < 8, left - 1.0, 0.0)
    last_off = jnp.where(side_lane >= LANES - 8, right - 1.0, 0.0)
    edge_part = jnp.zeros((4 * CH, LANES), F32)
    on_map = jnp.where(side_lane % 16 < 8, left, right)
    col_part = jnp.concatenate(col_part, axis=0)
    main_sum = jnp.zeros((4 * CH, cols), F32)
    two = jnp.zeros((3 * CH, 3 * CH), F32)
    row_of = jnp.zeros((24, 4 * CH), F32)
    x_half = [jnp.concatenate([x_ref[b, CH * gb : CH * (gb + 1), :] for b in range(3)], axis=0) for gb in range(2)]
    for k in range(9):
        span = slice(k * cols, (k + 1) * cols) if k < 8 else slice(8 * cols, 8 * cols + LANES)
        if k < 8:
            each = spread_over(row_part, k)
            edge_part = jnp.where(side_lane // 16 == k, each, edge_part)
            pieces = [each] * (cols // LANES)
            pieces[0] = pieces[0] + first_off * spread_over(by_tap[0], k)
            pieces[-1] = pieces[-1] + last_off * spread_over(by_tap[2], k)
            pre = jnp.concatenate(pieces, axis=1) + col_part[:, :cols]
        else:
            pre = edge_part + col_part[:, cols:]
        sig = 1.0 / (1.0 + jnp.exp(-pre))
        held = jnp.concatenate([sig[:CH] * top, sig[CH : 3 * CH], sig[3 * CH :] * bottom], axis=0)
        if k == 8:
            held = held * on_map
        act = (pre * held).astype(BF16)
        joined = jnp.concatenate([x_half[0][:, span], x_half[1][:, span]], axis=1)
        two = two + dot(joined, jnp.concatenate([act[: 3 * CH], act[CH:]], axis=1), NT)
        inner = (back_ref[:, span] * (held * (1.0 + pre * (1.0 - sig)))).astype(BF16)
        row_of = row_of + dot(ind_ref[:, span], inner, NT)
        if k < 8:
            main_sum = main_sum + inner.astype(F32)
    sums = jnp.concatenate([main_sum, inner.astype(F32)], axis=1)
    sums_of = [sums[CH * eb : CH * (eb + 1)] for eb in range(4)]

    row_sums = jnp.concatenate(
        [
            jnp.concatenate([row_of[8 * b : 8 * b + 8, CH * eb : CH * (eb + 1)] for b in range(3)], axis=1)
            for eb in range(4)
        ],
        axis=0,
    )
    row_split = jnp.concatenate(split(row_sums), axis=0)
    spread_row = dot(row_split, k1f_ref[...], NN)
    spread_row = spread_row[:32] + spread_row[32:]

    def part(eb, a):
        return spread_row[8 * eb : 8 * eb + 8, CH * a : CH * (a + 1)]

    reached = [sum(part(eb, pb - eb) for eb in range(4) if 0 <= pb - eb <= 2) for pb in range(6)]
    above, mine, below = (jnp.concatenate(reached[2 * k : 2 * k + 2], axis=1) for k in range(3))
    own_ref[...] = grad_rows_ref[...] + mine
    whole = sums_of[0] + sums_of[1] + sums_of[2] + sums_of[3]
    col_sums = jnp.concatenate(
        [whole - (1.0 - top) * sums_of[1], whole, whole - (1.0 - bottom) * sums_of[2]], axis=0
    )
    col_split = jnp.concatenate(split(col_sums), axis=1)
    spread_col = dot(k1ct_ref[...], col_split, NN)
    spread_col = spread_col[:, : cols + LANES] + spread_col[:, cols + LANES :]
    nothing = jnp.zeros((CH, LANES), F32)
    total = jnp.concatenate([nothing, grad_cols_ref[...], nothing], axis=1)
    for tap in range(3):
        piece = spread_col[CH * tap : CH * (tap + 1)]
        edge = piece[:, cols:]
        for width in (16, 32, 64):
            edge = edge + pltpu.roll(edge, width, 1)
        low = jnp.where(edge_lane >= LANES - 8, pltpu.roll(edge, LANES - 8, 1), 0.0)
        high_edge = jnp.where(edge_lane < 8, pltpu.roll(edge, LANES - 8, 1), 0.0)
        piece = jnp.concatenate([low, piece[:, :cols], high_edge], axis=1)
        total = total + (pltpu.roll(piece, (8 * (tap - 1)) % (cols + 2 * LANES), 1) if tap != 1 else piece)
    one_row = [dot(row_split, jnp.concatenate([piece, piece], axis=0), TN) for piece in row_taps]
    one_col = [dot(col_split, jnp.concatenate([piece, piece], axis=1), NT) for piece in taps]
    bias_row = jnp.sum(row_sums[:, :LANES], axis=0, keepdims=True)
    bias_row = pltpu.roll(jnp.where(lax.broadcasted_iota(jnp.int32, (8, LANES), 1) >= CH, bias_row, 0.0), 96, 1)
    for a in range(3):
        for b in range(3):
            one = one_row[a][CH * b : CH * (b + 1)] + one_col[b][CH * a : CH * (a + 1)]
            pair = jnp.concatenate([one, two[CH * b : CH * (b + 1), CH * a : CH * (a + 1)]], axis=1)
            w_scr[CH * (3 * a + b) : CH * (3 * a + b + 1), :] = pair

    weights, chans, sums_end = chunk_rows(n_row)
    tail = total[:, :LANES] + total[:, cols + LANES :] + bias_row[:1, :]
    before = lax.axis_index("row") - 1
    for j in range(n_row):
        for there, here in shares(n_row, j):
            chunk_scr[j, there, :] = w_scr[here, :]
        share = slice(chans * j, chans * (j + 1))
        chunk_scr[j, weights : weights + chans, :] = total[share, LANES : 2 * LANES]
        chunk_scr[j, weights + chans : weights + 2 * chans, :] = total[share, cols : cols + LANES]
        chunk_scr[j, weights + 2 * chans : sums_end, :] = tail[share]
        chunk_scr[j, sums_end:, :] = jnp.where(before == j, above, below)
    out_ref[...] = chunk_scr[...].astype(BF16)


def row_sum_kernel(n_row, n_col, got_ref, own_ref, out_ref):
    sums_end = chunk_rows(n_row)[2]
    me = lax.axis_index("row")
    total = got_ref[0].astype(F32)
    for j in range(1, n_row):
        total = total + got_ref[j].astype(F32)
    total = total[:sums_end]
    before = got_ref[jnp.maximum(me - 1, 0)].astype(F32)[sums_end:]
    after = got_ref[jnp.minimum(me + 1, n_row - 1)].astype(F32)[sums_end:]
    rows = own_ref[...] + off_edge("row", 0) * before + off_edge("row", n_row - 1) * after
    whole = jnp.concatenate([total, rows], axis=0).astype(BF16)
    for k in range(n_col):
        out_ref[k] = whole


def col_sum_kernel(n_row, n_col, cols, got_ref, kept_ref, out_ref, scr):
    weights, chans, sums_end = chunk_rows(n_row)
    me = lax.axis_index("col")
    whole = math.sqrt(16 * n_row * cols * n_col)
    total = got_ref[0].astype(F32)
    for k in range(1, n_col):
        total = total + got_ref[k].astype(F32)
    kept_ref[:8, :] = total[sums_end:, :] * (1.0 / math.sqrt(cols * n_col))
    kept_ref[8:, :] = total[sums_end - 8 : sums_end, :] * (1.0 / whole)
    before = got_ref[jnp.maximum(me - 1, 0)].astype(F32) * off_edge("col", 0)
    after = got_ref[jnp.minimum(me + 1, n_col - 1)].astype(F32) * off_edge("col", n_col - 1)
    mine = got_ref[me].astype(F32)
    edge = slice(weights + 2 * chans, sums_end)
    lane = lax.broadcasted_iota(jnp.int32, (chans, LANES), 1)
    low = mine[weights : weights + chans] + jnp.where(lane < 16, before[edge], 0.0)
    high = mine[weights + chans : weights + 2 * chans] + jnp.where(lane >= LANES - 16, after[edge], 0.0)
    scale = 1.0 / math.sqrt(16 * n_row)
    scr[...] = jnp.zeros(scr.shape, F32)
    scr[:weights, :] = total[:weights] * (1.0 / whole)
    scr[weights : weights + chans, :] = low * scale
    scr[weights + chans : weights + 2 * chans, :] = high * scale
    share = scr[...].astype(BF16)
    for j in range(n_row):
        out_ref[j] = share


def spread_kernel(n_row, got_ref, kept_ref, row_ref, col_ref, one_ref, bias_ref, two_ref):
    weights, chans, _ = chunk_rows(n_row)
    row_ref[:8, :] = kept_ref[:8, :CH]
    row_ref[8:, :] = kept_ref[:8, CH:]
    bias_ref[...] = kept_ref[15:, 32 : 32 + CH]
    for j in range(n_row):
        chunk = got_ref[j].astype(F32)
        for there, here in shares(n_row, j):
            one_ref[here, :] = chunk[there, :CH]
            two_ref[here, :] = chunk[there, CH:]
        col_ref[chans * j : chans * (j + 1), :LANES] = chunk[weights : weights + chans]
        col_ref[chans * j : chans * (j + 1), LANES:] = chunk[weights + chans : weights + 2 * chans]


PARAMS = pltpu.CompilerParams(vmem_limit_bytes=48 * 1024 * 1024)


def sds(shape, dtype=F32):
    return jax.ShapeDtypeStruct(shape, dtype)


def shards(n_row, n_col, grad_out, row_feat, col_feat, conv_one, bias_one, conv_two):
    cols = grad_out.shape[2]
    weights, chans, sums_end = chunk_rows(n_row)
    places = 8 * cols + LANES
    grad_out, row_feat, col_turned, conv_one, conv_two, bias_row = (
        pltpu.with_memory_space_constraint(x, pltpu.HBM)
        for x in (grad_out, row_feat, col_feat.T, conv_one, conv_two, bias_one.reshape(1, CH))
    )
    strip, *feats = pl.pallas_call(
        pack_kernel,
        out_shape=(sds((16 + CH, LANES), BF16), sds(row_feat.shape, BF16), sds(col_turned.shape, BF16)),
        in_specs=[pl.BlockSpec(memory_space=pltpu.HBM)] * 2,
        scratch_shapes=[pltpu.SemaphoreType.DMA((2,))],
        compiler_params=PARAMS,
    )(row_feat, col_turned)

    def twin(index, count):
        return index ^ 1

    def other(index, count):
        return min(max(index + (1 if index % 2 else -1), 0), count - 1)

    def swap(along_row, along_col):
        pairs = [
            (r * n_col + c, along_row(r, n_row) * n_col + along_col(c, n_col))
            for r in range(n_row)
            for c in range(n_col)
        ]
        return lax.ppermute(strip, ("row", "col"), pairs)

    col_twin = swap(other, twin)
    row_twin = swap(twin, other)

    square = sds((3 * CH, 3 * CH), BF16)
    held = pl.pallas_call(
        lambda *refs: own_kernel(n_col, *refs),
        out_shape=(
            sds((3, 2 * CH, places), BF16), sds((4 * CH, places)), sds((8, 2 * CH)), sds((CH, cols)),
            sds((24, places), BF16), square, square, square, sds((CH, 8)),
        ),
        in_specs=[pl.BlockSpec(memory_space=pltpu.HBM)] * 4,
        scratch_shapes=[
            pltpu.VMEM((cols // LANES, CH * 16, LANES), F32),
            pltpu.VMEM(conv_one.shape, BF16),
            pltpu.VMEM(conv_two.shape, BF16),
            pltpu.VMEM((1, CH), F32),
            pltpu.VMEM(grad_out.shape, BF16),
            pltpu.SemaphoreType.DMA((4,)),
        ],
        compiler_params=PARAMS,
    )(conv_one, conv_two, bias_row, grad_out)
    chunks, own = pl.pallas_call(
        lambda *refs: main_kernel(n_row, n_col, *refs),
        out_shape=(sds((n_row, sums_end + 8, LANES), BF16), sds((8, LANES))),
        scratch_shapes=[
            pltpu.VMEM((9 * CH, LANES), F32),
            pltpu.VMEM((n_row, sums_end + 8, LANES), F32),
        ],
        compiler_params=PARAMS,
    )(row_twin, col_twin, *feats, *held)
    got = lax.all_to_all(chunks, "row", 0, 0)
    copies = pl.pallas_call(
        lambda *refs: row_sum_kernel(n_row, n_col, *refs),
        out_shape=sds((n_col, sums_end + 8, LANES), BF16),
        compiler_params=PARAMS,
    )(got, own)
    got = lax.all_to_all(copies, "col", 0, 0)
    end = -(-(weights + 2 * chans) // 8) * 8
    kept, copies = pl.pallas_call(
        lambda *refs: col_sum_kernel(n_row, n_col, cols, *refs),
        out_shape=(sds((16, LANES)), sds((n_row, end, LANES), BF16)),
        scratch_shapes=[pltpu.VMEM((end, LANES), F32)],
        compiler_params=PARAMS,
    )(got)
    got = lax.all_to_all(copies, "row", 0, 0)
    row_grad, col_grad, one, bias_grad, two = pl.pallas_call(
        lambda *refs: spread_kernel(n_row, *refs),
        out_shape=(sds((16, CH)), sds((CH, cols)), sds((9 * CH, CH)), sds((1, CH)), sds((9 * CH, CH))),
        compiler_params=PARAMS,
    )(got, kept)
    shape = conv_one.shape
    return row_grad, col_grad.T, one.reshape(shape), bias_grad[0], two.reshape(shape)


def solution(mesh):
    in_specs = (P(None, "row", "col"), P("row", None), P("col", None), P(), P(), P())
    out_specs = (P("row", None), P("col", None), P(), P(), P())
    n_row, n_col = mesh.shape["row"], mesh.shape["col"]
    return jax.shard_map(
        lambda *args: shards(n_row, n_col, *args), mesh=mesh, in_specs=in_specs, out_specs=out_specs, check_vma=False
    )
```

```python
import math

import jax
import jax.numpy as jnp
from jax import lax
from jax.experimental import pallas as pl
from jax.experimental.pallas import tpu as pltpu
from jax.sharding import PartitionSpec as P

F32, BF16 = jnp.float32, jnp.bfloat16
NN = (((1,), (0,)), ((), ()))
NT = (((1,), (1,)), ((), ()))
TN = (((0,), (0,)), ((), ()))
CH = 64
LANES = 128


def dot(x, y, dims):
    return lax.dot_general(x, y, dims, preferred_element_type=F32)


def chunk_rows(n_row):
    weights, chans = 9 * CH // n_row, CH // n_row
    return weights, chans, weights + 3 * chans


def split(x):
    high = x.astype(BF16)
    return high, (x - high.astype(F32)).astype(BF16)


def shares(n_row, j):
    weights = 9 * CH // n_row
    main = weights // 8 * 8
    pieces = [(slice(0, main), slice(main * j, main * (j + 1)))]
    if main < weights:
        rest = weights - main
        pieces.append((slice(main, weights), slice(main * n_row + rest * j, main * n_row + rest * (j + 1))))
    return pieces


def start_copies(sources, targets, sems):
    copies = [pltpu.make_async_copy(x, y, sems.at[k]) for k, (x, y) in enumerate(zip(sources, targets, strict=True))]
    for copy in copies:
        copy.start()
    return copies


def pack_kernel(row_hbm, col_hbm, out_ref, row_ref, col_ref, sems):
    for copy in start_copies((row_hbm, col_hbm), (row_ref, col_ref), sems):
        copy.wait()
    rows = row_ref[...].astype(F32)
    out_ref[:16, :] = jnp.concatenate([rows, jnp.zeros_like(rows)], axis=1).astype(BF16)
    cols = col_ref.shape[1]
    lane = lax.broadcasted_iota(jnp.int32, (CH, LANES), 1)
    first, last = col_ref[:, :LANES].astype(F32), col_ref[:, cols - LANES :].astype(F32)
    out_ref[16:, :] = jnp.where(lane < LANES // 2, first, last).astype(BF16)


def off_edge(axis, index):
    return jnp.where(lax.axis_index(axis) == index, 0.0, 1.0).astype(F32)


def indicator(cols, n_col):
    lane = lax.broadcasted_iota(jnp.int32, (8, cols), 1)
    row = lax.broadcasted_iota(jnp.int32, (8, cols), 0)
    me = lax.axis_index("col")
    off_map = ((lane < 8) & (me == 0), lane < 0, (lane >= cols - 8) & (me == n_col - 1))
    edge_lane = lax.broadcasted_iota(jnp.int32, (8, LANES), 1)
    edge_row = lax.broadcasted_iota(jnp.int32, (8, LANES), 0)
    edge = jnp.where(edge_lane // 16 == edge_row, 1.0, 0.0)
    taps = []
    for tap in range(3):
        on_map = jnp.logical_not(off_map[tap])
        main = [jnp.where(on_map & (row == k), 1.0, 0.0) for k in range(8)]
        taps.append(jnp.concatenate(main + [edge], axis=1))
    taps.append(jnp.zeros(taps[0].shape, F32))
    return jnp.concatenate(taps, axis=0).astype(BF16)


def own_kernel(
    n_col, one_hbm, two_hbm, bias_hbm, grad_hbm,
    x_ref, back_ref, grad_rows_ref, grad_cols_ref, ind_ref, k1c_ref, k1ct_ref, k1f_ref, bias_col_ref,
    rows_scr, one_ref, two_ref, bias_ref, grad_ref, sems,
):
    copies = start_copies((one_hbm, two_hbm, bias_hbm, grad_hbm), (one_ref, two_ref, bias_ref, grad_ref), sems)
    cols = grad_ref.shape[2]
    ind_ref[...] = indicator(cols, n_col)
    for copy in copies[:3]:
        copy.wait()
    one = [[one_ref[a, b].astype(F32) for b in range(3)] for a in range(3)]
    for k in range(3):
        rows = slice(CH * k, CH * (k + 1))
        k1c_ref[rows, :] = jnp.concatenate(one[k], axis=1).astype(BF16)
        k1f_ref[rows, :] = jnp.concatenate([one[a][k] for a in range(3)], axis=1).astype(BF16)
        k1ct_ref[rows, :] = jnp.concatenate([one[a][k].T for a in range(3)], axis=1).astype(BF16)
    nil = jnp.zeros((CH, CH), F32)
    two = [[two_ref[a, b].astype(F32) for b in range(3)] for a in range(3)]
    w2 = jnp.concatenate(
        [
            jnp.concatenate([two[eb - gb][b] if 0 <= eb - gb <= 2 else nil for eb in range(4)], axis=1)
            for b in range(3)
            for gb in range(2)
        ],
        axis=0,
    ).astype(BF16)
    bias = jnp.concatenate([bias_ref[...], jnp.zeros((1, LANES - CH), F32)], axis=1)
    bias_col_ref[...] = jnp.broadcast_to(bias, (8, LANES)).T[:CH, :]
    copies[3].wait()
    lane = lax.broadcasted_iota(jnp.int32, (CH, cols), 1)
    edge_lane = lax.broadcasted_iota(jnp.int32, (CH, LANES), 1)
    for piece in range(cols // LANES):
        wide = grad_ref[:, :, LANES * piece : LANES * (piece + 1)]
        rows_scr[piece, : CH * 16, :] = wide.astype(F32).reshape(CH * 16, LANES)
    col_sum = jnp.zeros((CH, cols), F32)
    for half in range(2):
        rows = slice(half * CH, (half + 1) * CH)
        left = right = jnp.zeros((CH, LANES), F32)
        for k in range(8):
            pieces = [rows_scr[p, pl.ds(half * 8 + k, CH, stride=16), :] for p in range(cols // LANES)]
            line = jnp.concatenate(pieces, axis=1)
            col_sum = col_sum + line
            span = slice(k * cols, (k + 1) * cols)
            x_ref[1, rows, span] = line.astype(BF16)
            x_ref[0, rows, span] = jnp.where(lane < cols - 8, pltpu.roll(line, cols - 8, 1), 0.0).astype(BF16)
            x_ref[2, rows, span] = jnp.where(lane >= 8, pltpu.roll(line, 8, 1), 0.0).astype(BF16)
            first = pltpu.roll(pieces[0], 16 * k, 1) if k else pieces[0]
            last = pltpu.roll(pieces[-1], 16 * k + 16, 1) if k < 7 else pieces[-1]
            here = edge_lane // 16 == k
            left = jnp.where(here & (edge_lane % 16 < 8), first, left)
            right = jnp.where(here & (edge_lane % 16 >= 8), last, right)
        x_ref[0, rows, 8 * cols :] = left.astype(BF16)
        x_ref[1, rows, 8 * cols :] = jnp.zeros((CH, LANES), BF16)
        x_ref[2, rows, 8 * cols :] = right.astype(BF16)
    grad_cols_ref[...] = col_sum
    row = lax.broadcasted_iota(jnp.int32, (8, 8 * cols), 0)
    span = lax.broadcasted_iota(jnp.int32, (8, 8 * cols), 1) // cols
    grad_rows_ref[...] = dot(jnp.where(row == span, 1.0, 0.0).astype(BF16), x_ref[1, :, : 8 * cols], NT)
    x_all = x_ref[...].reshape(6 * CH, x_ref.shape[2])
    back_ref[...] = dot(w2, x_all, TN)


def main_kernel(
    n_row, n_col, row_twin_ref, col_twin_ref, row_ref, col_ref,
    x_ref, back_ref, grad_rows_ref, grad_cols_ref, ind_ref, k1c_ref, k1ct_ref, k1f_ref, bias_ref,
    out_ref, own_ref, w_scr, chunk_scr,
):
    cols = col_ref.shape[1]
    top, bottom = off_edge("row", 0), off_edge("row", n_row - 1)
    left, right = off_edge("col", 0), off_edge("col", n_col - 1)
    edge_lane = lax.broadcasted_iota(jnp.int32, (CH, LANES), 1)
    odd_row, odd_col = lax.axis_index("row") % 2 == 1, lax.axis_index("col") % 2 == 1
    twin, other = row_twin_ref[:16, :CH].astype(F32), col_twin_ref[:16, :CH].astype(F32) * (top * bottom)
    row_ext = jnp.concatenate(
        [jnp.where(odd_row, twin, other), row_ref[...].astype(F32), jnp.where(odd_row, other, twin)], axis=0
    )
    row_taps = [row_ext[8 * a : 8 * a + 32].astype(BF16) for a in range(3)]
    row_cat = jnp.concatenate([row_ext[8 * a : 8 * a + 32] for a in range(3)], axis=1).astype(BF16)
    twin, other = col_twin_ref[16:, :].astype(F32), row_twin_ref[16:, :].astype(F32) * (left * right)
    col_ext = jnp.concatenate(
        [jnp.where(odd_col, twin, other), col_ref[...].astype(F32), jnp.where(odd_col, other, twin)], axis=1
    )
    taps = []
    for tap in range(3):
        moved = pltpu.roll(col_ext, (8 * (1 - tap)) % (cols + 2 * LANES), 1) if tap != 1 else col_ext
        low, high = pltpu.roll(moved[:, :LANES], 8, 1), pltpu.roll(moved[:, LANES + cols :], 8, 1)
        edge = jnp.where(edge_lane < 8, low, jnp.where(edge_lane < 16, high, 0.0))
        for width in (16, 32, 64):
            edge = edge + pltpu.roll(edge, width, 1)
        taps.append(jnp.concatenate([moved[:, LANES : LANES + cols], edge], axis=1).astype(BF16))
    col_cat = jnp.concatenate(taps, axis=0)
    terms = dot(k1c_ref[...], col_cat, NN)
    low, mid, high = (terms[CH * a : CH * (a + 1)] for a in range(3))
    mid = mid + bias_ref[:, :1]
    col_part = [low + mid + high, top * low + mid + high, low + mid + bottom * high, low + mid + high]
    row_terms = dot(k1f_ref[...], row_cat, NT)
    by_tap = [row_terms[CH * b : CH * (b + 1)] for b in range(3)]
    row_part = by_tap[0] + by_tap[1] + by_tap[2]

    def spread_over(terms, k):
        return jnp.concatenate(
            [jnp.broadcast_to(terms[:, 8 * eb + k : 8 * eb + k + 1], (CH, LANES)) for eb in range(4)], axis=0
        )

    side_lane = lax.broadcasted_iota(jnp.int32, (4 * CH, LANES), 1)
    first_off = jnp.where(side_lane < 8, left - 1.0, 0.0)
    last_off = jnp.where(side_lane >= LANES - 8, right - 1.0, 0.0)
    edge_part = jnp.zeros((4 * CH, LANES), F32)
    on_map = jnp.where(side_lane % 16 < 8, left, right)
    col_part = jnp.concatenate(col_part, axis=0)
    main_sum = jnp.zeros((4 * CH, cols), F32)
    two = jnp.zeros((3 * CH, 3 * CH), F32)
    row_of = jnp.zeros((32, 4 * CH), F32)
    x_half = [jnp.concatenate([x_ref[b, CH * gb : CH * (gb + 1), :] for b in range(3)], axis=0) for gb in range(2)]
    for k in range(9):
        span = slice(k * cols, (k + 1) * cols) if k < 8 else slice(8 * cols, 8 * cols + LANES)
        if k < 8:
            each = spread_over(row_part, k)
            edge_part = jnp.where(side_lane // 16 == k, each, edge_part)
            pieces = [each] * (cols // LANES)
            pieces[0] = pieces[0] + first_off * spread_over(by_tap[0], k)
            pieces[-1] = pieces[-1] + last_off * spread_over(by_tap[2], k)
            pre = jnp.concatenate(pieces, axis=1) + col_part[:, :cols]
        else:
            pre = edge_part + col_part[:, cols:]
        sig = 1.0 / (1.0 + jnp.exp(-pre))
        held = jnp.concatenate([sig[:CH] * top, sig[CH : 3 * CH], sig[3 * CH :] * bottom], axis=0)
        if k == 8:
            held = held * on_map
        act = (pre * held).astype(BF16)
        joined = jnp.concatenate([x_half[0][:, span], x_half[1][:, span]], axis=1)
        two = two + dot(joined, jnp.concatenate([act[: 3 * CH], act[CH:]], axis=1), NT)
        inner = (back_ref[:, span] * (held * (1.0 + pre * (1.0 - sig)))).astype(BF16)
        row_of = row_of + dot(ind_ref[:, span], inner, NT)
        if k < 8:
            main_sum = main_sum + inner.astype(F32)
    sums = jnp.concatenate([main_sum, inner.astype(F32)], axis=1)
    sums_of = [sums[CH * eb : CH * (eb + 1)] for eb in range(4)]

    row_sums = jnp.concatenate(
        [
            jnp.concatenate([row_of[8 * b : 8 * b + 8, CH * eb : CH * (eb + 1)] for b in range(3)], axis=1)
            for eb in range(4)
        ],
        axis=0,
    )
    row_split = jnp.concatenate(split(row_sums), axis=0)
    spread_row = dot(row_split, k1f_ref[...], NN)
    spread_row = spread_row[:32] + spread_row[32:]

    def part(eb, a):
        return spread_row[8 * eb : 8 * eb + 8, CH * a : CH * (a + 1)]

    reached = [sum(part(eb, pb - eb) for eb in range(4) if 0 <= pb - eb <= 2) for pb in range(6)]
    above, mine, below = (jnp.concatenate(reached[2 * k : 2 * k + 2], axis=1) for k in range(3))
    own_ref[...] = grad_rows_ref[...] + mine
    whole = sums_of[0] + sums_of[1] + sums_of[2] + sums_of[3]
    col_sums = jnp.concatenate(
        [whole - (1.0 - top) * sums_of[1], whole, whole - (1.0 - bottom) * sums_of[2]], axis=0
    )
    col_split = jnp.concatenate(split(col_sums), axis=1)
    spread_col = dot(k1ct_ref[...], col_split, NN)
    spread_col = spread_col[:, : cols + LANES] + spread_col[:, cols + LANES :]
    nothing = jnp.zeros((CH, LANES), F32)
    total = jnp.concatenate([nothing, grad_cols_ref[...], nothing], axis=1)
    for tap in range(3):
        piece = spread_col[CH * tap : CH * (tap + 1)]
        edge = piece[:, cols:]
        for width in (16, 32, 64):
            edge = edge + pltpu.roll(edge, width, 1)
        low = jnp.where(edge_lane >= LANES - 8, pltpu.roll(edge, LANES - 8, 1), 0.0)
        high_edge = jnp.where(edge_lane < 8, pltpu.roll(edge, LANES - 8, 1), 0.0)
        piece = jnp.concatenate([low, piece[:, :cols], high_edge], axis=1)
        total = total + (pltpu.roll(piece, (8 * (tap - 1)) % (cols + 2 * LANES), 1) if tap != 1 else piece)
    one_row = [dot(row_split, jnp.concatenate([piece, piece], axis=0), TN) for piece in row_taps]
    one_col = [dot(col_split, jnp.concatenate([piece, piece], axis=1), NT) for piece in taps]
    bias_row = jnp.sum(row_sums[:, :LANES], axis=0, keepdims=True)
    bias_row = pltpu.roll(jnp.where(lax.broadcasted_iota(jnp.int32, (8, LANES), 1) >= CH, bias_row, 0.0), 96, 1)
    for a in range(3):
        for b in range(3):
            one = one_row[a][CH * b : CH * (b + 1)] + one_col[b][CH * a : CH * (a + 1)]
            pair = jnp.concatenate([one, two[CH * b : CH * (b + 1), CH * a : CH * (a + 1)]], axis=1)
            w_scr[CH * (3 * a + b) : CH * (3 * a + b + 1), :] = pair

    weights, chans, sums_end = chunk_rows(n_row)
    tail = total[:, :LANES] + total[:, cols + LANES :] + bias_row[:1, :]
    before = lax.axis_index("row") - 1
    for j in range(n_row):
        for there, here in shares(n_row, j):
            chunk_scr[j, there, :] = w_scr[here, :]
        share = slice(chans * j, chans * (j + 1))
        chunk_scr[j, weights : weights + chans, :] = total[share, LANES : 2 * LANES]
        chunk_scr[j, weights + chans : weights + 2 * chans, :] = total[share, cols : cols + LANES]
        chunk_scr[j, weights + 2 * chans : sums_end, :] = tail[share]
        chunk_scr[j, sums_end:, :] = jnp.where(before == j, above, below)
    out_ref[...] = chunk_scr[...].astype(BF16)


def row_sum_kernel(n_row, n_col, got_ref, own_ref, out_ref):
    sums_end = chunk_rows(n_row)[2]
    me = lax.axis_index("row")
    total = got_ref[0].astype(F32)
    for j in range(1, n_row):
        total = total + got_ref[j].astype(F32)
    total = total[:sums_end]
    before = got_ref[jnp.maximum(me - 1, 0)].astype(F32)[sums_end:]
    after = got_ref[jnp.minimum(me + 1, n_row - 1)].astype(F32)[sums_end:]
    rows = own_ref[...] + off_edge("row", 0) * before + off_edge("row", n_row - 1) * after
    whole = jnp.concatenate([total, rows], axis=0).astype(BF16)
    for k in range(n_col):
        out_ref[k] = whole


def col_sum_kernel(n_row, n_col, cols, got_ref, kept_ref, out_ref, scr):
    weights, chans, sums_end = chunk_rows(n_row)
    me = lax.axis_index("col")
    whole = math.sqrt(16 * n_row * cols * n_col)
    total = got_ref[0].astype(F32)
    for k in range(1, n_col):
        total = total + got_ref[k].astype(F32)
    kept_ref[:8, :] = total[sums_end:, :] * (1.0 / math.sqrt(cols * n_col))
    kept_ref[8:, :] = total[sums_end - 8 : sums_end, :] * (1.0 / whole)
    before = got_ref[jnp.maximum(me - 1, 0)].astype(F32) * off_edge("col", 0)
    after = got_ref[jnp.minimum(me + 1, n_col - 1)].astype(F32) * off_edge("col", n_col - 1)
    mine = got_ref[me].astype(F32)
    edge = slice(weights + 2 * chans, sums_end)
    lane = lax.broadcasted_iota(jnp.int32, (chans, LANES), 1)
    low = mine[weights : weights + chans] + jnp.where(lane < 16, before[edge], 0.0)
    high = mine[weights + chans : weights + 2 * chans] + jnp.where(lane >= LANES - 16, after[edge], 0.0)
    scale = 1.0 / math.sqrt(16 * n_row)
    scr[...] = jnp.zeros(scr.shape, F32)
    scr[:weights, :] = total[:weights] * (1.0 / whole)
    scr[weights : weights + chans, :] = low * scale
    scr[weights + chans : weights + 2 * chans, :] = high * scale
    share = scr[...].astype(BF16)
    for j in range(n_row):
        out_ref[j] = share


def spread_kernel(n_row, got_ref, kept_ref, row_ref, col_ref, one_ref, bias_ref, two_ref):
    weights, chans, _ = chunk_rows(n_row)
    row_ref[:8, :] = kept_ref[:8, :CH]
    row_ref[8:, :] = kept_ref[:8, CH:]
    bias_ref[...] = kept_ref[15:, 32 : 32 + CH]
    for j in range(n_row):
        chunk = got_ref[j].astype(F32)
        for there, here in shares(n_row, j):
            one_ref[here, :] = chunk[there, :CH]
            two_ref[here, :] = chunk[there, CH:]
        col_ref[chans * j : chans * (j + 1), :LANES] = chunk[weights : weights + chans]
        col_ref[chans * j : chans * (j + 1), LANES:] = chunk[weights + chans : weights + 2 * chans]


PARAMS = pltpu.CompilerParams(vmem_limit_bytes=48 * 1024 * 1024)


def sds(shape, dtype=F32):
    return jax.ShapeDtypeStruct(shape, dtype)


def shards(n_row, n_col, grad_out, row_feat, col_feat, conv_one, bias_one, conv_two):
    cols = grad_out.shape[2]
    weights, chans, sums_end = chunk_rows(n_row)
    places = 8 * cols + LANES
    grad_out, row_feat, col_turned, conv_one, conv_two, bias_row = (
        pltpu.with_memory_space_constraint(x, pltpu.HBM)
        for x in (grad_out, row_feat, col_feat.T, conv_one, conv_two, bias_one.reshape(1, CH))
    )
    strip, *feats = pl.pallas_call(
        pack_kernel,
        out_shape=(sds((16 + CH, LANES), BF16), sds(row_feat.shape, BF16), sds(col_turned.shape, BF16)),
        in_specs=[pl.BlockSpec(memory_space=pltpu.HBM)] * 2,
        scratch_shapes=[pltpu.SemaphoreType.DMA((2,))],
        compiler_params=PARAMS,
    )(row_feat, col_turned)

    def twin(index, count):
        return index ^ 1

    def other(index, count):
        return min(max(index + (1 if index % 2 else -1), 0), count - 1)

    def swap(along_row, along_col):
        pairs = [
            (r * n_col + c, along_row(r, n_row) * n_col + along_col(c, n_col))
            for r in range(n_row)
            for c in range(n_col)
        ]
        return lax.ppermute(strip, ("row", "col"), pairs)

    col_twin = swap(other, twin)
    row_twin = swap(twin, other)

    square = sds((3 * CH, 3 * CH), BF16)
    held = pl.pallas_call(
        lambda *refs: own_kernel(n_col, *refs),
        out_shape=(
            sds((3, 2 * CH, places), BF16), sds((4 * CH, places)), sds((8, 2 * CH)), sds((CH, cols)),
            sds((32, places), BF16), square, square, square, sds((CH, 8)),
        ),
        in_specs=[pl.BlockSpec(memory_space=pltpu.HBM)] * 4,
        scratch_shapes=[
            pltpu.VMEM((cols // LANES, CH * 16 + 16, LANES), F32),
            pltpu.VMEM(conv_one.shape, BF16),
            pltpu.VMEM(conv_two.shape, BF16),
            pltpu.VMEM((1, CH), F32),
            pltpu.VMEM(grad_out.shape, BF16),
            pltpu.SemaphoreType.DMA((4,)),
        ],
        compiler_params=PARAMS,
    )(conv_one, conv_two, bias_row, grad_out)
    chunks, own = pl.pallas_call(
        lambda *refs: main_kernel(n_row, n_col, *refs),
        out_shape=(sds((n_row, sums_end + 8, LANES), BF16), sds((8, LANES))),
        scratch_shapes=[
            pltpu.VMEM((9 * CH, LANES), F32),
            pltpu.VMEM((n_row, sums_end + 8, LANES), F32),
        ],
        compiler_params=PARAMS,
    )(row_twin, col_twin, *feats, *held)
    got = lax.all_to_all(chunks, "row", 0, 0)
    copies = pl.pallas_call(
        lambda *refs: row_sum_kernel(n_row, n_col, *refs),
        out_shape=sds((n_col, sums_end + 8, LANES), BF16),
        compiler_params=PARAMS,
    )(got, own)
    got = lax.all_to_all(copies, "col", 0, 0)
    end = -(-(weights + 2 * chans) // 16) * 16
    kept, copies = pl.pallas_call(
        lambda *refs: col_sum_kernel(n_row, n_col, cols, *refs),
        out_shape=(sds((16, LANES)), sds((n_row, end, LANES), BF16)),
        scratch_shapes=[pltpu.VMEM((end, LANES), F32)],
        compiler_params=PARAMS,
    )(got)
    got = lax.all_to_all(copies, "row", 0, 0)
    row_grad, col_grad, one, bias_grad, two = pl.pallas_call(
        lambda *refs: spread_kernel(n_row, *refs),
        out_shape=(sds((16, CH)), sds((CH, cols)), sds((9 * CH, CH)), sds((1, CH)), sds((9 * CH, CH))),
        compiler_params=PARAMS,
    )(got, kept)
    shape = conv_one.shape
    return row_grad, col_grad.T, one.reshape(shape), bias_grad[0], two.reshape(shape)


def solution(mesh):
    in_specs = (P(None, "row", "col"), P("row", None), P("col", None), P(), P(), P())
    out_specs = (P("row", None), P("col", None), P(), P(), P())
    n_row, n_col = mesh.shape["row"], mesh.shape["col"]
    return jax.shard_map(
        lambda *args: shards(n_row, n_col, *args), mesh=mesh, in_specs=in_specs, out_specs=out_specs, check_vma=False
    )
```

```python
import math

import jax
import jax.numpy as jnp
from jax import lax
from jax.experimental import pallas as pl
from jax.experimental.pallas import tpu as pltpu
from jax.sharding import PartitionSpec as P

F32, BF16 = jnp.float32, jnp.bfloat16
NN = (((1,), (0,)), ((), ()))
NT = (((1,), (1,)), ((), ()))
TN = (((0,), (0,)), ((), ()))
CH = 64
LANES = 128


def dot(x, y, dims):
    return lax.dot_general(x, y, dims, preferred_element_type=F32)


def chunk_rows(n_row):
    weights, chans = 9 * CH // n_row, CH // n_row
    return weights, chans, weights + 3 * chans


def split(x):
    high = x.astype(BF16)
    return high, (x - high.astype(F32)).astype(BF16)


def shares(n_row, j):
    weights = 9 * CH // n_row
    main = weights // 8 * 8
    pieces = [(slice(0, main), slice(main * j, main * (j + 1)))]
    if main < weights:
        rest = weights - main
        pieces.append((slice(main, weights), slice(main * n_row + rest * j, main * n_row + rest * (j + 1))))
    return pieces


def start_copies(sources, targets, sems):
    copies = [pltpu.make_async_copy(x, y, sems.at[k]) for k, (x, y) in enumerate(zip(sources, targets, strict=True))]
    for copy in copies:
        copy.start()
    return copies


def pack_kernel(row_hbm, col_hbm, out_ref, row_ref, col_ref, sems):
    for copy in start_copies((row_hbm, col_hbm), (row_ref, col_ref), sems):
        copy.wait()
    rows = row_ref[...].astype(F32)
    out_ref[:16, :] = jnp.concatenate([rows, jnp.zeros_like(rows)], axis=1).astype(BF16)
    cols = col_ref.shape[1]
    lane = lax.broadcasted_iota(jnp.int32, (CH, LANES), 1)
    first, last = col_ref[:, :LANES].astype(F32), col_ref[:, cols - LANES :].astype(F32)
    out_ref[16:, :] = jnp.where(lane < LANES // 2, first, last).astype(BF16)


def off_edge(axis, index):
    return jnp.where(lax.axis_index(axis) == index, 0.0, 1.0).astype(F32)


def indicator(cols, n_col):
    lane = lax.broadcasted_iota(jnp.int32, (8, cols), 1)
    row = lax.broadcasted_iota(jnp.int32, (8, cols), 0)
    me = lax.axis_index("col")
    off_map = ((lane < 8) & (me == 0), lane < 0, (lane >= cols - 8) & (me == n_col - 1))
    edge_lane = lax.broadcasted_iota(jnp.int32, (8, LANES), 1)
    edge_row = lax.broadcasted_iota(jnp.int32, (8, LANES), 0)
    edge = jnp.where(edge_lane // 16 == edge_row, 1.0, 0.0)
    taps = []
    for tap in range(3):
        on_map = jnp.logical_not(off_map[tap])
        main = [jnp.where(on_map & (row == k), 1.0, 0.0) for k in range(8)]
        taps.append(jnp.concatenate(main + [edge], axis=1))
    taps.append(jnp.zeros(taps[0].shape, F32))
    return jnp.concatenate(taps, axis=0).astype(BF16)


def own_kernel(
    n_col, one_hbm, two_hbm, bias_hbm, grad_hbm,
    x_ref, back_ref, grad_rows_ref, grad_cols_ref, ind_ref, k1c_ref, k1ct_ref, k1f_ref, bias_col_ref,
    rows_scr, one_ref, two_ref, bias_ref, grad_ref, sems,
):
    copies = start_copies((one_hbm, two_hbm, bias_hbm, grad_hbm), (one_ref, two_ref, bias_ref, grad_ref), sems)
    cols = grad_ref.shape[2]
    ind_ref[...] = indicator(cols, n_col)
    for copy in copies[:3]:
        copy.wait()
    one = [[one_ref[a, b].astype(F32) for b in range(3)] for a in range(3)]
    for k in range(3):
        rows = slice(CH * k, CH * (k + 1))
        k1c_ref[rows, :] = jnp.concatenate(one[k], axis=1).astype(BF16)
        k1f_ref[rows, :] = jnp.concatenate([one[a][k] for a in range(3)], axis=1).astype(BF16)
        k1ct_ref[rows, :] = jnp.concatenate([one[a][k].T for a in range(3)], axis=1).astype(BF16)
    nil = jnp.zeros((CH, CH), F32)
    two = [[two_ref[a, b].astype(F32) for b in range(3)] for a in range(3)]
    w2 = jnp.concatenate(
        [
            jnp.concatenate([two[eb - gb][b] if 0 <= eb - gb <= 2 else nil for eb in range(4)], axis=1)
            for b in range(3)
            for gb in range(2)
        ],
        axis=0,
    ).astype(BF16)
    bias = jnp.concatenate([bias_ref[...], jnp.zeros((1, LANES - CH), F32)], axis=1)
    bias_col_ref[...] = jnp.broadcast_to(bias, (8, LANES)).T[:CH, :]
    copies[3].wait()
    lane = lax.broadcasted_iota(jnp.int32, (CH, cols), 1)
    edge_lane = lax.broadcasted_iota(jnp.int32, (CH, LANES), 1)
    for piece in range(cols // LANES):
        wide = grad_ref[:, :, LANES * piece : LANES * (piece + 1)]
        rows_scr[piece, : CH * 16, :] = wide.astype(F32).reshape(CH * 16, LANES)
    col_sum = jnp.zeros((CH, cols), F32)
    for half in range(2):
        rows = slice(half * CH, (half + 1) * CH)
        left = right = jnp.zeros((CH, LANES), F32)
        for k in range(8):
            pieces = [rows_scr[p, pl.ds(half * 8 + k, CH, stride=16), :] for p in range(cols // LANES)]
            line = jnp.concatenate(pieces, axis=1)
            col_sum = col_sum + line
            span = slice(k * cols, (k + 1) * cols)
            x_ref[1, rows, span] = line.astype(BF16)
            x_ref[0, rows, span] = jnp.where(lane < cols - 8, pltpu.roll(line, cols - 8, 1), 0.0).astype(BF16)
            x_ref[2, rows, span] = jnp.where(lane >= 8, pltpu.roll(line, 8, 1), 0.0).astype(BF16)
            first = pltpu.roll(pieces[0], 16 * k, 1) if k else pieces[0]
            last = pltpu.roll(pieces[-1], 16 * k + 16, 1) if k < 7 else pieces[-1]
            here = edge_lane // 16 == k
            left = jnp.where(here & (edge_lane % 16 < 8), first, left)
            right = jnp.where(here & (edge_lane % 16 >= 8), last, right)
        x_ref[0, rows, 8 * cols :] = left.astype(BF16)
        x_ref[1, rows, 8 * cols :] = jnp.zeros((CH, LANES), BF16)
        x_ref[2, rows, 8 * cols :] = right.astype(BF16)
    grad_cols_ref[...] = col_sum
    row = lax.broadcasted_iota(jnp.int32, (8, 8 * cols), 0)
    span = lax.broadcasted_iota(jnp.int32, (8, 8 * cols), 1) // cols
    grad_rows_ref[...] = dot(jnp.where(row == span, 1.0, 0.0).astype(BF16), x_ref[1, :, : 8 * cols], NT)
    x_all = x_ref[...].reshape(6 * CH, x_ref.shape[2])
    back_ref[...] = dot(w2, x_all, TN)


def main_kernel(
    n_row, n_col, row_twin_ref, col_twin_ref, row_ref, col_ref,
    x_ref, back_ref, grad_rows_ref, grad_cols_ref, ind_ref, k1c_ref, k1ct_ref, k1f_ref, bias_ref,
    out_ref, own_ref, w_scr, chunk_scr,
):
    cols = col_ref.shape[1]
    top, bottom = off_edge("row", 0), off_edge("row", n_row - 1)
    left, right = off_edge("col", 0), off_edge("col", n_col - 1)
    edge_lane = lax.broadcasted_iota(jnp.int32, (CH, LANES), 1)
    odd_row, odd_col = lax.axis_index("row") % 2 == 1, lax.axis_index("col") % 2 == 1
    twin, other = row_twin_ref[:16, :CH].astype(F32), col_twin_ref[:16, :CH].astype(F32) * (top * bottom)
    row_ext = jnp.concatenate(
        [jnp.where(odd_row, twin, other), row_ref[...].astype(F32), jnp.where(odd_row, other, twin)], axis=0
    )
    row_taps = [row_ext[8 * a : 8 * a + 32].astype(BF16) for a in range(3)]
    row_cat = jnp.concatenate([row_ext[8 * a : 8 * a + 32] for a in range(3)], axis=1).astype(BF16)
    twin, other = col_twin_ref[16:, :].astype(F32), row_twin_ref[16:, :].astype(F32) * (left * right)
    col_ext = jnp.concatenate(
        [jnp.where(odd_col, twin, other), col_ref[...].astype(F32), jnp.where(odd_col, other, twin)], axis=1
    )
    taps = []
    for tap in range(3):
        moved = pltpu.roll(col_ext, (8 * (1 - tap)) % (cols + 2 * LANES), 1) if tap != 1 else col_ext
        low, high = pltpu.roll(moved[:, :LANES], 8, 1), pltpu.roll(moved[:, LANES + cols :], 8, 1)
        edge = jnp.where(edge_lane < 8, low, jnp.where(edge_lane < 16, high, 0.0))
        for width in (16, 32, 64):
            edge = edge + pltpu.roll(edge, width, 1)
        taps.append(jnp.concatenate([moved[:, LANES : LANES + cols], edge], axis=1).astype(BF16))
    col_cat = jnp.concatenate(taps, axis=0)
    terms = dot(k1c_ref[...], col_cat, NN)
    low, mid, high = (terms[CH * a : CH * (a + 1)] for a in range(3))
    mid = mid + bias_ref[:, :1]
    col_part = [low + mid + high, top * low + mid + high, low + mid + bottom * high, low + mid + high]
    row_terms = dot(k1f_ref[...], row_cat, NT)
    by_tap = [row_terms[CH * b : CH * (b + 1)] for b in range(3)]
    row_part = by_tap[0] + by_tap[1] + by_tap[2]

    def spread_over(terms, k):
        return jnp.concatenate(
            [jnp.broadcast_to(terms[:, 8 * eb + k : 8 * eb + k + 1], (CH, LANES)) for eb in range(4)], axis=0
        )

    side_lane = lax.broadcasted_iota(jnp.int32, (4 * CH, LANES), 1)
    first_off = jnp.where(side_lane < 8, left - 1.0, 0.0)
    last_off = jnp.where(side_lane >= LANES - 8, right - 1.0, 0.0)
    edge_part = jnp.zeros((4 * CH, LANES), F32)
    on_map = jnp.where(side_lane % 16 < 8, left, right)
    col_part = jnp.concatenate(col_part, axis=0)
    main_sum = jnp.zeros((4 * CH, cols), F32)
    two = jnp.zeros((3 * CH, 3 * CH), F32)
    row_of = jnp.zeros((32, 4 * CH), F32)
    x_half = [jnp.concatenate([x_ref[b, CH * gb : CH * (gb + 1), :] for b in range(3)], axis=0) for gb in range(2)]
    for k in range(9):
        span = slice(k * cols, (k + 1) * cols) if k < 8 else slice(8 * cols, 8 * cols + LANES)
        if k < 8:
            each = spread_over(row_part, k)
            edge_part = jnp.where(side_lane // 16 == k, each, edge_part)
            pieces = [each] * (cols // LANES)
            pieces[0] = pieces[0] + first_off * spread_over(by_tap[0], k)
            pieces[-1] = pieces[-1] + last_off * spread_over(by_tap[2], k)
            pre = jnp.concatenate(pieces, axis=1) + col_part[:, :cols]
        else:
            pre = edge_part + col_part[:, cols:]
        sig = 1.0 / (1.0 + jnp.exp(-pre))
        held = jnp.concatenate([sig[:CH] * top, sig[CH : 3 * CH], sig[3 * CH :] * bottom], axis=0)
        if k == 8:
            held = held * on_map
        act = (pre * held).astype(BF16)
        joined = jnp.concatenate([x_half[0][:, span], x_half[1][:, span]], axis=1)
        two = two + dot(joined, jnp.concatenate([act[: 3 * CH], act[CH:]], axis=1), NT)
        inner = (back_ref[:, span] * (held * (1.0 + pre * (1.0 - sig)))).astype(BF16)
        row_of = row_of + dot(ind_ref[:, span], inner, NT)
        if k < 8:
            main_sum = main_sum + inner.astype(F32)
    sums = jnp.concatenate([main_sum, inner.astype(F32)], axis=1)
    sums_of = [sums[CH * eb : CH * (eb + 1)] for eb in range(4)]

    row_sums = jnp.concatenate(
        [
            jnp.concatenate([row_of[8 * b : 8 * b + 8, CH * eb : CH * (eb + 1)] for b in range(3)], axis=1)
            for eb in range(4)
        ],
        axis=0,
    )
    row_split = jnp.concatenate(split(row_sums), axis=0)
    spread_row = dot(row_split, k1f_ref[...], NN)
    spread_row = spread_row[:32] + spread_row[32:]

    def part(eb, a):
        return spread_row[8 * eb : 8 * eb + 8, CH * a : CH * (a + 1)]

    reached = [sum(part(eb, pb - eb) for eb in range(4) if 0 <= pb - eb <= 2) for pb in range(6)]
    above, mine, below = (jnp.concatenate(reached[2 * k : 2 * k + 2], axis=1) for k in range(3))
    own_ref[...] = grad_rows_ref[...] + mine
    whole = sums_of[0] + sums_of[1] + sums_of[2] + sums_of[3]
    col_sums = jnp.concatenate(
        [whole - (1.0 - top) * sums_of[1], whole, whole - (1.0 - bottom) * sums_of[2]], axis=0
    )
    col_split = jnp.concatenate(split(col_sums), axis=1)
    spread_col = dot(k1ct_ref[...], col_split, NN)
    spread_col = spread_col[:, : cols + LANES] + spread_col[:, cols + LANES :]
    nothing = jnp.zeros((CH, LANES), F32)
    total = jnp.concatenate([nothing, grad_cols_ref[...], nothing], axis=1)
    for tap in range(3):
        piece = spread_col[CH * tap : CH * (tap + 1)]
        edge = piece[:, cols:]
        for width in (16, 32, 64):
            edge = edge + pltpu.roll(edge, width, 1)
        low = jnp.where(edge_lane >= LANES - 8, pltpu.roll(edge, LANES - 8, 1), 0.0)
        high_edge = jnp.where(edge_lane < 8, pltpu.roll(edge, LANES - 8, 1), 0.0)
        piece = jnp.concatenate([low, piece[:, :cols], high_edge], axis=1)
        total = total + (pltpu.roll(piece, (8 * (tap - 1)) % (cols + 2 * LANES), 1) if tap != 1 else piece)
    one_row = [dot(row_split, jnp.concatenate([piece, piece], axis=0), TN) for piece in row_taps]
    one_col = [dot(col_split, jnp.concatenate([piece, piece], axis=1), NT) for piece in taps]
    bias_row = jnp.sum(row_sums[:, :LANES], axis=0, keepdims=True)
    bias_row = pltpu.roll(jnp.where(lax.broadcasted_iota(jnp.int32, (8, LANES), 1) >= CH, bias_row, 0.0), 96, 1)
    for a in range(3):
        for b in range(3):
            one = one_row[a][CH * b : CH * (b + 1)] + one_col[b][CH * a : CH * (a + 1)]
            pair = jnp.concatenate([one, two[CH * b : CH * (b + 1), CH * a : CH * (a + 1)]], axis=1)
            w_scr[CH * (3 * a + b) : CH * (3 * a + b + 1), :] = pair

    weights, chans, sums_end = chunk_rows(n_row)
    tail = total[:, :LANES] + total[:, cols + LANES :] + bias_row[:1, :]
    before = lax.axis_index("row") - 1
    for j in range(n_row):
        for there, here in shares(n_row, j):
            chunk_scr[j, there, :] = w_scr[here, :]
        share = slice(chans * j, chans * (j + 1))
        chunk_scr[j, weights : weights + chans, :] = total[share, LANES : 2 * LANES]
        chunk_scr[j, weights + chans : weights + 2 * chans, :] = total[share, cols : cols + LANES]
        chunk_scr[j, weights + 2 * chans : sums_end, :] = tail[share]
        chunk_scr[j, sums_end:, :] = jnp.where(before == j, above, below)
    out_ref[...] = chunk_scr[...].astype(BF16)


def row_sum_kernel(n_row, got_ref, own_ref, out_ref):
    sums_end = chunk_rows(n_row)[2]
    me = lax.axis_index("row")
    total = got_ref[0].astype(F32)
    for j in range(1, n_row):
        total = total + got_ref[j].astype(F32)
    total = total[:sums_end]
    before = got_ref[jnp.maximum(me - 1, 0)].astype(F32)[sums_end:]
    after = got_ref[jnp.minimum(me + 1, n_row - 1)].astype(F32)[sums_end:]
    rows = own_ref[...] + off_edge("row", 0) * before + off_edge("row", n_row - 1) * after
    out_ref[...] = jnp.concatenate([total, rows], axis=0)


def pair_kernel(n_row, mine_ref, twin_ref, out_ref):
    weights, chans, sums_end = chunk_rows(n_row)
    edge = slice(weights + 2 * chans, sums_end)
    out_ref[...] = mine_ref[...] + twin_ref[...]
    lane = lax.broadcasted_iota(jnp.int32, (chans, LANES), 1)
    summed = (lane >= 32) & (lane < 32 + CH)
    out_ref[edge, :] = mine_ref[edge, :] + jnp.where(summed, twin_ref[edge, :], 0.0)


def four_kernel(left_ref, right_ref, out_ref):
    out_ref[...] = left_ref[...] + right_ref[...]


def col_sum_kernel(
    n_row, n_col, cols, mine_ref, twin_ref, other_ref, four_ref, last_ref, kept_ref, out_ref, scr
):
    weights, chans, sums_end = chunk_rows(n_row)
    odd = lax.axis_index("col") % 2 == 1
    whole = math.sqrt(16 * n_row * cols * n_col)
    total = four_ref[...] + last_ref[...]
    kept_ref[:8, :] = total[sums_end:, :] * (1.0 / math.sqrt(cols * n_col))
    kept_ref[8:, :] = total[sums_end - 8 : sums_end, :] * (1.0 / whole)
    mine, twin, other = mine_ref[...], twin_ref[...], other_ref[...]
    before = jnp.where(odd, twin, other) * off_edge("col", 0)
    after = jnp.where(odd, other, twin) * off_edge("col", n_col - 1)
    edge = slice(weights + 2 * chans, sums_end)
    lane = lax.broadcasted_iota(jnp.int32, (chans, LANES), 1)
    low = mine[weights : weights + chans] + jnp.where(lane < 16, before[edge], 0.0)
    high = mine[weights + chans : weights + 2 * chans] + jnp.where(lane >= LANES - 16, after[edge], 0.0)
    scale = 1.0 / math.sqrt(16 * n_row)
    scr[...] = jnp.zeros(scr.shape, F32)
    scr[:weights, :] = total[:weights] * (1.0 / whole)
    scr[weights : weights + chans, :] = low * scale
    scr[weights + chans : weights + 2 * chans, :] = high * scale
    share = scr[...].astype(BF16)
    for j in range(n_row):
        out_ref[j] = share


def spread_kernel(n_row, got_ref, kept_ref, row_ref, col_ref, one_ref, bias_ref, two_ref):
    weights, chans, _ = chunk_rows(n_row)
    row_ref[:8, :] = kept_ref[:8, :CH]
    row_ref[8:, :] = kept_ref[:8, CH:]
    bias_ref[...] = kept_ref[15:, 32 : 32 + CH]
    for j in range(n_row):
        chunk = got_ref[j].astype(F32)
        for there, here in shares(n_row, j):
            one_ref[here, :] = chunk[there, :CH]
            two_ref[here, :] = chunk[there, CH:]
        col_ref[chans * j : chans * (j + 1), :LANES] = chunk[weights : weights + chans]
        col_ref[chans * j : chans * (j + 1), LANES:] = chunk[weights + chans : weights + 2 * chans]


PARAMS = pltpu.CompilerParams(vmem_limit_bytes=48 * 1024 * 1024)


def sds(shape, dtype=F32):
    return jax.ShapeDtypeStruct(shape, dtype)


def shards(n_row, n_col, grad_out, row_feat, col_feat, conv_one, bias_one, conv_two):
    cols = grad_out.shape[2]
    weights, chans, sums_end = chunk_rows(n_row)
    places = 8 * cols + LANES
    grad_out, row_feat, col_turned, conv_one, conv_two, bias_row = (
        pltpu.with_memory_space_constraint(x, pltpu.HBM)
        for x in (grad_out, row_feat, col_feat.T, conv_one, conv_two, bias_one.reshape(1, CH))
    )
    strip, *feats = pl.pallas_call(
        pack_kernel,
        out_shape=(sds((16 + CH, LANES), BF16), sds(row_feat.shape, BF16), sds(col_turned.shape, BF16)),
        in_specs=[pl.BlockSpec(memory_space=pltpu.HBM)] * 2,
        scratch_shapes=[pltpu.SemaphoreType.DMA((2,))],
        compiler_params=PARAMS,
    )(row_feat, col_turned)

    def twin(index, count):
        return index ^ 1

    def other(index, count):
        return min(max(index + (1 if index % 2 else -1), 0), count - 1)

    def swap(along_row, along_col):
        pairs = [
            (r * n_col + c, along_row(r, n_row) * n_col + along_col(c, n_col))
            for r in range(n_row)
            for c in range(n_col)
        ]
        return lax.ppermute(strip, ("row", "col"), pairs)

    col_twin = swap(other, twin)
    row_twin = swap(twin, other)

    square = sds((3 * CH, 3 * CH), BF16)
    held = pl.pallas_call(
        lambda *refs: own_kernel(n_col, *refs),
        out_shape=(
            sds((3, 2 * CH, places), BF16), sds((4 * CH, places)), sds((8, 2 * CH)), sds((CH, cols)),
            sds((32, places), BF16), square, square, square, sds((CH, 8)),
        ),
        in_specs=[pl.BlockSpec(memory_space=pltpu.HBM)] * 4,
        scratch_shapes=[
            pltpu.VMEM((cols // LANES, CH * 16 + 16, LANES), F32),
            pltpu.VMEM(conv_one.shape, BF16),
            pltpu.VMEM(conv_two.shape, BF16),
            pltpu.VMEM((1, CH), F32),
            pltpu.VMEM(grad_out.shape, BF16),
            pltpu.SemaphoreType.DMA((4,)),
        ],
        compiler_params=PARAMS,
    )(conv_one, conv_two, bias_row, grad_out)
    chunks, own = pl.pallas_call(
        lambda *refs: main_kernel(n_row, n_col, *refs),
        out_shape=(sds((n_row, sums_end + 8, LANES), BF16), sds((8, LANES))),
        scratch_shapes=[
            pltpu.VMEM((9 * CH, LANES), F32),
            pltpu.VMEM((n_row, sums_end + 8, LANES), F32),
        ],
        compiler_params=PARAMS,
    )(row_twin, col_twin, *feats, *held)
    got = lax.all_to_all(chunks, "row", 0, 0)
    part = sds((sums_end + 8, LANES))
    mine = pl.pallas_call(
        lambda *refs: row_sum_kernel(n_row, *refs), out_shape=part, compiler_params=PARAMS
    )(got, own)
    beside = [(c, c ^ 1) for c in range(n_col)]
    outside = [(c, (c + (1 if c % 2 else -1)) % n_col) for c in range(n_col)]
    across = [(c, (c + (-3 if c % 2 else 3)) % n_col) for c in range(n_col)]
    paired = lax.ppermute(mine, "col", beside)
    two_sum = pl.pallas_call(
        lambda *refs: pair_kernel(n_row, *refs), out_shape=part, compiler_params=PARAMS
    )(mine, paired)
    side = lax.ppermute(two_sum, "col", outside)
    four = pl.pallas_call(four_kernel, out_shape=part, compiler_params=PARAMS)(two_sum, side)
    last = lax.ppermute(four, "col", across)
    end = -(-(weights + 2 * chans) // 16) * 16
    kept, copies = pl.pallas_call(
        lambda *refs: col_sum_kernel(n_row, n_col, cols, *refs),
        out_shape=(sds((16, LANES)), sds((n_row, end, LANES), BF16)),
        scratch_shapes=[pltpu.VMEM((end, LANES), F32)],
        compiler_params=PARAMS,
    )(mine, paired, side, four, last)
    got = lax.all_to_all(copies, "row", 0, 0)
    row_grad, col_grad, one, bias_grad, two = pl.pallas_call(
        lambda *refs: spread_kernel(n_row, *refs),
        out_shape=(sds((16, CH)), sds((CH, cols)), sds((9 * CH, CH)), sds((1, CH)), sds((9 * CH, CH))),
        compiler_params=PARAMS,
    )(got, kept)
    shape = conv_one.shape
    return row_grad, col_grad.T, one.reshape(shape), bias_grad[0], two.reshape(shape)


def solution(mesh):
    in_specs = (P(None, "row", "col"), P("row", None), P("col", None), P(), P(), P())
    out_specs = (P("row", None), P("col", None), P(), P(), P())
    n_row, n_col = mesh.shape["row"], mesh.shape["col"]
    return jax.shard_map(
        lambda *args: shards(n_row, n_col, *args), mesh=mesh, in_specs=in_specs, out_specs=out_specs, check_vma=False
    )
```

```python
import math

import jax
import jax.numpy as jnp
from jax import lax
from jax.experimental import pallas as pl
from jax.experimental.pallas import tpu as pltpu
from jax.sharding import PartitionSpec as P

F32, BF16 = jnp.float32, jnp.bfloat16
NN = (((1,), (0,)), ((), ()))
NT = (((1,), (1,)), ((), ()))
TN = (((0,), (0,)), ((), ()))
CH = 64
LANES = 128


def dot(x, y, dims):
    return lax.dot_general(x, y, dims, preferred_element_type=F32)


def chunk_rows(n_row):
    weights, chans = 9 * CH // n_row, CH // n_row
    return weights, chans, weights + 3 * chans


def split(x):
    high = x.astype(BF16)
    return high, (x - high.astype(F32)).astype(BF16)


def shares(n_row, j):
    weights = 9 * CH // n_row
    main = weights // 8 * 8
    pieces = [(slice(0, main), slice(main * j, main * (j + 1)))]
    if main < weights:
        rest = weights - main
        pieces.append((slice(main, weights), slice(main * n_row + rest * j, main * n_row + rest * (j + 1))))
    return pieces


def start_copies(sources, targets, sems):
    copies = [pltpu.make_async_copy(x, y, sems.at[k]) for k, (x, y) in enumerate(zip(sources, targets, strict=True))]
    for copy in copies:
        copy.start()
    return copies


def pack_kernel(*refs):
    out_ref, row_ref, col_ref = refs[6:9]
    copies = start_copies(refs[:6], refs[7:13], refs[13])
    for copy in copies[:2]:
        copy.wait()
    rows = row_ref[...].astype(F32)
    out_ref[:16, :] = jnp.concatenate([rows, jnp.zeros_like(rows)], axis=1).astype(BF16)
    cols = col_ref.shape[1]
    lane = lax.broadcasted_iota(jnp.int32, (CH, LANES), 1)
    first, last = col_ref[:, :LANES].astype(F32), col_ref[:, cols - LANES :].astype(F32)
    out_ref[16:, :] = jnp.where(lane < LANES // 2, first, last).astype(BF16)
    for copy in copies[2:]:
        copy.wait()


def off_edge(axis, index):
    return jnp.where(lax.axis_index(axis) == index, 0.0, 1.0).astype(F32)


def indicator(cols, n_col):
    lane = lax.broadcasted_iota(jnp.int32, (8, cols), 1)
    row = lax.broadcasted_iota(jnp.int32, (8, cols), 0)
    me = lax.axis_index("col")
    off_map = ((lane < 8) & (me == 0), lane < 0, (lane >= cols - 8) & (me == n_col - 1))
    edge_lane = lax.broadcasted_iota(jnp.int32, (8, LANES), 1)
    edge_row = lax.broadcasted_iota(jnp.int32, (8, LANES), 0)
    edge = jnp.where(edge_lane // 16 == edge_row, 1.0, 0.0)
    taps = []
    for tap in range(3):
        on_map = jnp.logical_not(off_map[tap])
        main = [jnp.where(on_map & (row == k), 1.0, 0.0) for k in range(8)]
        taps.append(jnp.concatenate(main + [edge], axis=1))
    taps.append(jnp.zeros(taps[0].shape, F32))
    return jnp.concatenate(taps, axis=0).astype(BF16)


def own_kernel(
    n_col, one_ref, two_ref, bias_ref, grad_ref,
    x_ref, back_ref, grad_rows_ref, grad_cols_ref, ind_ref, k1c_ref, k1ct_ref, k1f_ref, bias_col_ref,
    rows_scr,
):
    cols = grad_ref.shape[2]
    ind_ref[...] = indicator(cols, n_col)
    one = [[one_ref[a, b].astype(F32) for b in range(3)] for a in range(3)]
    for k in range(3):
        rows = slice(CH * k, CH * (k + 1))
        k1c_ref[rows, :] = jnp.concatenate(one[k], axis=1).astype(BF16)
        k1f_ref[rows, :] = jnp.concatenate([one[a][k] for a in range(3)], axis=1).astype(BF16)
        k1ct_ref[rows, :] = jnp.concatenate([one[a][k].T for a in range(3)], axis=1).astype(BF16)
    nil = jnp.zeros((CH, CH), F32)
    two = [[two_ref[a, b].astype(F32) for b in range(3)] for a in range(3)]
    w2 = jnp.concatenate(
        [
            jnp.concatenate([two[eb - gb][b] if 0 <= eb - gb <= 2 else nil for eb in range(4)], axis=1)
            for b in range(3)
            for gb in range(2)
        ],
        axis=0,
    ).astype(BF16)
    bias = jnp.concatenate([bias_ref[...], jnp.zeros((1, LANES - CH), F32)], axis=1)
    bias_col_ref[...] = jnp.broadcast_to(bias, (8, LANES)).T[:CH, :]
    lane = lax.broadcasted_iota(jnp.int32, (CH, cols), 1)
    edge_lane = lax.broadcasted_iota(jnp.int32, (CH, LANES), 1)
    for piece in range(cols // LANES):
        wide = grad_ref[:, :, LANES * piece : LANES * (piece + 1)]
        rows_scr[piece, : CH * 16, :] = wide.astype(F32).reshape(CH * 16, LANES)
    col_sum = jnp.zeros((CH, cols), F32)
    for half in range(2):
        rows = slice(half * CH, (half + 1) * CH)
        left = right = jnp.zeros((CH, LANES), F32)
        for k in range(8):
            pieces = [rows_scr[p, pl.ds(half * 8 + k, CH, stride=16), :] for p in range(cols // LANES)]
            line = jnp.concatenate(pieces, axis=1)
            col_sum = col_sum + line
            span = slice(k * cols, (k + 1) * cols)
            x_ref[1, rows, span] = line.astype(BF16)
            x_ref[0, rows, span] = jnp.where(lane < cols - 8, pltpu.roll(line, cols - 8, 1), 0.0).astype(BF16)
            x_ref[2, rows, span] = jnp.where(lane >= 8, pltpu.roll(line, 8, 1), 0.0).astype(BF16)
            first = pltpu.roll(pieces[0], 16 * k, 1) if k else pieces[0]
            last = pltpu.roll(pieces[-1], 16 * k + 16, 1) if k < 7 else pieces[-1]
            here = edge_lane // 16 == k
            left = jnp.where(here & (edge_lane % 16 < 8), first, left)
            right = jnp.where(here & (edge_lane % 16 >= 8), last, right)
        x_ref[0, rows, 8 * cols :] = left.astype(BF16)
        x_ref[1, rows, 8 * cols :] = jnp.zeros((CH, LANES), BF16)
        x_ref[2, rows, 8 * cols :] = right.astype(BF16)
    grad_cols_ref[...] = col_sum
    row = lax.broadcasted_iota(jnp.int32, (8, 8 * cols), 0)
    span = lax.broadcasted_iota(jnp.int32, (8, 8 * cols), 1) // cols
    grad_rows_ref[...] = dot(jnp.where(row == span, 1.0, 0.0).astype(BF16), x_ref[1, :, : 8 * cols], NT)
    x_all = x_ref[...].reshape(6 * CH, x_ref.shape[2])
    back_ref[...] = dot(w2, x_all, TN)


def main_kernel(
    n_row, n_col, col_twin_ref, row_twin_ref, row_ref, col_ref,
    x_ref, back_ref, grad_rows_ref, grad_cols_ref, ind_ref, k1c_ref, k1ct_ref, k1f_ref, bias_ref,
    out_ref, own_ref, w_scr, chunk_scr,
):
    cols = col_ref.shape[1]
    top, bottom = off_edge("row", 0), off_edge("row", n_row - 1)
    left, right = off_edge("col", 0), off_edge("col", n_col - 1)
    edge_lane = lax.broadcasted_iota(jnp.int32, (CH, LANES), 1)
    odd_row, odd_col = lax.axis_index("row") % 2 == 1, lax.axis_index("col") % 2 == 1
    twin, other = row_twin_ref[:16, :CH].astype(F32), col_twin_ref[:16, :CH].astype(F32) * (top * bottom)
    row_ext = jnp.concatenate(
        [jnp.where(odd_row, twin, other), row_ref[...].astype(F32), jnp.where(odd_row, other, twin)], axis=0
    )
    row_taps = [row_ext[8 * a : 8 * a + 32].astype(BF16) for a in range(3)]
    row_cat = jnp.concatenate([row_ext[8 * a : 8 * a + 32] for a in range(3)], axis=1).astype(BF16)
    twin, other = col_twin_ref[16:, :].astype(F32), row_twin_ref[16:, :].astype(F32) * (left * right)
    col_ext = jnp.concatenate(
        [jnp.where(odd_col, twin, other), col_ref[...].astype(F32), jnp.where(odd_col, other, twin)], axis=1
    )
    taps = []
    for tap in range(3):
        moved = pltpu.roll(col_ext, (8 * (1 - tap)) % (cols + 2 * LANES), 1) if tap != 1 else col_ext
        low, high = pltpu.roll(moved[:, :LANES], 8, 1), pltpu.roll(moved[:, LANES + cols :], 8, 1)
        edge = jnp.where(edge_lane < 8, low, jnp.where(edge_lane < 16, high, 0.0))
        for width in (16, 32, 64):
            edge = edge + pltpu.roll(edge, width, 1)
        taps.append(jnp.concatenate([moved[:, LANES : LANES + cols], edge], axis=1).astype(BF16))
    col_cat = jnp.concatenate(taps, axis=0)
    terms = dot(k1c_ref[...], col_cat, NN)
    low, mid, high = (terms[CH * a : CH * (a + 1)] for a in range(3))
    mid = mid + bias_ref[:, :1]
    col_part = [low + mid + high, top * low + mid + high, low + mid + bottom * high, low + mid + high]
    row_terms = dot(k1f_ref[...], row_cat, NT)
    by_tap = [row_terms[CH * b : CH * (b + 1)] for b in range(3)]
    row_part = by_tap[0] + by_tap[1] + by_tap[2]

    def spread_over(terms, k):
        return jnp.concatenate(
            [jnp.broadcast_to(terms[:, 8 * eb + k : 8 * eb + k + 1], (CH, LANES)) for eb in range(4)], axis=0
        )

    side_lane = lax.broadcasted_iota(jnp.int32, (4 * CH, LANES), 1)
    first_off = jnp.where(side_lane < 8, left - 1.0, 0.0)
    last_off = jnp.where(side_lane >= LANES - 8, right - 1.0, 0.0)
    edge_part = jnp.zeros((4 * CH, LANES), F32)
    on_map = jnp.where(side_lane % 16 < 8, left, right)
    col_part = jnp.concatenate(col_part, axis=0)
    main_sum = jnp.zeros((4 * CH, cols), F32)
    two = jnp.zeros((3 * CH, 3 * CH), F32)
    row_of = jnp.zeros((32, 4 * CH), F32)
    x_half = [jnp.concatenate([x_ref[b, CH * gb : CH * (gb + 1), :] for b in range(3)], axis=0) for gb in range(2)]
    for k in range(9):
        span = slice(k * cols, (k + 1) * cols) if k < 8 else slice(8 * cols, 8 * cols + LANES)
        if k < 8:
            each = spread_over(row_part, k)
            edge_part = jnp.where(side_lane // 16 == k, each, edge_part)
            pieces = [each] * (cols // LANES)
            pieces[0] = pieces[0] + first_off * spread_over(by_tap[0], k)
            pieces[-1] = pieces[-1] + last_off * spread_over(by_tap[2], k)
            pre = jnp.concatenate(pieces, axis=1) + col_part[:, :cols]
        else:
            pre = edge_part + col_part[:, cols:]
        sig = 1.0 / (1.0 + jnp.exp(-pre))
        held = jnp.concatenate([sig[:CH] * top, sig[CH : 3 * CH], sig[3 * CH :] * bottom], axis=0)
        if k == 8:
            held = held * on_map
        act = (pre * held).astype(BF16)
        joined = jnp.concatenate([x_half[0][:, span], x_half[1][:, span]], axis=1)
        two = two + dot(joined, jnp.concatenate([act[: 3 * CH], act[CH:]], axis=1), NT)
        inner = (back_ref[:, span] * (held * (1.0 + pre * (1.0 - sig)))).astype(BF16)
        row_of = row_of + dot(ind_ref[:, span], inner, NT)
        if k < 8:
            main_sum = main_sum + inner.astype(F32)
    sums = jnp.concatenate([main_sum, inner.astype(F32)], axis=1)
    sums_of = [sums[CH * eb : CH * (eb + 1)] for eb in range(4)]

    row_sums = jnp.concatenate(
        [
            jnp.concatenate([row_of[8 * b : 8 * b + 8, CH * eb : CH * (eb + 1)] for b in range(3)], axis=1)
            for eb in range(4)
        ],
        axis=0,
    )
    row_split = jnp.concatenate(split(row_sums), axis=0)
    spread_row = dot(row_split, k1f_ref[...], NN)
    spread_row = spread_row[:32] + spread_row[32:]

    def part(eb, a):
        return spread_row[8 * eb : 8 * eb + 8, CH * a : CH * (a + 1)]

    reached = [sum(part(eb, pb - eb) for eb in range(4) if 0 <= pb - eb <= 2) for pb in range(6)]
    above, mine, below = (jnp.concatenate(reached[2 * k : 2 * k + 2], axis=1) for k in range(3))
    own_ref[...] = grad_rows_ref[...] + mine
    whole = sums_of[0] + sums_of[1] + sums_of[2] + sums_of[3]
    col_sums = jnp.concatenate(
        [whole - (1.0 - top) * sums_of[1], whole, whole - (1.0 - bottom) * sums_of[2]], axis=0
    )
    col_split = jnp.concatenate(split(col_sums), axis=1)
    spread_col = dot(k1ct_ref[...], col_split, NN)
    spread_col = spread_col[:, : cols + LANES] + spread_col[:, cols + LANES :]
    nothing = jnp.zeros((CH, LANES), F32)
    total = jnp.concatenate([nothing, grad_cols_ref[...], nothing], axis=1)
    for tap in range(3):
        piece = spread_col[CH * tap : CH * (tap + 1)]
        edge = piece[:, cols:]
        for width in (16, 32, 64):
            edge = edge + pltpu.roll(edge, width, 1)
        low = jnp.where(edge_lane >= LANES - 8, pltpu.roll(edge, LANES - 8, 1), 0.0)
        high_edge = jnp.where(edge_lane < 8, pltpu.roll(edge, LANES - 8, 1), 0.0)
        piece = jnp.concatenate([low, piece[:, :cols], high_edge], axis=1)
        total = total + (pltpu.roll(piece, (8 * (tap - 1)) % (cols + 2 * LANES), 1) if tap != 1 else piece)
    one_row = [dot(row_split, jnp.concatenate([piece, piece], axis=0), TN) for piece in row_taps]
    one_col = [dot(col_split, jnp.concatenate([piece, piece], axis=1), NT) for piece in taps]
    bias_row = jnp.sum(row_sums[:, :LANES], axis=0, keepdims=True)
    bias_row = pltpu.roll(jnp.where(lax.broadcasted_iota(jnp.int32, (8, LANES), 1) >= CH, bias_row, 0.0), 96, 1)
    for a in range(3):
        for b in range(3):
            one = one_row[a][CH * b : CH * (b + 1)] + one_col[b][CH * a : CH * (a + 1)]
            pair = jnp.concatenate([one, two[CH * b : CH * (b + 1), CH * a : CH * (a + 1)]], axis=1)
            w_scr[CH * (3 * a + b) : CH * (3 * a + b + 1), :] = pair

    weights, chans, sums_end = chunk_rows(n_row)
    tail = total[:, :LANES] + total[:, cols + LANES :] + bias_row[:1, :]
    before = lax.axis_index("row") - 1
    for j in range(n_row):
        for there, here in shares(n_row, j):
            chunk_scr[j, there, :] = w_scr[here, :]
        share = slice(chans * j, chans * (j + 1))
        chunk_scr[j, weights : weights + chans, :] = total[share, LANES : 2 * LANES]
        chunk_scr[j, weights + chans : weights + 2 * chans, :] = total[share, cols : cols + LANES]
        chunk_scr[j, weights + 2 * chans : sums_end, :] = tail[share]
        chunk_scr[j, sums_end:, :] = jnp.where(before == j, above, below)
    out_ref[...] = chunk_scr[...].astype(BF16)


def row_sum_kernel(n_row, got_ref, own_ref, out_ref):
    sums_end = chunk_rows(n_row)[2]
    me = lax.axis_index("row")
    total = got_ref[0].astype(F32)
    for j in range(1, n_row):
        total = total + got_ref[j].astype(F32)
    total = total[:sums_end]
    before = got_ref[jnp.maximum(me - 1, 0)].astype(F32)[sums_end:]
    after = got_ref[jnp.minimum(me + 1, n_row - 1)].astype(F32)[sums_end:]
    rows = own_ref[...] + off_edge("row", 0) * before + off_edge("row", n_row - 1) * after
    out_ref[...] = jnp.concatenate([total, rows], axis=0)


def pair_kernel(n_row, mine_ref, twin_ref, out_ref):
    weights, chans, sums_end = chunk_rows(n_row)
    edge = slice(weights + 2 * chans, sums_end)
    out_ref[...] = mine_ref[...] + twin_ref[...]
    lane = lax.broadcasted_iota(jnp.int32, (chans, LANES), 1)
    summed = (lane >= 32) & (lane < 32 + CH)
    out_ref[edge, :] = mine_ref[edge, :] + jnp.where(summed, twin_ref[edge, :], 0.0)


def four_kernel(left_ref, right_ref, out_ref):
    out_ref[...] = left_ref[...] + right_ref[...]


def col_sum_kernel(
    n_row, n_col, cols, mine_ref, twin_ref, other_ref, four_ref, last_ref, kept_ref, out_ref, scr
):
    weights, chans, sums_end = chunk_rows(n_row)
    odd = lax.axis_index("col") % 2 == 1
    whole = math.sqrt(16 * n_row * cols * n_col)
    total = four_ref[...] + last_ref[...]
    kept_ref[:8, :] = total[sums_end:, :] * (1.0 / math.sqrt(cols * n_col))
    kept_ref[8:, :] = total[sums_end - 8 : sums_end, :] * (1.0 / whole)
    mine, twin, other = mine_ref[...], twin_ref[...], other_ref[...]
    before = jnp.where(odd, twin, other) * off_edge("col", 0)
    after = jnp.where(odd, other, twin) * off_edge("col", n_col - 1)
    edge = slice(weights + 2 * chans, sums_end)
    lane = lax.broadcasted_iota(jnp.int32, (chans, LANES), 1)
    low = mine[weights : weights + chans] + jnp.where(lane < 16, before[edge], 0.0)
    high = mine[weights + chans : weights + 2 * chans] + jnp.where(lane >= LANES - 16, after[edge], 0.0)
    scale = 1.0 / math.sqrt(16 * n_row)
    scr[...] = jnp.zeros(scr.shape, F32)
    scr[:weights, :] = total[:weights] * (1.0 / whole)
    scr[weights : weights + chans, :] = low * scale
    scr[weights + chans : weights + 2 * chans, :] = high * scale
    share = scr[...].astype(BF16)
    for j in range(n_row):
        out_ref[j] = share


def spread_kernel(n_row, got_ref, kept_ref, row_ref, col_ref, one_ref, bias_ref, two_ref):
    weights, chans, _ = chunk_rows(n_row)
    row_ref[:8, :] = kept_ref[:8, :CH]
    row_ref[8:, :] = kept_ref[:8, CH:]
    bias_ref[...] = kept_ref[15:, 32 : 32 + CH]
    for j in range(n_row):
        chunk = got_ref[j].astype(F32)
        for there, here in shares(n_row, j):
            one_ref[here, :] = chunk[there, :CH]
            two_ref[here, :] = chunk[there, CH:]
        col_ref[chans * j : chans * (j + 1), :LANES] = chunk[weights : weights + chans]
        col_ref[chans * j : chans * (j + 1), LANES:] = chunk[weights + chans : weights + 2 * chans]


PARAMS = pltpu.CompilerParams(vmem_limit_bytes=48 * 1024 * 1024)


def sds(shape, dtype=F32):
    return jax.ShapeDtypeStruct(shape, dtype)


def shards(n_row, n_col, grad_out, row_feat, col_feat, conv_one, bias_one, conv_two):
    cols = grad_out.shape[2]
    weights, chans, sums_end = chunk_rows(n_row)
    places = 8 * cols + LANES
    grad_out, row_feat, col_turned, conv_one, conv_two, bias_row = (
        pltpu.with_memory_space_constraint(x, pltpu.HBM)
        for x in (grad_out, row_feat, col_feat.T, conv_one, conv_two, bias_one.reshape(1, CH))
    )
    given = (row_feat, col_turned, conv_one, conv_two, bias_row, grad_out)
    strip, *feats, conv_one, conv_two, bias_row, grad_out = pl.pallas_call(
        pack_kernel,
        out_shape=(sds((16 + CH, LANES), BF16), *(sds(x.shape, x.dtype) for x in given)),
        in_specs=[pl.BlockSpec(memory_space=pltpu.HBM)] * 6,
        scratch_shapes=[pltpu.SemaphoreType.DMA((6,))],
        compiler_params=PARAMS,
    )(*given)


    def twin(index, count):
        return index ^ 1

    def other(index, count):
        return min(max(index + (1 if index % 2 else -1), 0), count - 1)

    def swap(along_row, along_col):
        pairs = [
            (r * n_col + c, along_row(r, n_row) * n_col + along_col(c, n_col))
            for r in range(n_row)
            for c in range(n_col)
        ]
        return lax.ppermute(strip, ("row", "col"), pairs)

    col_twin = swap(other, twin)
    row_twin = swap(twin, other)

    square = sds((3 * CH, 3 * CH), BF16)
    held = pl.pallas_call(
        lambda *refs: own_kernel(n_col, *refs),
        out_shape=(
            sds((3, 2 * CH, places), BF16), sds((4 * CH, places)), sds((8, 2 * CH)), sds((CH, cols)),
            sds((32, places), BF16), square, square, square, sds((CH, 8)),
        ),
        scratch_shapes=[pltpu.VMEM((cols // LANES, CH * 16 + 16, LANES), F32)],
        compiler_params=PARAMS,
    )(conv_one, conv_two, bias_row, grad_out)
    chunks, own = pl.pallas_call(
        lambda *refs: main_kernel(n_row, n_col, *refs),
        out_shape=(sds((n_row, sums_end + 8, LANES), BF16), sds((8, LANES))),
        scratch_shapes=[
            pltpu.VMEM((9 * CH, LANES), F32),
            pltpu.VMEM((n_row, sums_end + 8, LANES), F32),
        ],
        compiler_params=PARAMS,
    )(col_twin, row_twin, *feats, *held)
    got = lax.all_to_all(chunks, "row", 0, 0)
    part = sds((sums_end + 8, LANES))
    mine = pl.pallas_call(
        lambda *refs: row_sum_kernel(n_row, *refs), out_shape=part, compiler_params=PARAMS
    )(got, own)
    beside = [(c, c ^ 1) for c in range(n_col)]
    outside = [(c, (c + (1 if c % 2 else -1)) % n_col) for c in range(n_col)]
    across = [(c, (c + (-3 if c % 2 else 3)) % n_col) for c in range(n_col)]
    paired = lax.ppermute(mine, "col", beside)
    two_sum = pl.pallas_call(
        lambda *refs: pair_kernel(n_row, *refs), out_shape=part, compiler_params=PARAMS
    )(mine, paired)
    side = lax.ppermute(two_sum, "col", outside)
    four = pl.pallas_call(four_kernel, out_shape=part, compiler_params=PARAMS)(two_sum, side)
    last = lax.ppermute(four, "col", across)
    end = -(-(weights + 2 * chans) // 16) * 16
    kept, copies = pl.pallas_call(
        lambda *refs: col_sum_kernel(n_row, n_col, cols, *refs),
        out_shape=(sds((16, LANES)), sds((n_row, end, LANES), BF16)),
        scratch_shapes=[pltpu.VMEM((end, LANES), F32)],
        compiler_params=PARAMS,
    )(mine, paired, side, four, last)
    got = lax.all_to_all(copies, "row", 0, 0)
    row_grad, col_grad, one, bias_grad, two = pl.pallas_call(
        lambda *refs: spread_kernel(n_row, *refs),
        out_shape=(sds((16, CH)), sds((CH, cols)), sds((9 * CH, CH)), sds((1, CH)), sds((9 * CH, CH))),
        compiler_params=PARAMS,
    )(got, kept)
    shape = conv_one.shape
    return row_grad, col_grad.T, one.reshape(shape), bias_grad[0], two.reshape(shape)


def solution(mesh):
    in_specs = (P(None, "row", "col"), P("row", None), P("col", None), P(), P(), P())
    out_specs = (P("row", None), P("col", None), P(), P(), P())
    n_row, n_col = mesh.shape["row"], mesh.shape["col"]
    return jax.shard_map(
        lambda *args: shards(n_row, n_col, *args), mesh=mesh, in_specs=in_specs, out_specs=out_specs, check_vma=False
    )
```

```python
import math

import jax
import jax.numpy as jnp
from jax import lax
from jax.experimental import pallas as pl
from jax.experimental.pallas import tpu as pltpu
from jax.sharding import PartitionSpec as P

F32, BF16 = jnp.float32, jnp.bfloat16
NN = (((1,), (0,)), ((), ()))
NT = (((1,), (1,)), ((), ()))
TN = (((0,), (0,)), ((), ()))
CH = 64
LANES = 128


def dot(x, y, dims):
    return lax.dot_general(x, y, dims, preferred_element_type=F32)


def chunk_rows(n_row):
    weights, chans = 9 * CH // n_row, CH // n_row
    return weights, chans, weights + 3 * chans


def split(x):
    high = x.astype(BF16)
    return high, (x - high.astype(F32)).astype(BF16)


def shares(n_row, j):
    weights = 9 * CH // n_row
    main = weights // 8 * 8
    pieces = [(slice(0, main), slice(main * j, main * (j + 1)))]
    if main < weights:
        rest = weights - main
        pieces.append((slice(main, weights), slice(main * n_row + rest * j, main * n_row + rest * (j + 1))))
    return pieces


def start_copies(sources, targets, sems):
    copies = [pltpu.make_async_copy(x, y, sems.at[k]) for k, (x, y) in enumerate(zip(sources, targets, strict=True))]
    for copy in copies:
        copy.start()
    return copies


def pack_kernel(row_hbm, col_hbm, out_ref, row_ref, col_ref, sems):
    for copy in start_copies((row_hbm, col_hbm), (row_ref, col_ref), sems):
        copy.wait()
    rows = row_ref[...].astype(F32)
    out_ref[:16, :] = jnp.concatenate([rows, jnp.zeros_like(rows)], axis=1).astype(BF16)
    cols = col_ref.shape[1]
    lane = lax.broadcasted_iota(jnp.int32, (CH, LANES), 1)
    first, last = col_ref[:, :LANES].astype(F32), col_ref[:, cols - LANES :].astype(F32)
    out_ref[16:, :] = jnp.where(lane < LANES // 2, first, last).astype(BF16)


def off_edge(axis, index):
    return jnp.where(lax.axis_index(axis) == index, 0.0, 1.0).astype(F32)


def indicator(cols, n_col):
    lane = lax.broadcasted_iota(jnp.int32, (8, cols), 1)
    row = lax.broadcasted_iota(jnp.int32, (8, cols), 0)
    me = lax.axis_index("col")
    off_map = ((lane < 8) & (me == 0), lane < 0, (lane >= cols - 8) & (me == n_col - 1))
    edge_lane = lax.broadcasted_iota(jnp.int32, (8, LANES), 1)
    edge_row = lax.broadcasted_iota(jnp.int32, (8, LANES), 0)
    edge = jnp.where(edge_lane // 16 == edge_row, 1.0, 0.0)
    taps = []
    for tap in range(3):
        on_map = jnp.logical_not(off_map[tap])
        main = [jnp.where(on_map & (row == k), 1.0, 0.0) for k in range(8)]
        taps.append(jnp.concatenate(main + [edge], axis=1))
    taps.append(jnp.zeros(taps[0].shape, F32))
    return jnp.concatenate(taps, axis=0).astype(BF16)


def own_kernel(
    n_col, one_hbm, two_hbm, bias_hbm, grad_hbm,
    x_ref, back_ref, grad_rows_ref, grad_cols_ref, ind_ref, k1c_ref, k1ct_ref, k1f_ref, bias_col_ref,
    rows_scr, one_ref, two_ref, bias_ref, grad_ref, sems,
):
    copies = start_copies((one_hbm, two_hbm, bias_hbm, grad_hbm), (one_ref, two_ref, bias_ref, grad_ref), sems)
    cols = grad_ref.shape[2]
    ind_ref[...] = indicator(cols, n_col)
    for copy in copies[:3]:
        copy.wait()
    one = [[one_ref[a, b].astype(F32) for b in range(3)] for a in range(3)]
    for k in range(3):
        rows = slice(CH * k, CH * (k + 1))
        k1c_ref[rows, :] = jnp.concatenate(one[k], axis=1).astype(BF16)
        k1f_ref[rows, :] = jnp.concatenate([one[a][k] for a in range(3)], axis=1).astype(BF16)
        k1ct_ref[rows, :] = jnp.concatenate([one[a][k].T for a in range(3)], axis=1).astype(BF16)
    nil = jnp.zeros((CH, CH), F32)
    two = [[two_ref[a, b].astype(F32) for b in range(3)] for a in range(3)]
    w2 = jnp.concatenate(
        [
            jnp.concatenate([two[eb - gb][b] if 0 <= eb - gb <= 2 else nil for eb in range(4)], axis=1)
            for b in range(3)
            for gb in range(2)
        ],
        axis=0,
    ).astype(BF16)
    bias = jnp.concatenate([bias_ref[...], jnp.zeros((1, LANES - CH), F32)], axis=1)
    bias_col_ref[...] = jnp.broadcast_to(bias, (8, LANES)).T[:CH, :]
    copies[3].wait()
    lane = lax.broadcasted_iota(jnp.int32, (CH, cols), 1)
    edge_lane = lax.broadcasted_iota(jnp.int32, (CH, LANES), 1)
    for piece in range(cols // LANES):
        wide = grad_ref[:, :, LANES * piece : LANES * (piece + 1)]
        rows_scr[piece, : CH * 16, :] = wide.astype(F32).reshape(CH * 16, LANES)
    col_sum = jnp.zeros((CH, cols), F32)
    for half in range(2):
        rows = slice(half * CH, (half + 1) * CH)
        left = right = jnp.zeros((CH, LANES), F32)
        for k in range(8):
            pieces = [rows_scr[p, pl.ds(half * 8 + k, CH, stride=16), :] for p in range(cols // LANES)]
            line = jnp.concatenate(pieces, axis=1)
            col_sum = col_sum + line
            span = slice(k * cols, (k + 1) * cols)
            x_ref[1, rows, span] = line.astype(BF16)
            x_ref[0, rows, span] = jnp.where(lane < cols - 8, pltpu.roll(line, cols - 8, 1), 0.0).astype(BF16)
            x_ref[2, rows, span] = jnp.where(lane >= 8, pltpu.roll(line, 8, 1), 0.0).astype(BF16)
            first = pltpu.roll(pieces[0], 16 * k, 1) if k else pieces[0]
            last = pltpu.roll(pieces[-1], 16 * k + 16, 1) if k < 7 else pieces[-1]
            here = edge_lane // 16 == k
            left = jnp.where(here & (edge_lane % 16 < 8), first, left)
            right = jnp.where(here & (edge_lane % 16 >= 8), last, right)
        x_ref[0, rows, 8 * cols :] = left.astype(BF16)
        x_ref[1, rows, 8 * cols :] = jnp.zeros((CH, LANES), BF16)
        x_ref[2, rows, 8 * cols :] = right.astype(BF16)
    grad_cols_ref[...] = col_sum
    row = lax.broadcasted_iota(jnp.int32, (8, 8 * cols), 0)
    span = lax.broadcasted_iota(jnp.int32, (8, 8 * cols), 1) // cols
    grad_rows_ref[...] = dot(jnp.where(row == span, 1.0, 0.0).astype(BF16), x_ref[1, :, : 8 * cols], NT)
    x_all = x_ref[...].reshape(6 * CH, x_ref.shape[2])
    back_ref[...] = dot(w2, x_all, TN)


def main_kernel(
    n_row, n_col, col_twin_ref, row_twin_ref, row_ref, col_ref,
    x_ref, back_ref, grad_rows_ref, grad_cols_ref, ind_ref, k1c_ref, k1ct_ref, k1f_ref, bias_ref,
    out_ref, own_ref, w_scr, chunk_scr,
):
    cols = col_ref.shape[1]
    top, bottom = off_edge("row", 0), off_edge("row", n_row - 1)
    left, right = off_edge("col", 0), off_edge("col", n_col - 1)
    edge_lane = lax.broadcasted_iota(jnp.int32, (CH, LANES), 1)
    odd_row, odd_col = lax.axis_index("row") % 2 == 1, lax.axis_index("col") % 2 == 1
    twin, other = row_twin_ref[:16, :CH].astype(F32), col_twin_ref[:16, :CH].astype(F32) * (top * bottom)
    row_ext = jnp.concatenate(
        [jnp.where(odd_row, twin, other), row_ref[...].astype(F32), jnp.where(odd_row, other, twin)], axis=0
    )
    row_taps = [row_ext[8 * a : 8 * a + 32].astype(BF16) for a in range(3)]
    row_cat = jnp.concatenate([row_ext[8 * a : 8 * a + 32] for a in range(3)], axis=1).astype(BF16)
    twin, other = col_twin_ref[16:, :].astype(F32), row_twin_ref[16:, :].astype(F32) * (left * right)
    col_ext = jnp.concatenate(
        [jnp.where(odd_col, twin, other), col_ref[...].astype(F32), jnp.where(odd_col, other, twin)], axis=1
    )
    taps = []
    for tap in range(3):
        moved = pltpu.roll(col_ext, (8 * (1 - tap)) % (cols + 2 * LANES), 1) if tap != 1 else col_ext
        low, high = pltpu.roll(moved[:, :LANES], 8, 1), pltpu.roll(moved[:, LANES + cols :], 8, 1)
        edge = jnp.where(edge_lane < 8, low, jnp.where(edge_lane < 16, high, 0.0))
        for width in (16, 32, 64):
            edge = edge + pltpu.roll(edge, width, 1)
        taps.append(jnp.concatenate([moved[:, LANES : LANES + cols], edge], axis=1).astype(BF16))
    col_cat = jnp.concatenate(taps, axis=0)
    terms = dot(k1c_ref[...], col_cat, NN)
    low, mid, high = (terms[CH * a : CH * (a + 1)] for a in range(3))
    mid = mid + bias_ref[:, :1]
    col_part = [low + mid + high, top * low + mid + high, low + mid + bottom * high, low + mid + high]
    row_terms = dot(k1f_ref[...], row_cat, NT)
    by_tap = [row_terms[CH * b : CH * (b + 1)] for b in range(3)]
    row_part = by_tap[0] + by_tap[1] + by_tap[2]

    def spread_over(terms, k):
        return jnp.concatenate(
            [jnp.broadcast_to(terms[:, 8 * eb + k : 8 * eb + k + 1], (CH, LANES)) for eb in range(4)], axis=0
        )

    side_lane = lax.broadcasted_iota(jnp.int32, (4 * CH, LANES), 1)
    first_off = jnp.where(side_lane < 8, left - 1.0, 0.0)
    last_off = jnp.where(side_lane >= LANES - 8, right - 1.0, 0.0)
    edge_part = jnp.zeros((4 * CH, LANES), F32)
    on_map = jnp.where(side_lane % 16 < 8, left, right)
    col_part = jnp.concatenate(col_part, axis=0)
    main_sum = jnp.zeros((4 * CH, cols), F32)
    two = jnp.zeros((3 * CH, 3 * CH), F32)
    row_of = jnp.zeros((32, 4 * CH), F32)
    x_half = [jnp.concatenate([x_ref[b, CH * gb : CH * (gb + 1), :] for b in range(3)], axis=0) for gb in range(2)]
    for k in range(9):
        span = slice(k * cols, (k + 1) * cols) if k < 8 else slice(8 * cols, 8 * cols + LANES)
        if k < 8:
            each = spread_over(row_part, k)
            edge_part = jnp.where(side_lane // 16 == k, each, edge_part)
            pieces = [each] * (cols // LANES)
            pieces[0] = pieces[0] + first_off * spread_over(by_tap[0], k)
            pieces[-1] = pieces[-1] + last_off * spread_over(by_tap[2], k)
            pre = jnp.concatenate(pieces, axis=1) + col_part[:, :cols]
        else:
            pre = edge_part + col_part[:, cols:]
        sig = 1.0 / (1.0 + jnp.exp(-pre))
        held = jnp.concatenate([sig[:CH] * top, sig[CH : 3 * CH], sig[3 * CH :] * bottom], axis=0)
        if k == 8:
            held = held * on_map
        act = (pre * held).astype(BF16)
        joined = jnp.concatenate([x_half[0][:, span], x_half[1][:, span]], axis=1)
        two = two + dot(joined, jnp.concatenate([act[: 3 * CH], act[CH:]], axis=1), NT)
        inner = (back_ref[:, span] * (held * (1.0 + pre * (1.0 - sig)))).astype(BF16)
        row_of = row_of + dot(ind_ref[:, span], inner, NT)
        if k < 8:
            main_sum = main_sum + inner.astype(F32)
    sums = jnp.concatenate([main_sum, inner.astype(F32)], axis=1)
    sums_of = [sums[CH * eb : CH * (eb + 1)] for eb in range(4)]

    row_sums = jnp.concatenate(
        [
            jnp.concatenate([row_of[8 * b : 8 * b + 8, CH * eb : CH * (eb + 1)] for b in range(3)], axis=1)
            for eb in range(4)
        ],
        axis=0,
    )
    row_split = jnp.concatenate(split(row_sums), axis=0)
    spread_row = dot(row_split, k1f_ref[...], NN)
    spread_row = spread_row[:32] + spread_row[32:]

    def part(eb, a):
        return spread_row[8 * eb : 8 * eb + 8, CH * a : CH * (a + 1)]

    reached = [sum(part(eb, pb - eb) for eb in range(4) if 0 <= pb - eb <= 2) for pb in range(6)]
    above, mine, below = (jnp.concatenate(reached[2 * k : 2 * k + 2], axis=1) for k in range(3))
    own_ref[...] = grad_rows_ref[...] + mine
    whole = sums_of[0] + sums_of[1] + sums_of[2] + sums_of[3]
    col_sums = jnp.concatenate(
        [whole - (1.0 - top) * sums_of[1], whole, whole - (1.0 - bottom) * sums_of[2]], axis=0
    )
    col_split = jnp.concatenate(split(col_sums), axis=1)
    spread_col = dot(k1ct_ref[...], col_split, NN)
    spread_col = spread_col[:, : cols + LANES] + spread_col[:, cols + LANES :]
    nothing = jnp.zeros((CH, LANES), F32)
    total = jnp.concatenate([nothing, grad_cols_ref[...], nothing], axis=1)
    for tap in range(3):
        piece = spread_col[CH * tap : CH * (tap + 1)]
        edge = piece[:, cols:]
        for width in (16, 32, 64):
            edge = edge + pltpu.roll(edge, width, 1)
        low = jnp.where(edge_lane >= LANES - 8, pltpu.roll(edge, LANES - 8, 1), 0.0)
        high_edge = jnp.where(edge_lane < 8, pltpu.roll(edge, LANES - 8, 1), 0.0)
        piece = jnp.concatenate([low, piece[:, :cols], high_edge], axis=1)
        total = total + (pltpu.roll(piece, (8 * (tap - 1)) % (cols + 2 * LANES), 1) if tap != 1 else piece)
    one_row = [dot(row_split, jnp.concatenate([piece, piece], axis=0), TN) for piece in row_taps]
    one_col = [dot(col_split, jnp.concatenate([piece, piece], axis=1), NT) for piece in taps]
    bias_row = jnp.sum(row_sums[:, :LANES], axis=0, keepdims=True)
    bias_row = pltpu.roll(jnp.where(lax.broadcasted_iota(jnp.int32, (8, LANES), 1) >= CH, bias_row, 0.0), 96, 1)
    for a in range(3):
        for b in range(3):
            one = one_row[a][CH * b : CH * (b + 1)] + one_col[b][CH * a : CH * (a + 1)]
            pair = jnp.concatenate([one, two[CH * b : CH * (b + 1), CH * a : CH * (a + 1)]], axis=1)
            w_scr[CH * (3 * a + b) : CH * (3 * a + b + 1), :] = pair

    weights, chans, sums_end = chunk_rows(n_row)
    tail = total[:, :LANES] + total[:, cols + LANES :] + bias_row[:1, :]
    before = lax.axis_index("row") - 1
    for j in range(n_row):
        for there, here in shares(n_row, j):
            chunk_scr[j, there, :] = w_scr[here, :]
        share = slice(chans * j, chans * (j + 1))
        chunk_scr[j, weights : weights + chans, :] = total[share, LANES : 2 * LANES]
        chunk_scr[j, weights + chans : weights + 2 * chans, :] = total[share, cols : cols + LANES]
        chunk_scr[j, weights + 2 * chans : sums_end, :] = tail[share]
        chunk_scr[j, sums_end:, :] = jnp.where(before == j, above, below)
    out_ref[...] = chunk_scr[...].astype(BF16)


def row_sum_kernel(n_row, got_ref, own_ref, out_ref):
    sums_end = chunk_rows(n_row)[2]
    me = lax.axis_index("row")
    total = got_ref[0].astype(F32)
    for j in range(1, n_row):
        total = total + got_ref[j].astype(F32)
    total = total[:sums_end]
    before = got_ref[jnp.maximum(me - 1, 0)].astype(F32)[sums_end:]
    after = got_ref[jnp.minimum(me + 1, n_row - 1)].astype(F32)[sums_end:]
    rows = own_ref[...] + off_edge("row", 0) * before + off_edge("row", n_row - 1) * after
    out_ref[...] = jnp.concatenate([total, rows], axis=0)


def pair_kernel(n_row, mine_ref, twin_ref, out_ref):
    weights, chans, sums_end = chunk_rows(n_row)
    edge = slice(weights + 2 * chans, sums_end)
    out_ref[...] = mine_ref[...] + twin_ref[...]
    lane = lax.broadcasted_iota(jnp.int32, (chans, LANES), 1)
    summed = (lane >= 32) & (lane < 32 + CH)
    out_ref[edge, :] = mine_ref[edge, :] + jnp.where(summed, twin_ref[edge, :], 0.0)


def four_kernel(left_ref, right_ref, out_ref):
    out_ref[...] = left_ref[...] + right_ref[...]


def col_sum_kernel(
    n_row, n_col, cols, mine_ref, twin_ref, other_ref, four_ref, last_ref, kept_ref, out_ref, scr
):
    weights, chans, sums_end = chunk_rows(n_row)
    odd = lax.axis_index("col") % 2 == 1
    whole = math.sqrt(16 * n_row * cols * n_col)
    total = four_ref[...] + last_ref[...]
    kept_ref[:8, :] = total[sums_end:, :] * (1.0 / math.sqrt(cols * n_col))
    kept_ref[8:, :] = total[sums_end - 8 : sums_end, :] * (1.0 / whole)
    mine, twin, other = mine_ref[...], twin_ref[...], other_ref[...]
    before = jnp.where(odd, twin, other) * off_edge("col", 0)
    after = jnp.where(odd, other, twin) * off_edge("col", n_col - 1)
    edge = slice(weights + 2 * chans, sums_end)
    lane = lax.broadcasted_iota(jnp.int32, (chans, LANES), 1)
    low = mine[weights : weights + chans] + jnp.where(lane < 16, before[edge], 0.0)
    high = mine[weights + chans : weights + 2 * chans] + jnp.where(lane >= LANES - 16, after[edge], 0.0)
    scale = 1.0 / math.sqrt(16 * n_row)
    scr[...] = jnp.zeros(scr.shape, F32)
    scr[:weights, :] = total[:weights] * (1.0 / whole)
    scr[weights : weights + chans, :] = low * scale
    scr[weights + chans : weights + 2 * chans, :] = high * scale
    share = scr[...].astype(BF16)
    for j in range(n_row):
        out_ref[j] = share


def spread_kernel(n_row, got_ref, kept_ref, row_ref, col_ref, one_ref, bias_ref, two_ref):
    weights, chans, _ = chunk_rows(n_row)
    row_ref[:8, :] = kept_ref[:8, :CH]
    row_ref[8:, :] = kept_ref[:8, CH:]
    bias_ref[...] = kept_ref[15:, 32 : 32 + CH]
    for j in range(n_row):
        chunk = got_ref[j].astype(F32)
        for there, here in shares(n_row, j):
            one_ref[here, :] = chunk[there, :CH]
            two_ref[here, :] = chunk[there, CH:]
        col_ref[chans * j : chans * (j + 1), :LANES] = chunk[weights : weights + chans]
        col_ref[chans * j : chans * (j + 1), LANES:] = chunk[weights + chans : weights + 2 * chans]


PARAMS = pltpu.CompilerParams(vmem_limit_bytes=48 * 1024 * 1024)


def sds(shape, dtype=F32):
    return jax.ShapeDtypeStruct(shape, dtype)


def shards(n_row, n_col, grad_out, row_feat, col_feat, conv_one, bias_one, conv_two):
    cols = grad_out.shape[2]
    weights, chans, sums_end = chunk_rows(n_row)
    places = 8 * cols + LANES
    grad_out, row_feat, col_turned, conv_one, conv_two, bias_row = (
        pltpu.with_memory_space_constraint(x, pltpu.HBM)
        for x in (grad_out, row_feat, col_feat.T, conv_one, conv_two, bias_one.reshape(1, CH))
    )
    strip, *feats = pl.pallas_call(
        pack_kernel,
        out_shape=(sds((16 + CH, LANES), BF16), sds(row_feat.shape, BF16), sds(col_turned.shape, BF16)),
        in_specs=[pl.BlockSpec(memory_space=pltpu.HBM)] * 2,
        scratch_shapes=[pltpu.SemaphoreType.DMA((2,))],
        compiler_params=PARAMS,
    )(row_feat, col_turned)

    def twin(index, count):
        return index ^ 1

    def other(index, count):
        return min(max(index + (1 if index % 2 else -1), 0), count - 1)

    def swap(along_row, along_col):
        pairs = [
            (r * n_col + c, along_row(r, n_row) * n_col + along_col(c, n_col))
            for r in range(n_row)
            for c in range(n_col)
        ]
        return lax.ppermute(strip, ("row", "col"), pairs)

    col_twin = swap(other, twin)
    row_twin = swap(twin, other)

    square = sds((3 * CH, 3 * CH), BF16)
    held = pl.pallas_call(
        lambda *refs: own_kernel(n_col, *refs),
        out_shape=(
            sds((3, 2 * CH, places), BF16), sds((4 * CH, places)), sds((8, 2 * CH)), sds((CH, cols)),
            sds((32, places), BF16), square, square, square, sds((CH, 8)),
        ),
        in_specs=[pl.BlockSpec(memory_space=pltpu.HBM)] * 4,
        scratch_shapes=[
            pltpu.VMEM((cols // LANES, CH * 16 + 16, LANES), F32),
            pltpu.VMEM(conv_one.shape, BF16),
            pltpu.VMEM(conv_two.shape, BF16),
            pltpu.VMEM((1, CH), F32),
            pltpu.VMEM(grad_out.shape, BF16),
            pltpu.SemaphoreType.DMA((4,)),
        ],
        compiler_params=PARAMS,
    )(conv_one, conv_two, bias_row, grad_out)
    chunks, own = pl.pallas_call(
        lambda *refs: main_kernel(n_row, n_col, *refs),
        out_shape=(sds((n_row, sums_end + 8, LANES), BF16), sds((8, LANES))),
        scratch_shapes=[
            pltpu.VMEM((9 * CH, LANES), F32),
            pltpu.VMEM((n_row, sums_end + 8, LANES), F32),
        ],
        compiler_params=PARAMS,
    )(col_twin, row_twin, *feats, *held)
    got = lax.all_to_all(chunks, "row", 0, 0)
    part = sds((sums_end + 8, LANES))
    mine = pl.pallas_call(
        lambda *refs: row_sum_kernel(n_row, *refs), out_shape=part, compiler_params=PARAMS
    )(got, own)
    beside = [(c, c ^ 1) for c in range(n_col)]
    outside = [(c, (c + (1 if c % 2 else -1)) % n_col) for c in range(n_col)]
    across = [(c, (c + (-3 if c % 2 else 3)) % n_col) for c in range(n_col)]
    paired = lax.ppermute(mine, "col", beside)
    two_sum = pl.pallas_call(
        lambda *refs: pair_kernel(n_row, *refs), out_shape=part, compiler_params=PARAMS
    )(mine, paired)
    side = lax.ppermute(two_sum, "col", outside)
    four = pl.pallas_call(four_kernel, out_shape=part, compiler_params=PARAMS)(two_sum, side)
    last = lax.ppermute(four, "col", across)
    end = -(-(weights + 2 * chans) // 16) * 16
    kept, copies = pl.pallas_call(
        lambda *refs: col_sum_kernel(n_row, n_col, cols, *refs),
        out_shape=(sds((16, LANES)), sds((n_row, end, LANES), BF16)),
        scratch_shapes=[pltpu.VMEM((end, LANES), F32)],
        compiler_params=PARAMS,
    )(mine, paired, side, four, last)
    got = lax.all_to_all(copies, "row", 0, 0)
    row_grad, col_grad, one, bias_grad, two = pl.pallas_call(
        lambda *refs: spread_kernel(n_row, *refs),
        out_shape=(sds((16, CH)), sds((CH, cols)), sds((9 * CH, CH)), sds((1, CH)), sds((9 * CH, CH))),
        compiler_params=PARAMS,
    )(got, kept)
    shape = conv_one.shape
    return row_grad, col_grad.T, one.reshape(shape), bias_grad[0], two.reshape(shape)


def solution(mesh):
    in_specs = (P(None, "row", "col"), P("row", None), P("col", None), P(), P(), P())
    out_specs = (P("row", None), P("col", None), P(), P(), P())
    n_row, n_col = mesh.shape["row"], mesh.shape["col"]
    return jax.shard_map(
        lambda *args: shards(n_row, n_col, *args), mesh=mesh, in_specs=in_specs, out_specs=out_specs, check_vma=False
    )
```
